32 devices in a mesh: seq: 8 (over y, x, core), head: 4 (over z).
Axes of the slice: x: 2, y: 2, z: 4, core: 2. Of those that a mesh axis runs over, the one named last changes fastest.
Arguments:
- slab_query: bfloat16 [1024, 8192], P('seq', 'head'), may hold values from -6 to 6
- slab_key: bfloat16 [1024, 8192], P('seq', 'head'), may hold values from -6 to 6
- slab_value: bfloat16 [1024, 8192], P('seq', 'head'), may hold values from -6 to 6
- slab_levels: bfloat16 [6, 64, 1024], P(None, 'head', 'seq'), may hold values from 0.1 to 10
- norm_gain: bfloat16 [8192], P('head'), may hold values from 0.5 to 1.5
- user_query: bfloat16 [32, 64, 8192], P('seq', None, 'head'), may hold values from -6 to 6
- user_key: bfloat16 [32, 64, 8192], P('seq', None, 'head'), may hold values from -6 to 6
- user_value: bfloat16 [32, 64, 8192], P('seq', None, 'head'), may hold values from -6 to 6
- user_levels: bfloat16 [32, 6, 64, 64], P('seq', None, 'head'), may hold values from 0.1 to 10
- prefix_lengths: int32 [32], P('seq'), may hold values from 1 to 7, as said below
Outputs:
- slab_out: bfloat16 [1024, 8192], P('seq', 'head')
- user_out: bfloat16 [32, 64, 8192], P('seq', None, 'head')
The draws below stay inside these ranges and needn't reach their ends.
Inputs may be any that keep to these rules, and one draw needn't show every extreme that they name: `prefix_lengths`: the 4 users that lie on one index of seq have distinct prefix lengths; one prefix length is held by one user of every index of seq.
All inputs are finite; a program needn't handle non-finite values.
Results may differ from the reference program's by a relative error of at most 0.012.
Values may be sent and summed in bfloat16 or wider, within the bound.
No kernel may reach another device: no remote copies, remote signals or barrier semaphores. Data moves between devices by JAX's collectives and lax.ppermute only.
A program may use at most 64 MiB of HBM per device.

```python
import math
import jax
import jax.numpy as jnp
from jax import lax

HEADS = 64
HD = 128
TOK_DEV = 128
SUF = 64
LEVELS = 6
TOKENS = 1024
USERS_DEV = 4
USERS = 32
N_SEQ = 8


def level_draw(key, array_shape, head_axis):
    head_total = array_shape[head_axis]
    head_frac = jnp.arange(head_total, dtype=jnp.float32) / max(head_total - 1, 1)
    head_rise = jnp.power(10.0, head_frac)
    broadcast_shape = [1] * len(array_shape)
    broadcast_shape[head_axis] = head_total
    head_rise = head_rise.reshape(broadcast_shape)
    magnitude = jnp.exp(jax.random.uniform(key, array_shape, jnp.float32, math.log(0.1), 0.0))
    return magnitude * head_rise


def draw_slab_levels(key, part):
    return level_draw(jax.random.fold_in(key, 3), (LEVELS, HEADS, TOKENS), 1).astype(jnp.bfloat16)


def draw_user_levels(key, part):
    return level_draw(jax.random.fold_in(key, 5), (USERS, LEVELS, HEADS, SUF), 2).astype(jnp.bfloat16)


def draw_prefix_lengths(key, part):
    shared_len = jax.random.randint(jax.random.fold_in(key, 7), (), 1, N_SEQ)
    first_dev = jax.random.randint(jax.random.fold_in(key, 9), (), 0, N_SEQ)
    second_dev = (first_dev + 1 + jax.random.randint(jax.random.fold_in(key, 13), (), 0, N_SEQ - 1)) % N_SEQ
    device_keys = jax.random.split(jax.random.fold_in(key, 11), N_SEQ)
    device_ids = jnp.arange(N_SEQ, dtype=jnp.int32)

    def device_draw(device_key, device_id):
        key_scores, key_order = jax.random.split(device_key)
        candidates = jnp.arange(1, N_SEQ, dtype=jnp.int32)
        ranking = jax.random.permutation(key_scores, N_SEQ - 1).astype(jnp.int32)
        ranking = jnp.where(candidates == shared_len, -3, ranking)
        ranking = jnp.where(jnp.logical_and(device_id == first_dev, candidates == 1), -2, ranking)
        ranking = jnp.where(jnp.logical_and(device_id == second_dev, candidates == N_SEQ - 1), -2, ranking)
        ordering = jnp.argsort(ranking, stable=True)
        picked = candidates[ordering[:USERS_DEV]]
        return jax.random.permutation(key_order, picked)
    drawn = jax.vmap(device_draw)(device_keys, device_ids)
    return drawn.reshape(USERS).astype(jnp.int32)


def block_scale(key, extent, pieces, smallest, top_value):
    gain = 1.0
    for dim, shards_of in pieces:
        draws = jax.random.uniform(jax.random.fold_in(jax.random.fold_in(key, 6), dim), (shards_of,), jnp.float32, smallest / len(pieces), top_value / len(pieces))
        gain = gain * jnp.repeat(jnp.exp(draws), extent[dim] // shards_of).reshape((-1,) + (1,) * (len(extent) - 1 - dim))
    return gain


def normal_values(stream_key, extent, scale, limit, cuts=(), kind=jnp.bfloat16):
    gain = block_scale(stream_key, extent, cuts, -0.22, 0.18) if cuts else 1.0
    array = jax.random.normal(stream_key, extent, jnp.float32) * scale * gain
    return jnp.minimum(jnp.maximum(array, -limit), limit).astype(kind)


def setup_inputs(seed: int = 0) -> dict:
    splits = jax.random.split(jax.random.key(seed), 11)
    return {
        "slab_query": normal_values(splits[0], (TOKENS, HEADS * HD), 1.0, 6.0, ((0, 8), (1, 4))),
        "slab_key": normal_values(splits[1], (TOKENS, HEADS * HD), 1.0, 6.0, ((0, 8), (1, 4))),
        "slab_value": normal_values(splits[2], (TOKENS, HEADS * HD), 1.0, 6.0, ((0, 8), (1, 4))),
        "slab_levels": draw_slab_levels(jax.random.fold_in(splits[10], 71), 0),
        "norm_gain": jnp.clip(1.0 + 0.1 * jax.random.normal(splits[4], (HEADS * HD,), jnp.float32), 0.5, 1.5).astype(jnp.bfloat16),
        "user_query": normal_values(splits[5], (USERS, SUF, HEADS * HD), 1.0, 6.0, ((0, 8), (2, 4))),
        "user_key": normal_values(splits[6], (USERS, SUF, HEADS * HD), 1.0, 6.0, ((0, 8), (2, 4))),
        "user_value": normal_values(splits[7], (USERS, SUF, HEADS * HD), 1.0, 6.0, ((0, 8), (2, 4))),
        "user_levels": draw_user_levels(jax.random.fold_in(splits[10], 71), 0),
        "prefix_lengths": draw_prefix_lengths(jax.random.fold_in(splits[10], 71), 0),
    }


def local_part(query_rows, key_rows, value_rows, first_weights):
    scores = jnp.einsum('bthd,bshd->bhts', query_rows.astype(jnp.float32), key_rows.astype(jnp.float32))
    token_count = query_rows.shape[1]
    causal_mask = jnp.arange(token_count)[:, None] >= jnp.arange(token_count)[None, :]
    scores = jnp.where(causal_mask, scores, jnp.zeros_like(scores)).astype(jnp.bfloat16)
    result = jnp.einsum('bhts,bshd->bthd', scores.astype(jnp.float32), value_rows.astype(jnp.float32))
    return result * jnp.transpose(first_weights, (0, 2, 1)).astype(jnp.float32)[..., None]

def read_prefix(query_rows, level_weights, node_states):
    level_count, head_count, inner, outer = node_states.shape
    merged = jnp.transpose(node_states, (1, 2, 0, 3)).reshape(head_count, inner, level_count * outer).astype(jnp.float32)
    projected = jnp.einsum('bthd,hdf->bthf', query_rows.astype(jnp.float32), merged, precision=lax.Precision.HIGHEST)
    projected = projected.reshape(projected.shape[:3] + (level_count, outer))
    scale_rows = jnp.transpose(level_weights, (0, 3, 2, 1)).astype(jnp.float32)[..., None]
    return lax.optimization_barrier(jnp.sum(projected * scale_rows, axis=3))

def reference(slab_query, slab_key, slab_value, slab_levels, norm_gain, user_query, user_key, user_value, user_levels, prefix_lengths):
    tree_depth = N_SEQ.bit_length() - 1
    slab_queries = slab_query.reshape(N_SEQ, TOK_DEV, HEADS, HD)
    slab_keys = slab_key.reshape(N_SEQ, TOK_DEV, HEADS, HD)
    slab_values = slab_value.reshape(N_SEQ, TOK_DEV, HEADS, HD)
    block_states = jnp.einsum('cthd,cthe->chde', slab_keys.astype(jnp.float32), slab_values.astype(jnp.float32))
    block_states = lax.optimization_barrier(block_states.astype(jnp.bfloat16)).astype(jnp.float32)
    tiers = [block_states]
    for level_index in range(tree_depth):
        paired = tiers[-1].reshape(-1, 2, HEADS, HD, HD)
        tiers.append(paired[:, 0] + paired[:, 1])

    def nodes_of(position):
        collected = []
        for level_index in range(tree_depth):
            shifted = jnp.right_shift(position, level_index)
            sibling = jnp.bitwise_xor(shifted, 1).astype(jnp.int32)
            chosen = tiers[level_index][sibling]
            upper = jnp.bitwise_and(shifted, 1)
            collected.append(jnp.where(upper == 1, chosen, jnp.zeros_like(chosen)))
        stacked = jnp.stack(collected)
        return lax.optimization_barrier(stacked.astype(jnp.bfloat16)).astype(jnp.float32)
    slab_weights = slab_levels.reshape(LEVELS, HEADS, N_SEQ, TOK_DEV).transpose(2, 0, 1, 3)

    def slab_block(packed):
        position, query_rows, key_rows, value_rows, weights = packed
        local = local_part(query_rows[None], key_rows[None], value_rows[None], weights[None, 0])
        prefix = read_prefix(query_rows[None], weights[None, 1:1 + tree_depth], nodes_of(position))
        return (local + prefix)[0]
    slab_total = lax.map(slab_block, (jnp.arange(N_SEQ, dtype=jnp.int32), slab_queries, slab_keys, slab_values, slab_weights))
    user_queries = user_query.reshape(USERS, SUF, HEADS, HD)
    user_keys = user_key.reshape(USERS, SUF, HEADS, HD)
    user_values = user_value.reshape(USERS, SUF, HEADS, HD)

    def user_block(packed):
        position, query_rows, key_rows, value_rows, weights = packed
        local = local_part(query_rows[None], key_rows[None], value_rows[None], weights[None, 0])
        prefix = read_prefix(query_rows[None], weights[None, 1:1 + tree_depth], nodes_of(position))
        prefix = lax.optimization_barrier(prefix.astype(jnp.bfloat16)).astype(jnp.float32)
        return (local + prefix)[0]
    user_total = lax.map(user_block, (prefix_lengths.astype(jnp.int32), user_queries, user_keys, user_values, user_levels))
    gain_rows = norm_gain.reshape(HEADS, HD).astype(jnp.float32)

    def finish_norm(total):
        square_sum = lax.optimization_barrier(jnp.sum(total * total, axis=(-2, -1)))
        root_mean = jnp.sqrt(square_sum / (HEADS * HD) + 1e-06)
        return (total / root_mean[..., None, None] * gain_rows).astype(jnp.bfloat16)
    slab_out = finish_norm(slab_total).reshape(TOKENS, HEADS * HD)
    user_out = finish_norm(user_total).reshape(USERS, SUF, HEADS * HD)
    return (slab_out, user_out)
```

```python
import functools

import jax
import jax.numpy as jnp
from jax import lax
from jax.experimental import pallas as pl
from jax.experimental.pallas import tpu as pltpu
from jax.sharding import PartitionSpec as P

HEADS = 64
HD = 128
ROWS = 128
VMEM_BYTES = 48 * 1024 * 1024


def matmul(a, b, contract):
    return lax.dot_general(a, b, (contract, ((), ())), preferred_element_type=jnp.float32)


def state_kernel(key_ref, value_ref, first_ref, second_ref):
    half = first_ref.shape[0]
    for head in range(2 * half):
        cols = slice(head * HD, (head + 1) * HD)
        state = matmul(key_ref[:, cols], value_ref[:, cols], ((0,), (0,)))
        target = first_ref if head < half else second_ref
        target[head % half] = state.astype(jnp.bfloat16)


def local_kernel(suffix, sq_ref, sk_ref, sv_ref, uq_ref, uk_ref, uv_ref, sw_ref, uw_ref, so_ref, uo_ref):
    head_count = sq_ref.shape[1] // HD
    row = lax.broadcasted_iota(jnp.int32, (ROWS, ROWS), 0)
    col = lax.broadcasted_iota(jnp.int32, (ROWS, ROWS), 1)
    causal = row >= col
    within = jnp.logical_and(causal, row // suffix == col // suffix)
    parts = [(sq_ref, sk_ref, sv_ref, sw_ref, so_ref, causal), (uq_ref, uk_ref, uv_ref, uw_ref, uo_ref, within)]
    for head in range(head_count):
        cols = slice(head * HD, (head + 1) * HD)
        for q_ref, k_ref, v_ref, w_ref, o_ref, mask in parts:
            for start in range(0, q_ref.shape[0], ROWS):
                rows = slice(start, start + ROWS)
                scores = matmul(q_ref[rows, cols], k_ref[rows, cols], ((1,), (1,)))
                scores = jnp.where(mask, scores, 0.0).astype(jnp.bfloat16)
                result = matmul(scores, v_ref[rows, cols], ((1,), (0,)))
                o_ref[rows, cols] = result * w_ref[rows, head : head + 1]


def prefix_kernel(depth, suffix, order_ref, length_ref, sq_ref, uq_ref, sw_ref, uw_ref, sl_ref, ul_ref, *rest):
    block_count = 1 << depth
    pieces = rest[: 2 * block_count]
    st_ref, ut_ref, square_ref, nodes, s_square, u_square, sems = rest[2 * block_count :]
    position = order_ref[0]
    head_count = nodes.shape[1]
    half = head_count // 2
    copies = []
    for offset in range(block_count):
        for side in range(2):
            copies.append(
                pltpu.make_async_copy(
                    pieces[2 * offset + side],
                    nodes.at[position ^ offset, pl.ds(side * half, half)],
                    sems.at[2 * offset + side],
                )
            )
    for copy in copies:
        copy.start()
    for copy in copies:
        copy.wait()
    for level in range(depth, 1, -1):
        for group in range(block_count >> level):
            base = group << level
            size = 1 << (level - 1)
            total = nodes[base].astype(jnp.float32)
            for extra in range(1, size):
                total = total + nodes[base + extra].astype(jnp.float32)
            nodes[base + size - 1] = total.astype(jnp.bfloat16)

    def slots(target):
        return [
            lax.shift_left(lax.shift_right_logical(target, level), level) + ((1 << (level - 1)) - 1)
            for level in range(1, depth + 1)
        ]

    slab_slots = slots(position)
    user_slots = [slots(length_ref[user]) for user in range(uq_ref.shape[0] // suffix)]
    for head in range(head_count):
        cols = slice(head * HD, (head + 1) * HD)

        def read(q_ref, w_ref, rows, node_slots):
            total = None
            for level, slot in enumerate(node_slots):
                column = (level + 1) * head_count + head
                part = matmul(q_ref[rows, cols], nodes[slot, head], ((1,), (0,)))
                part = part * w_ref[rows, column : column + 1]
                total = part if total is None else total + part
            return total

        def accumulate(acc_ref, rows, total):
            if head == 0:
                acc_ref[rows] = total * total
            else:
                acc_ref[rows] += total * total

        rows = slice(0, sq_ref.shape[0])
        total = sl_ref[:, cols] + read(sq_ref, sw_ref, rows, slab_slots)
        st_ref[:, cols] = total
        accumulate(s_square, rows, total)
        for user, node_slots in enumerate(user_slots):
            rows = slice(user * suffix, (user + 1) * suffix)
            prefix = read(uq_ref, uw_ref, rows, node_slots).astype(jnp.bfloat16)
            total = ul_ref[rows, cols] + prefix.astype(jnp.float32)
            ut_ref[rows, cols] = total
            accumulate(u_square, rows, total)
    line = 0
    for acc_ref in (s_square, u_square):
        for start in range(0, acc_ref.shape[0], ROWS):
            turned = jnp.transpose(acc_ref[start : start + ROWS])
            square_ref[line : line + 1] = jnp.sum(turned, axis=0, keepdims=True)
            line += 1


def norm_kernel(features, st_ref, ut_ref, gain_ref, *rest):
    squares = rest[:-3]
    so_ref, uo_ref, scale_ref = rest[-3:]

    @pl.when(pl.program_id(0) == 0)
    def _():
        total = squares[0][...]
        for part in squares[1:]:
            total = total + part[...]
        scale = lax.rsqrt(total / features + 1e-06)
        for line in range(scale.shape[0]):
            spread = jnp.broadcast_to(scale[line : line + 1], (ROWS, ROWS))
            scale_ref[line] = jnp.transpose(spread)

    gain = gain_ref[...].astype(jnp.float32)
    line = 0
    for t_ref, o_ref in ((st_ref, so_ref), (ut_ref, uo_ref)):
        for start in range(0, t_ref.shape[0], ROWS):
            rows = slice(start, start + ROWS)
            for low in range(0, t_ref.shape[1], HD):
                cols = slice(low, low + HD)
                o_ref[rows, cols] = (t_ref[rows, cols] * scale_ref[line] * gain[:, cols]).astype(jnp.bfloat16)
            line += 1


def exchange(first, second, depth):
    block_count = 1 << depth

    def swap(value, bit):
        return lax.ppermute(value, "seq", [(i, i ^ (1 << bit)) for i in range(block_count)])

    outer = list(range(1, depth))
    held = []
    for piece, bits in ((first, outer), (second, outer[::-1])):
        have = {0: piece}
        for bit in bits:
            have.update({key | (1 << bit): swap(value, bit) for key, value in list(have.items())})
        held.append(have)
    for have in held:
        have.update({key | 1: swap(value, 0) for key, value in list(have.items())})
    return [have[key] for key in range(block_count) for have in held]


def local(
    slab_query,
    slab_key,
    slab_value,
    slab_levels,
    norm_gain,
    user_query,
    user_key,
    user_value,
    user_levels,
    prefix_lengths,
):
    seq_count = lax.axis_size("seq")
    head_axis = lax.axis_size("head")
    depth = seq_count.bit_length() - 1
    position = lax.axis_index("seq").astype(jnp.int32)
    token_count, width = slab_query.shape
    head_count = width // HD
    user_count, suffix = user_query.shape[:2]
    user_rows = user_count * suffix
    lines = (token_count + user_rows) // ROWS
    params = pltpu.CompilerParams(vmem_limit_bytes=VMEM_BYTES)
    f32 = functools.partial(jax.ShapeDtypeStruct, dtype=jnp.float32)
    bf16 = functools.partial(jax.ShapeDtypeStruct, dtype=jnp.bfloat16)
    vmem = pl.BlockSpec(memory_space=pltpu.VMEM)
    smem = pl.BlockSpec(memory_space=pltpu.SMEM)
    whole = pl.BlockSpec(memory_space=pl.ANY)

    first, second = pl.pallas_call(
        state_kernel,
        out_shape=[bf16((head_count // 2, HD, HD))] * 2,
        in_specs=[vmem] * 2,
        out_specs=[vmem] * 2,
        compiler_params=params,
    )(slab_key, slab_value)
    pieces = exchange(first, second, depth)

    steps = jnp.arange(depth, dtype=jnp.int32)
    slab_bits = jnp.bitwise_and(jnp.right_shift(position, steps), 1)
    user_bits = jnp.bitwise_and(jnp.right_shift(prefix_lengths[:, None], steps), 1)
    slab_keep = jnp.concatenate([jnp.ones((1,), jnp.int32), slab_bits]).astype(jnp.float32)
    user_keep = jnp.concatenate([jnp.ones((user_count, 1), jnp.int32), user_bits], axis=1).astype(jnp.float32)
    slab_weights = slab_levels[: depth + 1].astype(jnp.float32) * slab_keep[:, None, None]
    user_weights = user_levels[:, : depth + 1].astype(jnp.float32) * user_keep[:, :, None, None]
    slab_weights = jnp.transpose(slab_weights, (2, 0, 1)).reshape(token_count, -1)
    user_weights = jnp.transpose(user_weights, (0, 3, 1, 2)).reshape(user_rows, -1)
    user_queries = user_query.reshape(user_rows, width)
    user_keys = user_key.reshape(user_rows, width)
    user_values = user_value.reshape(user_rows, width)

    slab_local, user_local = pl.pallas_call(
        functools.partial(local_kernel, suffix),
        out_shape=[f32((token_count, width)), f32((user_rows, width))],
        in_specs=[vmem] * 8,
        out_specs=[vmem] * 2,
        compiler_params=params,
        cost_estimate=pl.CostEstimate(
            flops=4 * ROWS * width * (token_count + user_rows),
            bytes_accessed=10 * width * (token_count + user_rows),
            transcendentals=0,
        ),
    )(slab_query, slab_key, slab_value, user_queries, user_keys, user_values, slab_weights, user_weights)

    slab_total, user_total, square = pl.pallas_call(
        functools.partial(prefix_kernel, depth, suffix),
        out_shape=[f32((token_count, width)), f32((user_rows, width)), f32((lines, ROWS))],
        in_specs=[smem] * 2 + [vmem] * 6 + [whole] * (2 * seq_count),
        out_specs=[vmem] * 3,
        scratch_shapes=[
            pltpu.VMEM((seq_count, head_count, HD, HD), jnp.bfloat16),
            pltpu.VMEM((token_count, HD), jnp.float32),
            pltpu.VMEM((user_rows, HD), jnp.float32),
            pltpu.SemaphoreType.DMA((2 * seq_count,)),
        ],
        compiler_params=params,
    )(
        position.reshape(1),
        prefix_lengths,
        slab_query,
        user_queries,
        slab_weights,
        user_weights,
        slab_local,
        user_local,
        *pieces,
    )

    squares = [square]
    for shift in range(1, head_axis):
        pairs = [(i, (i + shift) % head_axis) for i in range(head_axis)]
        squares.append(lax.ppermute(square, "head", pairs))

    chunk = width // 4
    slab_out, user_out = pl.pallas_call(
        functools.partial(norm_kernel, float(width * head_axis)),
        out_shape=[bf16((token_count, width)), bf16((user_rows, width))],
        grid=(width // chunk,),
        in_specs=[
            pl.BlockSpec((token_count, chunk), lambda i: (0, i)),
            pl.BlockSpec((user_rows, chunk), lambda i: (0, i)),
            pl.BlockSpec((1, chunk), lambda i: (0, i)),
        ]
        + [pl.BlockSpec((lines, ROWS), lambda i: (0, 0))] * head_axis,
        out_specs=[
            pl.BlockSpec((token_count, chunk), lambda i: (0, i)),
            pl.BlockSpec((user_rows, chunk), lambda i: (0, i)),
        ],
        scratch_shapes=[pltpu.VMEM((lines, ROWS, ROWS), jnp.float32)],
        compiler_params=params,
    )(slab_total, user_total, norm_gain.reshape(1, width), *squares)
    return slab_out, user_out.reshape(user_count, suffix, width)


def solution(mesh):
    return jax.shard_map(
        local,
        mesh=mesh,
        in_specs=(
            P("seq", "head"),
            P("seq", "head"),
            P("seq", "head"),
            P(None, "head", "seq"),
            P("head"),
            P("seq", None, "head"),
            P("seq", None, "head"),
            P("seq", None, "head"),
            P("seq", None, "head", None),
            P("seq"),
        ),
        out_specs=(P("seq", "head"), P("seq", None, "head")),
        check_vma=False,
    )
```

```python
import functools

import jax
import jax.numpy as jnp
from jax import lax
from jax.experimental import pallas as pl
from jax.experimental.pallas import tpu as pltpu
from jax.sharding import PartitionSpec as P

HEADS = 64
HD = 128
ROWS = 128
VMEM_BYTES = 20 * 1024 * 1024
STATE_VMEM_BYTES = 62 * 1024 * 1024
LOCAL_VMEM_BYTES = 52 * 1024 * 1024


def matmul(a, b, contract):
    return lax.dot_general(a, b, (contract, ((), ())), preferred_element_type=jnp.float32)


def load_columns(sources, targets, sems, chunks):
    copies = []
    for chunk in range(chunks):
        group = []
        for i, (source, target) in enumerate(zip(sources, targets)):
            size = source.shape[1] // chunks
            cols = pl.ds(chunk * size, size)
            group.append(pltpu.make_async_copy(source.at[:, cols], target.at[:, cols], sems.at[i, chunk]))
            group[-1].start()
        copies.append(group)

    def wait(chunk):
        for copy in copies[chunk]:
            copy.wait()

    return wait


def state_kernel(chunks, key_hbm, value_hbm, out_ref, key_ref, value_ref, sems):
    head_count = out_ref.shape[0]
    wait = load_columns((key_hbm, value_hbm), (key_ref, value_ref), sems, chunks)
    for head in range(head_count):
        if head % (head_count // chunks) == 0:
            wait(head // (head_count // chunks))
        cols = slice(head * HD, (head + 1) * HD)
        state = matmul(key_ref[:, cols], value_ref[:, cols], ((0,), (0,)))
        out_ref[head] = state.astype(jnp.bfloat16)


def split_kernel(count, half, order_ref, *refs):
    for i in range(count):
        for head in range(half):
            refs[count + 2 * i][head] = refs[i][head]
            refs[count + 2 * i + 1][head] = refs[i][half + head]


def choose_levels(target, position, depth, level_count, head_count):
    block_count = 1 << depth
    shift = head_count.bit_length() - 1
    shape = (level_count * head_count, (block_count + 1) * head_count)
    row = lax.broadcasted_iota(jnp.int32, shape, 0)
    col = lax.broadcasted_iota(jnp.int32, shape, 1)
    level = row >> shift
    offset = col >> shift
    block = offset ^ position
    diff = block ^ target
    chosen = jnp.logical_and(level == 0, offset == block_count)
    below = jnp.logical_and(offset < block_count, block < target)
    for step in range(1, depth + 1):
        span = jnp.logical_and(diff >= (1 << (step - 1)), diff < (1 << step))
        chosen = jnp.logical_or(chosen, jnp.logical_and(below, jnp.logical_and(span, level == step)))
    same = (row & (head_count - 1)) == (col & (head_count - 1))
    return jnp.where(jnp.logical_and(chosen, same), 1.0, 0.0).astype(jnp.bfloat16)


def local_kernel(depth, suffix, chunks, length_ref, sw_ref, uw_ref, *rest):
    sources, (so_ref, uo_ref, sc_ref, uc_ref), loaded, sems = rest[:6], rest[6:10], rest[10:16], rest[16]
    sq_ref, sk_ref, sv_ref, uq_ref, uk_ref, uv_ref = loaded
    wait = load_columns(sources, loaded, sems, chunks)
    head_count = sq_ref.shape[1] // HD
    level_count = sw_ref.shape[0] // head_count
    position = lax.axis_index("seq").astype(jnp.int32)
    pick = functools.partial(
        choose_levels, position=position, depth=depth, level_count=level_count, head_count=head_count
    )
    sc_ref[...] = matmul(sw_ref[...], pick(position), ((0,), (0,)))
    for user in range(uw_ref.shape[0]):
        weights = matmul(uw_ref[user], pick(length_ref[user]), ((0,), (0,)))
        uc_ref[user * suffix : (user + 1) * suffix] = weights
    own = (1 << depth) * head_count
    row = lax.broadcasted_iota(jnp.int32, (ROWS, ROWS), 0)
    col = lax.broadcasted_iota(jnp.int32, (ROWS, ROWS), 1)
    causal = row >= col
    within = jnp.logical_and(causal, row // suffix == col // suffix)
    parts = [(sq_ref, sk_ref, sv_ref, sc_ref, so_ref, causal), (uq_ref, uk_ref, uv_ref, uc_ref, uo_ref, within)]
    for head in range(head_count):
        if head % (head_count // chunks) == 0:
            wait(head // (head_count // chunks))
        cols = slice(head * HD, (head + 1) * HD)
        for q_ref, k_ref, v_ref, c_ref, o_ref, mask in parts:
            for start in range(0, q_ref.shape[0], ROWS):
                rows = slice(start, start + ROWS)
                scores = matmul(q_ref[rows, cols], k_ref[rows, cols], ((1,), (1,)))
                scores = jnp.where(mask, scores, 0.0).astype(jnp.bfloat16)
                result = matmul(scores, v_ref[rows, cols], ((1,), (0,)))
                o_ref[rows, cols] = result * c_ref[rows, own + head : own + head + 1]


def add_blocks(groups, state_refs, head_count, head, q_ref, c_ref, base):
    cols = slice(head * HD, (head + 1) * HD)
    query = q_ref[:, cols]
    total = base
    for group in groups:
        scaled = []
        for offset in group:
            column = offset * head_count + head
            weight = jnp.broadcast_to(c_ref[:, column : column + 1], query.shape).astype(jnp.bfloat16)
            scaled.append(query * weight)
        states = []
        for offset in group:
            parts = state_refs[offset]
            share = head_count // len(parts)
            states.append(parts[head // share][head % share])
        total = total + matmul(jnp.concatenate(scaled, axis=1), jnp.concatenate(states, axis=0), ((1,), (0,)))
    return total


def read_kernel(groups, halves, last, sq_ref, uq_ref, sc_ref, uc_ref, sa_ref, ua_ref, *rest):
    head_count = sq_ref.shape[1] // HD
    state_refs = {}
    used = 0
    for offset in [offset for group in groups for offset in group]:
        state_refs[offset] = rest[used : used + halves]
        used += halves
    st_ref, ut_ref = rest[used : used + 2]
    squares = {}
    for head in range(head_count):
        cols = slice(head * HD, (head + 1) * HD)
        for side, (q_ref, c_ref, a_ref, t_ref) in enumerate(
            ((sq_ref, sc_ref, sa_ref, st_ref), (uq_ref, uc_ref, ua_ref, ut_ref))
        ):
            total = add_blocks(groups, state_refs, head_count, head, q_ref, c_ref, a_ref[:, cols])
            t_ref[:, cols] = total
            if last:
                acc_ref = rest[used + 3 + side]
                if head == 0:
                    acc_ref[...] = total * total
                else:
                    acc_ref[...] += total * total
    if last:
        square_ref = rest[used + 2]
        line = 0
        for acc_ref in rest[used + 3 : used + 5]:
            for start in range(0, acc_ref.shape[0], ROWS):
                turned = jnp.transpose(acc_ref[start : start + ROWS])
                value = jnp.sum(turned, axis=0, keepdims=True)
                for copy in range(square_ref.shape[0]):
                    square_ref[copy, line : line + 1] = value
                line += 1


def norm_kernel(features, st_ref, ut_ref, gain_ref, square_ref, so_ref, uo_ref, scale_ref):
    @pl.when(pl.program_id(0) == 0)
    def _():
        total = square_ref[0]
        for part in range(1, square_ref.shape[0]):
            total = total + square_ref[part]
        scale = lax.rsqrt(total / features + 1e-06)
        for line in range(scale.shape[0]):
            spread = jnp.broadcast_to(scale[line : line + 1], (ROWS, ROWS))
            scale_ref[line] = jnp.transpose(spread)

    gain = gain_ref[...].astype(jnp.float32)
    line = 0
    for t_ref, o_ref in ((st_ref, so_ref), (ut_ref, uo_ref)):
        for start in range(0, t_ref.shape[0], ROWS):
            rows = slice(start, start + ROWS)
            for low in range(0, t_ref.shape[1], HD):
                cols = slice(low, low + HD)
                o_ref[rows, cols] = (t_ref[rows, cols] * scale_ref[line] * gain[:, cols]).astype(jnp.bfloat16)
            line += 1


def local(
    slab_query,
    slab_key,
    slab_value,
    slab_levels,
    norm_gain,
    user_query,
    user_key,
    user_value,
    user_levels,
    prefix_lengths,
):
    seq_count = lax.axis_size("seq")
    head_axis = lax.axis_size("head")
    depth = seq_count.bit_length() - 1
    token_count, width = slab_query.shape
    head_count = width // HD
    half = head_count // 2
    user_count, suffix = user_query.shape[:2]
    user_rows = user_count * suffix
    lines = (token_count + user_rows) // ROWS
    params = pltpu.CompilerParams(vmem_limit_bytes=VMEM_BYTES)
    state_params = pltpu.CompilerParams(vmem_limit_bytes=STATE_VMEM_BYTES)
    local_params = pltpu.CompilerParams(vmem_limit_bytes=LOCAL_VMEM_BYTES)
    f32 = functools.partial(jax.ShapeDtypeStruct, dtype=jnp.float32)
    bf16 = functools.partial(jax.ShapeDtypeStruct, dtype=jnp.bfloat16)
    vmem = pl.BlockSpec(memory_space=pltpu.VMEM)
    smem = pl.BlockSpec(memory_space=pltpu.SMEM)
    anywhere = pl.BlockSpec(memory_space=pl.ANY)
    hbm = pl.BlockSpec(memory_space=pltpu.HBM)
    chunks = min(4, half)
    rows_cost = 2 * width * (token_count + user_rows)

    def cost(flops, moved):
        return pl.CostEstimate(flops=flops, bytes_accessed=moved, transcendentals=0)

    def swap(value, bit):
        return lax.ppermute(value, "seq", [(i, i ^ (1 << bit)) for i in range(seq_count)])

    state = pl.pallas_call(
        functools.partial(state_kernel, chunks),
        out_shape=bf16((head_count, HD, HD)),
        in_specs=[hbm] * 2,
        out_specs=vmem,
        scratch_shapes=[pltpu.VMEM((token_count, width), jnp.bfloat16)] * 2 + [pltpu.SemaphoreType.DMA((2, chunks))],
        compiler_params=state_params,
    )(slab_key, slab_value)

    outer = list(range(1, depth))
    whole = {0: state}
    for bit in outer:
        whole[1 << bit] = swap(state, bit)
    whole[1] = swap(state, 0)

    user_queries = user_query.reshape(user_rows, width)
    user_keys = user_key.reshape(user_rows, width)
    user_values = user_value.reshape(user_rows, width)
    columns = (seq_count + 1) * head_count
    slab_acc, user_acc, slab_coef, user_coef = pl.pallas_call(
        functools.partial(local_kernel, depth, suffix, chunks),
        out_shape=[
            f32((token_count, width)),
            f32((user_rows, width)),
            f32((token_count, columns)),
            f32((user_rows, columns)),
        ],
        in_specs=[smem] + [vmem] * 2 + [hbm] * 6,
        out_specs=[vmem] * 4,
        scratch_shapes=[pltpu.VMEM((token_count, width), jnp.bfloat16)] * 3
        + [pltpu.VMEM((user_rows, width), jnp.bfloat16)] * 3
        + [pltpu.SemaphoreType.DMA((6, chunks))],
        compiler_params=local_params,
        cost_estimate=cost(ROWS, ROWS),
    )(
        prefix_lengths,
        slab_levels.reshape(-1, token_count),
        user_levels.reshape(user_count, -1, suffix),
        slab_query,
        slab_key,
        slab_value,
        user_queries,
        user_keys,
        user_values,
    )

    sides = {}
    received = lax.optimization_barrier((slab_coef, *[whole[1 << bit] for bit in outer]))[1:]
    for bit, value in zip(outer, received):
        whole[1 << bit] = value
    if len(outer) > 1:
        split = pl.pallas_call(
            functools.partial(split_kernel, len(outer), half),
            out_shape=[bf16((half, HD, HD))] * (2 * len(outer)),
            in_specs=[anywhere] + [vmem] * len(outer),
            out_specs=[vmem] * (2 * len(outer)),
            compiler_params=params,
        )(slab_coef, *received)
        for i, bit in enumerate(outer):
            sides[1 << bit] = [split[2 * i], split[2 * i + 1]]
    later = sorted((m for m in range(0, seq_count, 2) if m.bit_count() > 1), key=lambda m: m.bit_count())
    for m in later:
        high, low = m.bit_length() - 1, (m & -m).bit_length() - 1
        sides[m] = [swap(sides[m ^ (1 << high)][0], high), swap(sides[m ^ (1 << low)][1], low)]
    def read(groups, states, halves, accs, last):
        outs = [f32((token_count, width)), f32((user_rows, width))]
        scratch = []
        if last:
            outs.append(f32((head_axis, lines, ROWS)))
            scratch = [pltpu.VMEM((token_count, HD), jnp.float32), pltpu.VMEM((user_rows, HD), jnp.float32)]
        return pl.pallas_call(
            functools.partial(read_kernel, groups, halves, last),
            out_shape=outs,
            in_specs=[vmem] * (6 + len(states)),
            out_specs=[vmem] * len(outs),
            scratch_shapes=scratch,
            compiler_params=params,
            cost_estimate=cost(ROWS, ROWS),
        )(slab_query, user_queries, slab_coef, user_coef, *accs, *states)

    def after(results, values):
        return list(lax.optimization_barrier((results, values))[1])

    def read_whole(offsets, accs):
        groups = [tuple(offsets[i : i + 2]) for i in range(0, len(offsets), 2)]
        return read(groups, [whole[m] for m in offsets], 1, accs, False)

    direct = [1 << bit for bit in outer]
    if later:
        for m, value in zip(direct, after(sides[direct[0]], [whole[m] for m in direct])):
            whole[m] = value
    accs = read_whole([0, 1] + direct, (slab_acc, user_acc))
    for m, value in zip(direct, after(accs[0], [whole[m] for m in direct])):
        whole[m | 1] = swap(value, 0)
    accs = read_whole([m | 1 for m in direct], accs)
    for m in later:
        sides[m | 1] = [swap(piece, 0) for piece in after(accs[0], sides[m])]
    late = [(m, m | 1) for m in later]
    late_states = [piece for group in late for m in group for piece in sides[m]]
    slab_total, user_total, square = read(late, late_states, 2, accs, True)

    squares = lax.all_to_all(square, "head", 0, 0)

    chunk = width // 4
    slab_out, user_out = pl.pallas_call(
        functools.partial(norm_kernel, float(width * head_axis)),
        out_shape=[bf16((token_count, width)), bf16((user_rows, width))],
        grid=(width // chunk,),
        in_specs=[
            pl.BlockSpec((token_count, chunk), lambda i: (0, i)),
            pl.BlockSpec((user_rows, chunk), lambda i: (0, i)),
            pl.BlockSpec((1, chunk), lambda i: (0, i)),
            pl.BlockSpec((head_axis, lines, ROWS), lambda i: (0, 0, 0)),
        ],
        out_specs=[
            pl.BlockSpec((token_count, chunk), lambda i: (0, i)),
            pl.BlockSpec((user_rows, chunk), lambda i: (0, i)),
        ],
        scratch_shapes=[pltpu.VMEM((lines, ROWS, ROWS), jnp.float32)],
        compiler_params=params,
    )(slab_total, user_total, norm_gain.reshape(1, width), squares)
    return slab_out, user_out.reshape(user_count, suffix, width)


def solution(mesh):
    return jax.shard_map(
        local,
        mesh=mesh,
        in_specs=(
            P("seq", "head"),
            P("seq", "head"),
            P("seq", "head"),
            P(None, "head", "seq"),
            P("head"),
            P("seq", None, "head"),
            P("seq", None, "head"),
            P("seq", None, "head"),
            P("seq", None, "head", None),
            P("seq"),
        ),
        out_specs=(P("seq", "head"), P("seq", None, "head")),
        check_vma=False,
    )
```

```python
import functools

import jax
import jax.numpy as jnp
from jax import lax
from jax.experimental import pallas as pl
from jax.experimental.pallas import tpu as pltpu
from jax.sharding import PartitionSpec as P

HEADS = 64
HD = 128
ROWS = 128
VMEM_BYTES = 20 * 1024 * 1024


def matmul(a, b, contract):
    return lax.dot_general(a, b, (contract, ((), ())), preferred_element_type=jnp.float32)


def load_columns(sources, targets, sems, chunks):
    copies = []
    for chunk in range(chunks):
        group = []
        for i, (source, target) in enumerate(zip(sources, targets)):
            size = source.shape[1] // chunks
            cols = pl.ds(chunk * size, size)
            group.append(pltpu.make_async_copy(source.at[:, cols], target.at[:, cols], sems.at[i, chunk]))
            group[-1].start()
        copies.append(group)

    def wait(chunk):
        for copy in copies[chunk]:
            copy.wait()

    return wait


def state_kernel(chunks, key_hbm, value_hbm, out_ref, key_ref, value_ref, sems):
    head_count = out_ref.shape[0]
    wait = load_columns((key_hbm, value_hbm), (key_ref, value_ref), sems, chunks)
    for head in range(head_count):
        if head % (head_count // chunks) == 0:
            wait(head // (head_count // chunks))
        cols = slice(head * HD, (head + 1) * HD)
        state = matmul(key_ref[:, cols], value_ref[:, cols], ((0,), (0,)))
        out_ref[head] = state.astype(jnp.bfloat16)


def split_kernel(picks, order_ref, *refs):
    for (i, side), out_ref in zip(picks, refs[len(refs) - len(picks) :]):
        half = out_ref.shape[0]
        for head in range(half):
            out_ref[head] = refs[i][side * half + head]


def choose_levels(target, position, depth, level_count, head_count):
    block_count = 1 << depth
    shift = head_count.bit_length() - 1
    shape = (level_count * head_count, (block_count + 1) * head_count)
    row = lax.broadcasted_iota(jnp.int32, shape, 0)
    col = lax.broadcasted_iota(jnp.int32, shape, 1)
    level = row >> shift
    offset = col >> shift
    block = offset ^ position
    diff = block ^ target
    chosen = jnp.logical_and(level == 0, offset == block_count)
    below = jnp.logical_and(offset < block_count, block < target)
    for step in range(1, depth + 1):
        span = jnp.logical_and(diff >= (1 << (step - 1)), diff < (1 << step))
        chosen = jnp.logical_or(chosen, jnp.logical_and(below, jnp.logical_and(span, level == step)))
    same = (row & (head_count - 1)) == (col & (head_count - 1))
    return jnp.where(jnp.logical_and(chosen, same), 1.0, 0.0).astype(jnp.bfloat16)


def local_kernel(depth, suffix, chunks, *refs):
    small, sources, (so_ref, uo_ref, sc_ref, uc_ref) = refs[:3], refs[3:9], refs[9:13]
    small_loaded, loaded, small_sems, sems = refs[13:16], refs[16:22], refs[22], refs[23]
    length_ref, sw_ref, uw_ref = small_loaded
    sq_ref, sk_ref, sv_ref, uq_ref, uk_ref, uv_ref = loaded
    small_copies = [
        pltpu.make_async_copy(source, target, small_sems.at[i])
        for i, (source, target) in enumerate(zip(small, small_loaded))
    ]
    for copy in small_copies:
        copy.start()
    wait = load_columns(sources, loaded, sems, chunks)
    for copy in small_copies:
        copy.wait()
    head_count = sq_ref.shape[1] // HD
    level_count = sw_ref.shape[0] // head_count
    position = lax.axis_index("seq").astype(jnp.int32)
    pick = functools.partial(
        choose_levels, position=position, depth=depth, level_count=level_count, head_count=head_count
    )
    sc_ref[...] = matmul(sw_ref[...], pick(position), ((0,), (0,)))
    for user in range(uw_ref.shape[0]):
        weights = matmul(uw_ref[user], pick(length_ref[user]), ((0,), (0,)))
        uc_ref[user * suffix : (user + 1) * suffix] = weights
    own = (1 << depth) * head_count
    row = lax.broadcasted_iota(jnp.int32, (ROWS, ROWS), 0)
    col = lax.broadcasted_iota(jnp.int32, (ROWS, ROWS), 1)
    causal = row >= col
    within = jnp.logical_and(causal, row // suffix == col // suffix)
    parts = [(sq_ref, sk_ref, sv_ref, sc_ref, so_ref, causal), (uq_ref, uk_ref, uv_ref, uc_ref, uo_ref, within)]
    step = 2
    for first in range(0, head_count, step):
        if first % (head_count // chunks) == 0:
            wait(first // (head_count // chunks))
        units = [
            (head, slice(head * HD, (head + 1) * HD), slice(start, start + ROWS), part)
            for head in range(first, first + step)
            for part in parts
            for start in range(0, part[0].shape[0], ROWS)
        ]
        scores = [matmul(part[0][rows, cols], part[1][rows, cols], ((1,), (1,))) for _, cols, rows, part in units]
        scores = [jnp.where(unit[3][5], score, 0.0).astype(jnp.bfloat16) for unit, score in zip(units, scores)]
        results = [
            matmul(score, part[2][rows, cols], ((1,), (0,))) for score, (_, cols, rows, part) in zip(scores, units)
        ]
        for result, (head, cols, rows, part) in zip(results, units):
            part[4][rows, cols] = result * part[3][rows, own + head : own + head + 1]


def add_blocks(groups, state_refs, head_count, head, q_ref, c_ref, base):
    cols = slice(head * HD, (head + 1) * HD)
    query = q_ref[:, cols]
    total = base
    for group in groups:
        scaled = []
        for offset in group:
            column = offset * head_count + head
            weight = jnp.broadcast_to(c_ref[:, column : column + 1], query.shape).astype(jnp.bfloat16)
            scaled.append(query * weight)
        states = []
        for offset in group:
            parts = state_refs[offset]
            share = head_count // len(parts)
            states.append(parts[head // share][head % share])
        total = total + matmul(jnp.concatenate(scaled, axis=1), jnp.concatenate(states, axis=0), ((1,), (0,)))
    return total


def read_kernel(groups, halves, last, sq_ref, uq_ref, sc_ref, uc_ref, sa_ref, ua_ref, *rest):
    head_count = sq_ref.shape[1] // HD
    state_refs = {}
    used = 0
    for offset in [offset for group in groups for offset in group]:
        state_refs[offset] = rest[used : used + halves]
        used += halves
    st_ref, ut_ref = rest[used : used + 2]
    squares = {}
    for head in range(head_count):
        cols = slice(head * HD, (head + 1) * HD)
        for side, (q_ref, c_ref, a_ref, t_ref) in enumerate(
            ((sq_ref, sc_ref, sa_ref, st_ref), (uq_ref, uc_ref, ua_ref, ut_ref))
        ):
            total = add_blocks(groups, state_refs, head_count, head, q_ref, c_ref, a_ref[:, cols])
            t_ref[:, cols] = total
            if last:
                acc_ref = rest[used + 3 + side]
                if head == 0:
                    acc_ref[...] = total * total
                else:
                    acc_ref[...] += total * total
    if last:
        square_ref = rest[used + 2]
        line = 0
        for acc_ref in rest[used + 3 : used + 5]:
            for start in range(0, acc_ref.shape[0], ROWS):
                turned = jnp.transpose(acc_ref[start : start + ROWS])
                square_ref[line : line + 1] = jnp.sum(turned, axis=0, keepdims=True)
                line += 1


def norm_kernel(features, chunks, st_ref, ut_ref, gain_ref, one_ref, two_ref, so_hbm, uo_hbm, so_ref, uo_ref, sems):
    square = one_ref[...] + two_ref[...]
    scale = lax.rsqrt(square / features + 1e-06)
    scales = [jnp.transpose(jnp.broadcast_to(scale[line : line + 1], (ROWS, ROWS))) for line in range(scale.shape[0])]
    size = st_ref.shape[1] // chunks
    copies = []
    for chunk in range(chunks):
        line = 0
        wide = pl.ds(chunk * size, size)
        for side, (t_ref, o_ref, o_hbm) in enumerate(((st_ref, so_ref, so_hbm), (ut_ref, uo_ref, uo_hbm))):
            for start in range(0, t_ref.shape[0], ROWS):
                rows = slice(start, start + ROWS)
                for low in range(chunk * size, (chunk + 1) * size, HD):
                    cols = slice(low, low + HD)
                    gain = gain_ref[:, cols].astype(jnp.float32)
                    o_ref[rows, cols] = (t_ref[rows, cols] * scales[line] * gain).astype(jnp.bfloat16)
                line += 1
            copies.append(pltpu.make_async_copy(o_ref.at[:, wide], o_hbm.at[:, wide], sems.at[side, chunk]))
            copies[-1].start()
    for copy in copies:
        copy.wait()


def local(
    slab_query,
    slab_key,
    slab_value,
    slab_levels,
    norm_gain,
    user_query,
    user_key,
    user_value,
    user_levels,
    prefix_lengths,
):
    seq_count = lax.axis_size("seq")
    head_axis = lax.axis_size("head")
    depth = seq_count.bit_length() - 1
    token_count, width = slab_query.shape
    head_count = width // HD
    half = head_count // 2
    user_count, suffix = user_query.shape[:2]
    user_rows = user_count * suffix
    lines = (token_count + user_rows) // ROWS
    params = pltpu.CompilerParams(vmem_limit_bytes=VMEM_BYTES)
    bf16 = functools.partial(jax.ShapeDtypeStruct, dtype=jnp.bfloat16)
    vmem = pl.BlockSpec(memory_space=pltpu.VMEM)
    anywhere = pl.BlockSpec(memory_space=pl.ANY)
    hbm = pl.BlockSpec(memory_space=pltpu.HBM)
    chunks = min(4, half)
    rows_cost = 2 * width * (token_count + user_rows)

    def pinned(*arrays):
        return [pltpu.with_memory_space_constraint(array, pltpu.HBM) for array in arrays]

    def cost(flops, moved):
        return pl.CostEstimate(flops=flops, bytes_accessed=moved, transcendentals=0)

    def swap(value, bit):
        return lax.ppermute(value, "seq", [(i, i ^ (1 << bit)) for i in range(seq_count)])

    state = pl.pallas_call(
        functools.partial(state_kernel, chunks),
        out_shape=pltpu.VMEM((head_count, HD, HD), jnp.bfloat16),
        in_specs=[hbm] * 2,
        out_specs=vmem,
        scratch_shapes=[pltpu.VMEM((token_count, width), jnp.bfloat16)] * 2 + [pltpu.SemaphoreType.DMA((2, chunks))],
        compiler_params=params,
    )(*pinned(slab_key, slab_value))

    outer = list(range(1, depth))
    whole = {0: state}
    for bit in outer:
        whole[1 << bit] = swap(state, bit)
    whole[1] = swap(state, 0)

    user_queries = user_query.reshape(user_rows, width)
    user_keys = user_key.reshape(user_rows, width)
    user_values = user_value.reshape(user_rows, width)
    slab_table = slab_levels.reshape(-1, token_count)
    user_table = user_levels.reshape(user_count, -1, suffix)
    columns = (seq_count + 1) * head_count
    slab_acc, user_acc, slab_coef, user_coef = pl.pallas_call(
        functools.partial(local_kernel, depth, suffix, chunks),
        out_shape=[
            pltpu.VMEM((token_count, width), jnp.float32),
            pltpu.VMEM((user_rows, width), jnp.float32),
            pltpu.VMEM((token_count, columns), jnp.float32),
            pltpu.VMEM((user_rows, columns), jnp.float32),
        ],
        in_specs=[hbm] * 9,
        out_specs=[vmem] * 4,
        scratch_shapes=[
            pltpu.SMEM((user_count,), jnp.int32),
            pltpu.VMEM(slab_table.shape, jnp.bfloat16),
            pltpu.VMEM(user_table.shape, jnp.bfloat16),
        ]
        + [pltpu.VMEM((token_count, width), jnp.bfloat16)] * 3
        + [pltpu.VMEM((user_rows, width), jnp.bfloat16)] * 3
        + [pltpu.SemaphoreType.DMA((3,)), pltpu.SemaphoreType.DMA((6, chunks))],
        compiler_params=params,
        cost_estimate=cost(ROWS, ROWS),
    )(
        *pinned(prefix_lengths, slab_table, user_table),
        *pinned(slab_query, slab_key, slab_value, user_queries, user_keys, user_values),
    )

    sides = {}
    received = lax.optimization_barrier((slab_coef, *[whole[1 << bit] for bit in outer]))[1:]
    for bit, value in zip(outer, received):
        whole[1 << bit] = value
    if len(outer) > 1:
        picks = [(i, 0) for i in range(len(outer) - 1)] + [(i, 1) for i in range(1, len(outer))]
        split = pl.pallas_call(
            functools.partial(split_kernel, picks),
            out_shape=[pltpu.VMEM((half, HD, HD), jnp.bfloat16)] * len(picks),
            in_specs=[anywhere] + [vmem] * len(outer),
            out_specs=[vmem] * len(picks),
            compiler_params=params,
        )(slab_coef, *received)
        for bit in outer:
            sides[1 << bit] = [None, None]
        for (i, side), value in zip(picks, split):
            sides[1 << outer[i]][side] = value
    later = sorted((m for m in range(0, seq_count, 2) if m.bit_count() > 1), key=lambda m: m.bit_count())
    for m in later:
        high, low = m.bit_length() - 1, (m & -m).bit_length() - 1
        sides[m] = [swap(sides[m ^ (1 << high)][0], high), swap(sides[m ^ (1 << low)][1], low)]
    def read(groups, states, halves, accs, last):
        outs = [pltpu.VMEM((token_count, width), jnp.float32), pltpu.VMEM((user_rows, width), jnp.float32)]
        scratch = []
        if last:
            outs.append(pltpu.VMEM((lines, ROWS), jnp.float32))
            scratch = [pltpu.VMEM((token_count, HD), jnp.float32), pltpu.VMEM((user_rows, HD), jnp.float32)]
        return pl.pallas_call(
            functools.partial(read_kernel, groups, halves, last),
            out_shape=outs,
            in_specs=[vmem] * (6 + len(states)),
            out_specs=[vmem] * len(outs),
            scratch_shapes=scratch,
            compiler_params=params,
            cost_estimate=cost(ROWS, ROWS),
        )(slab_query, user_queries, slab_coef, user_coef, *accs, *states)

    def after(results, values):
        return list(lax.optimization_barrier((results, values))[1])

    def read_whole(offsets, accs):
        groups = [tuple(offsets[i : i + 2]) for i in range(0, len(offsets), 2)]
        return read(groups, [whole[m] for m in offsets], 1, accs, False)

    direct = [1 << bit for bit in outer]
    if later:
        for m, value in zip(direct, after(split, [whole[m] for m in direct])):
            whole[m] = value
    for m in direct:
        whole[m | 1] = swap(whole[m], 0)
    accs = read_whole([0, 1] + direct, (slab_acc, user_acc))
    accs = read_whole([m | 1 for m in direct], accs)
    for m in later:
        sides[m | 1] = [swap(piece, 0) for piece in after(accs[0], sides[m])]
    late = [(m, m | 1) for m in later]
    late_states = [piece for group in late for m in group for piece in sides[m]]
    slab_total, user_total, square = read(late, late_states, 2, accs, True)

    mate = jnp.zeros_like(square)
    for bit in range(head_axis.bit_length() - 1):
        square = square + mate
        mate = lax.ppermute(square, "head", [(i, i ^ (1 << bit)) for i in range(head_axis)])

    slab_out, user_out = pl.pallas_call(
        functools.partial(norm_kernel, float(width * head_axis), chunks),
        out_shape=[bf16((token_count, width)), bf16((user_rows, width))],
        in_specs=[vmem] * 5,
        out_specs=[hbm] * 2,
        scratch_shapes=[
            pltpu.VMEM((token_count, width), jnp.bfloat16),
            pltpu.VMEM((user_rows, width), jnp.bfloat16),
            pltpu.SemaphoreType.DMA((2, chunks)),
        ],
        compiler_params=params,
    )(slab_total, user_total, norm_gain.reshape(1, width), square, mate)
    return slab_out, user_out.reshape(user_count, suffix, width)


def solution(mesh):
    return jax.shard_map(
        local,
        mesh=mesh,
        in_specs=(
            P("seq", "head"),
            P("seq", "head"),
            P("seq", "head"),
            P(None, "head", "seq"),
            P("head"),
            P("seq", None, "head"),
            P("seq", None, "head"),
            P("seq", None, "head"),
            P("seq", None, "head", None),
            P("seq"),
        ),
        out_specs=(P("seq", "head"), P("seq", None, "head")),
        check_vma=False,
    )
```

```python
import functools

import jax
import jax.numpy as jnp
from jax import lax
from jax.experimental import pallas as pl
from jax.experimental.pallas import tpu as pltpu
from jax.sharding import PartitionSpec as P

HEADS = 64
HD = 128
ROWS = 128
VMEM_BYTES = 20 * 1024 * 1024


def matmul(a, b, contract):
    return lax.dot_general(a, b, (contract, ((), ())), preferred_element_type=jnp.float32)


def load_columns(sources, targets, sems, chunks):
    copies = []
    for chunk in range(chunks):
        group = []
        for i, (source, target) in enumerate(zip(sources, targets)):
            size = source.shape[1] // chunks
            cols = pl.ds(chunk * size, size)
            group.append(pltpu.make_async_copy(source.at[:, cols], target.at[:, cols], sems.at[i, chunk]))
            group[-1].start()
        copies.append(group)

    def wait(chunk):
        for copy in copies[chunk]:
            copy.wait()

    return wait


def state_kernel(chunks, key_hbm, value_hbm, first_ref, second_ref, whole_ref, key_ref, value_ref, sems):
    half = first_ref.shape[0]
    head_count = 2 * half
    wait = load_columns((key_hbm, value_hbm), (key_ref, value_ref), sems, chunks)
    for head in range(head_count):
        if head % (head_count // chunks) == 0:
            wait(head // (head_count // chunks))
        cols = slice(head * HD, (head + 1) * HD)
        state = matmul(key_ref[:, cols], value_ref[:, cols], ((0,), (0,))).astype(jnp.bfloat16)
        whole_ref[0, head] = state
        if head < half:
            first_ref[head] = state
        else:
            second_ref[head - half] = state


def join_kernel(order_ref, *refs):
    out_ref = refs[-1]
    half = out_ref.shape[1] // 2
    for i in range(out_ref.shape[0]):
        for side in range(2):
            for head in range(half):
                out_ref[i, side * half + head] = refs[2 * i + side][head]


def choose_levels(target, position, depth, level_count, head_count):
    block_count = 1 << depth
    shift = head_count.bit_length() - 1
    shape = (level_count * head_count, (block_count + 1) * head_count)
    row = lax.broadcasted_iota(jnp.int32, shape, 0)
    col = lax.broadcasted_iota(jnp.int32, shape, 1)
    level = row >> shift
    offset = col >> shift
    block = offset ^ position
    diff = block ^ target
    chosen = jnp.logical_and(level == 0, offset == block_count)
    below = jnp.logical_and(offset < block_count, block < target)
    for step in range(1, depth + 1):
        span = jnp.logical_and(diff >= (1 << (step - 1)), diff < (1 << step))
        chosen = jnp.logical_or(chosen, jnp.logical_and(below, jnp.logical_and(span, level == step)))
    same = (row & (head_count - 1)) == (col & (head_count - 1))
    return jnp.where(jnp.logical_and(chosen, same), 1.0, 0.0).astype(jnp.bfloat16)


def attend(mask, chunks, wait, q_ref, k_ref, v_ref, c_ref, o_ref, own):
    head_count = q_ref.shape[1] // HD
    step = 2
    for first in range(0, head_count, step):
        if first % (head_count // chunks) == 0:
            wait(first // (head_count // chunks))
        units = [
            (head, slice(head * HD, (head + 1) * HD), slice(start, start + ROWS))
            for head in range(first, first + step)
            for start in range(0, q_ref.shape[0], ROWS)
        ]
        scores = [matmul(q_ref[rows, cols], k_ref[rows, cols], ((1,), (1,))) for _, cols, rows in units]
        scores = [jnp.where(mask, score, 0.0).astype(jnp.bfloat16) for score in scores]
        results = [matmul(score, v_ref[rows, cols], ((1,), (0,))) for score, (_, cols, rows) in zip(scores, units)]
        for result, (head, cols, rows) in zip(results, units):
            o_ref[rows, cols] = result * c_ref[rows, own + head : own + head + 1]


def local_kernel(depth, suffix, chunks, *refs):
    small_count = 2 if suffix else 1
    refs = list(refs)
    take = lambda count: [refs.pop(0) for _ in range(count)]
    small, sources, (o_ref, c_ref), small_loaded, loaded = take(small_count), take(3), take(2), take(small_count), take(3)
    small_sems, sems = refs
    small_copies = [
        pltpu.make_async_copy(source, target, small_sems.at[i])
        for i, (source, target) in enumerate(zip(small, small_loaded))
    ]
    for copy in small_copies:
        copy.start()
    wait = load_columns(sources, loaded, sems, chunks)
    for copy in small_copies:
        copy.wait()
    weight_ref = small_loaded[-1]
    head_count = loaded[0].shape[1] // HD
    position = lax.axis_index("seq").astype(jnp.int32)
    pick = functools.partial(
        choose_levels,
        position=position,
        depth=depth,
        level_count=weight_ref.shape[-2] // head_count,
        head_count=head_count,
    )
    row = lax.broadcasted_iota(jnp.int32, (ROWS, ROWS), 0)
    col = lax.broadcasted_iota(jnp.int32, (ROWS, ROWS), 1)
    mask = row >= col
    if suffix:
        mask = jnp.logical_and(mask, row // suffix == col // suffix)
        for user in range(weight_ref.shape[0]):
            weights = matmul(weight_ref[user], pick(small_loaded[0][user]), ((0,), (0,)))
            c_ref[user * suffix : (user + 1) * suffix] = weights
    else:
        c_ref[...] = matmul(weight_ref[...], pick(position), ((0,), (0,)))
    attend(mask, chunks, wait, *loaded, c_ref, o_ref, (1 << depth) * head_count)


def add_blocks(groups, state_refs, head_count, head, q_ref, c_ref, base):
    cols = slice(head * HD, (head + 1) * HD)
    query = q_ref[:, cols]
    total = base
    for group in groups:
        scaled = []
        for offset in group:
            column = offset * head_count + head
            weight = jnp.broadcast_to(c_ref[:, column : column + 1], query.shape).astype(jnp.bfloat16)
            scaled.append(query * weight)
        states = [state_refs[offset][0][state_refs[offset][1], head] for offset in group]
        total = total + matmul(jnp.concatenate(scaled, axis=1), jnp.concatenate(states, axis=0), ((1,), (0,)))
    return total


def read_kernel(groups, places, last, sq_ref, uq_ref, sc_ref, uc_ref, sa_ref, ua_ref, *rest):
    head_count = sq_ref.shape[1] // HD
    used = 1 + max(which for which, _ in places.values())
    state_refs = {offset: (rest[which], index) for offset, (which, index) in places.items()}
    st_ref, ut_ref = rest[used : used + 2]
    for head in range(head_count):
        cols = slice(head * HD, (head + 1) * HD)
        for side, (q_ref, c_ref, a_ref, t_ref) in enumerate(
            ((sq_ref, sc_ref, sa_ref, st_ref), (uq_ref, uc_ref, ua_ref, ut_ref))
        ):
            total = add_blocks(groups, state_refs, head_count, head, q_ref, c_ref, a_ref[:, cols])
            t_ref[:, cols] = total
            if last:
                acc_ref = rest[used + 3 + side]
                if head == 0:
                    acc_ref[...] = total * total
                else:
                    acc_ref[...] += total * total
    if last:
        square_ref = rest[used + 2]
        line = 0
        for acc_ref in rest[used + 3 : used + 5]:
            for start in range(0, acc_ref.shape[0], ROWS):
                turned = jnp.transpose(acc_ref[start : start + ROWS])
                square_ref[line : line + 1] = jnp.sum(turned, axis=0, keepdims=True)
                line += 1


def norm_kernel(features, chunks, st_ref, ut_ref, gain_ref, one_ref, two_ref, so_hbm, uo_hbm, so_ref, uo_ref, sems):
    square = one_ref[...] + two_ref[...]
    scale = lax.rsqrt(square / features + 1e-06)
    scales = [jnp.transpose(jnp.broadcast_to(scale[line : line + 1], (ROWS, ROWS))) for line in range(scale.shape[0])]
    size = st_ref.shape[1] // chunks
    copies = []
    for chunk in range(chunks):
        line = 0
        wide = pl.ds(chunk * size, size)
        for side, (t_ref, o_ref, o_hbm) in enumerate(((st_ref, so_ref, so_hbm), (ut_ref, uo_ref, uo_hbm))):
            for start in range(0, t_ref.shape[0], ROWS):
                rows = slice(start, start + ROWS)
                for low in range(chunk * size, (chunk + 1) * size, HD):
                    cols = slice(low, low + HD)
                    gain = gain_ref[:, cols].astype(jnp.float32)
                    o_ref[rows, cols] = (t_ref[rows, cols] * scales[line] * gain).astype(jnp.bfloat16)
                line += 1
            copies.append(pltpu.make_async_copy(o_ref.at[:, wide], o_hbm.at[:, wide], sems.at[side, chunk]))
            copies[-1].start()
    for copy in copies:
        copy.wait()


def local(
    slab_query,
    slab_key,
    slab_value,
    slab_levels,
    norm_gain,
    user_query,
    user_key,
    user_value,
    user_levels,
    prefix_lengths,
):
    seq_count = lax.axis_size("seq")
    head_axis = lax.axis_size("head")
    depth = seq_count.bit_length() - 1
    token_count, width = slab_query.shape
    head_count = width // HD
    half = head_count // 2
    user_count, suffix = user_query.shape[:2]
    user_rows = user_count * suffix
    lines = (token_count + user_rows) // ROWS
    params = pltpu.CompilerParams(vmem_limit_bytes=VMEM_BYTES)
    bf16 = functools.partial(jax.ShapeDtypeStruct, dtype=jnp.bfloat16)
    vmem = pl.BlockSpec(memory_space=pltpu.VMEM)
    anywhere = pl.BlockSpec(memory_space=pl.ANY)
    hbm = pl.BlockSpec(memory_space=pltpu.HBM)
    chunks = min(4, half)
    rows_cost = 2 * width * (token_count + user_rows)

    def pinned(*arrays):
        return [pltpu.with_memory_space_constraint(array, pltpu.HBM) for array in arrays]

    def cost(flops, moved):
        return pl.CostEstimate(flops=flops, bytes_accessed=moved, transcendentals=0)

    def swap(value, bit):
        return lax.ppermute(value, "seq", [(i, i ^ (1 << bit)) for i in range(seq_count)])

    def after(results, values):
        return list(lax.optimization_barrier((results, values))[1])

    def join(order, halves):
        return pl.pallas_call(
            join_kernel,
            out_shape=pltpu.VMEM((len(halves) // 2, head_count, HD, HD), jnp.bfloat16),
            in_specs=[anywhere] + [vmem] * len(halves),
            out_specs=vmem,
            compiler_params=params,
        )(order, *halves)

    half_state = pltpu.VMEM((half, HD, HD), jnp.bfloat16)
    first, second, state = pl.pallas_call(
        functools.partial(state_kernel, chunks),
        out_shape=[half_state, half_state, pltpu.VMEM((1, head_count, HD, HD), jnp.bfloat16)],
        in_specs=[hbm] * 2,
        out_specs=[vmem] * 3,
        scratch_shapes=[pltpu.VMEM((token_count, width), jnp.bfloat16)] * 2 + [pltpu.SemaphoreType.DMA((2, chunks))],
        compiler_params=params,
    )(*pinned(slab_key, slab_value))
    halves = [first, second]

    columns = (seq_count + 1) * head_count

    def local_part(rows, suffix, small, scratch, arrays):
        return pl.pallas_call(
            functools.partial(local_kernel, depth, suffix, chunks),
            out_shape=[pltpu.VMEM((rows, width), jnp.float32), pltpu.VMEM((rows, columns), jnp.float32)],
            in_specs=[hbm] * (len(small) + 3),
            out_specs=[vmem] * 2,
            scratch_shapes=scratch
            + [pltpu.VMEM((rows, width), jnp.bfloat16)] * 3
            + [pltpu.SemaphoreType.DMA((len(small),)), pltpu.SemaphoreType.DMA((3, chunks))],
            compiler_params=params,
            cost_estimate=cost(0, 0),
        )(*pinned(*small), *pinned(*arrays))

    outer = list(range(1, depth))
    places = [(bit, side) for bit in outer for side in range(2)]
    ahead = [(bit, 0) for bit in outer[:-1]] + [(bit, 1) for bit in outer[1:]] or places
    sides = {1 << bit: [None, None] for bit in outer}
    for bit, side in ahead:
        sides[1 << bit][side] = swap(halves[side], bit)
    slab_table = slab_levels.reshape(-1, token_count)
    slab_acc, slab_coef = local_part(
        token_count,
        0,
        [slab_table],
        [pltpu.VMEM(slab_table.shape, jnp.bfloat16)],
        [slab_query, slab_key, slab_value],
    )
    state, *halves = after(slab_coef, [state] + halves)
    whole = {0: state, 1: swap(state, 0)}
    for bit, side in places:
        if (bit, side) not in ahead:
            sides[1 << bit][side] = swap(halves[side], bit)

    later = sorted((m for m in range(0, seq_count, 2) if m.bit_count() > 1), key=lambda m: m.bit_count())
    for m in later:
        high, low = m.bit_length() - 1, (m & -m).bit_length() - 1
        sides[m] = [swap(sides[m ^ (1 << high)][0], high), swap(sides[m ^ (1 << low)][1], low)]
    user_queries = user_query.reshape(user_rows, width)
    user_table = user_levels.reshape(user_count, -1, suffix)
    lengths = after([whole[1]] + [sides[1 << bit][side] for bit, side in ahead], [prefix_lengths])[0]
    user_acc, user_coef = local_part(
        user_rows,
        suffix,
        [lengths, user_table],
        [pltpu.SMEM((user_count,), jnp.int32), pltpu.VMEM(user_table.shape, jnp.bfloat16)],
        [user_queries, user_key.reshape(user_rows, width), user_value.reshape(user_rows, width)],
    )

    def read(groups, states, accs, last):
        found = {}
        for which, (offsets, _) in enumerate(states):
            found.update({offset: (which, index) for index, offset in enumerate(offsets)})
        outs = [pltpu.VMEM((token_count, width), jnp.float32), pltpu.VMEM((user_rows, width), jnp.float32)]
        scratch = []
        if last:
            outs.append(pltpu.VMEM((lines, ROWS), jnp.float32))
            scratch = [pltpu.VMEM((token_count, HD), jnp.float32), pltpu.VMEM((user_rows, HD), jnp.float32)]
        return pl.pallas_call(
            functools.partial(read_kernel, groups, found, last),
            out_shape=outs,
            in_specs=[vmem] * (6 + len(states)),
            out_specs=[vmem] * len(outs),
            scratch_shapes=scratch,
            compiler_params=params,
            cost_estimate=cost(0, 0),
        )(slab_query, user_queries, slab_coef, user_coef, *accs, *[array for _, array in states])

    def pairs(offsets):
        return [tuple(offsets[i : i + 2]) for i in range(0, len(offsets), 2)]

    direct = [1 << bit for bit in outer]
    mates = [m | 1 for m in direct]
    for m in direct:
        whole[m] = join(user_coef, sides[m])
    for m in direct:
        whole[m | 1] = swap(whole[m], 0)
    accs = read(pairs([0, 1] + direct), [([m], whole[m]) for m in [0, 1] + direct], (slab_acc, user_acc), False)
    late = join(accs[0], [piece for m in later for piece in sides[m]])
    accs = read(pairs(mates), [([m], whole[m]) for m in mates], accs, False)
    late_mates = swap(late, 0)
    slab_total, user_total, square = read(
        [(m, m | 1) for m in later], [(later, late), ([m | 1 for m in later], late_mates)], accs, True
    )

    mate = jnp.zeros_like(square)
    for bit in range(head_axis.bit_length() - 1):
        square = square + mate
        mate = lax.ppermute(square, "head", [(i, i ^ (1 << bit)) for i in range(head_axis)])

    slab_out, user_out = pl.pallas_call(
        functools.partial(norm_kernel, float(width * head_axis), chunks),
        out_shape=[bf16((token_count, width)), bf16((user_rows, width))],
        in_specs=[vmem] * 5,
        out_specs=[hbm] * 2,
        scratch_shapes=[
            pltpu.VMEM((token_count, width), jnp.bfloat16),
            pltpu.VMEM((user_rows, width), jnp.bfloat16),
            pltpu.SemaphoreType.DMA((2, chunks)),
        ],
        compiler_params=params,
    )(slab_total, user_total, norm_gain.reshape(1, width), square, mate)
    return slab_out, user_out.reshape(user_count, suffix, width)


def solution(mesh):
    return jax.shard_map(
        local,
        mesh=mesh,
        in_specs=(
            P("seq", "head"),
            P("seq", "head"),
            P("seq", "head"),
            P(None, "head", "seq"),
            P("head"),
            P("seq", None, "head"),
            P("seq", None, "head"),
            P("seq", None, "head"),
            P("seq", None, "head", None),
            P("seq"),
        ),
        out_specs=(P("seq", "head"), P("seq", None, "head")),
        check_vma=False,
    )
```

```python
import functools

import jax
import jax.numpy as jnp
from jax import lax
from jax.experimental import pallas as pl
from jax.experimental.pallas import tpu as pltpu
from jax.sharding import PartitionSpec as P

HEADS = 64
HD = 128
ROWS = 128
VMEM_BYTES = 20 * 1024 * 1024


def matmul(a, b, contract):
    return lax.dot_general(a, b, (contract, ((), ())), preferred_element_type=jnp.float32)


def load_columns(sources, targets, sems, chunks):
    copies = []
    for chunk in range(chunks):
        group = []
        for i, (source, target) in enumerate(zip(sources, targets)):
            size = source.shape[1] // chunks
            cols = pl.ds(chunk * size, size)
            group.append(pltpu.make_async_copy(source.at[:, cols], target.at[:, cols], sems.at[i, chunk]))
            group[-1].start()
        copies.append(group)

    def wait(chunk):
        for copy in copies[chunk]:
            copy.wait()

    return wait


def state_kernel(chunks, key_hbm, value_hbm, first_ref, second_ref, whole_ref, key_ref, value_ref, sems):
    half = first_ref.shape[0]
    head_count = 2 * half
    wait = load_columns((key_hbm, value_hbm), (key_ref, value_ref), sems, chunks)
    for head in range(head_count):
        if head % (head_count // chunks) == 0:
            wait(head // (head_count // chunks))
        cols = slice(head * HD, (head + 1) * HD)
        state = matmul(key_ref[:, cols], value_ref[:, cols], ((0,), (0,))).astype(jnp.bfloat16)
        whole_ref[0, head] = state
        if head < half:
            first_ref[head] = state
        else:
            second_ref[head - half] = state


def join_kernel(order_ref, *refs):
    out_ref = refs[-1]
    half = out_ref.shape[1] // 2
    for i in range(out_ref.shape[0]):
        for side in range(2):
            for head in range(half):
                out_ref[i, side * half + head] = refs[2 * i + side][head]


def choose_levels(target, position, depth, level_count, head_count):
    block_count = 1 << depth
    shift = head_count.bit_length() - 1
    shape = (level_count * head_count, (block_count + 1) * head_count)
    row = lax.broadcasted_iota(jnp.int32, shape, 0)
    col = lax.broadcasted_iota(jnp.int32, shape, 1)
    level = row >> shift
    offset = col >> shift
    block = offset ^ position
    diff = block ^ target
    chosen = jnp.logical_and(level == 0, offset == block_count)
    below = jnp.logical_and(offset < block_count, block < target)
    for step in range(1, depth + 1):
        span = jnp.logical_and(diff >= (1 << (step - 1)), diff < (1 << step))
        chosen = jnp.logical_or(chosen, jnp.logical_and(below, jnp.logical_and(span, level == step)))
    same = (row & (head_count - 1)) == (col & (head_count - 1))
    return jnp.where(jnp.logical_and(chosen, same), 1.0, 0.0).astype(jnp.bfloat16)


def attend(mask, q_ref, k_ref, v_ref, c_ref, o_ref, own):
    head_count = q_ref.shape[1] // HD
    step = 2
    for first in range(0, head_count, step):
        units = [
            (head, slice(head * HD, (head + 1) * HD), slice(start, start + ROWS))
            for head in range(first, first + step)
            for start in range(0, q_ref.shape[0], ROWS)
        ]
        scores = [matmul(q_ref[rows, cols], k_ref[rows, cols], ((1,), (1,))) for _, cols, rows in units]
        scores = [jnp.where(mask, score, 0.0).astype(jnp.bfloat16) for score in scores]
        results = [matmul(score, v_ref[rows, cols], ((1,), (0,))) for score, (_, cols, rows) in zip(scores, units)]
        for result, (head, cols, rows) in zip(results, units):
            o_ref[rows, cols] = result * c_ref[rows, own + head : own + head + 1]


def causal_mask(suffix=ROWS):
    row = lax.broadcasted_iota(jnp.int32, (ROWS, ROWS), 0)
    col = lax.broadcasted_iota(jnp.int32, (ROWS, ROWS), 1)
    return jnp.logical_and(row >= col, row // suffix == col // suffix)


def slab_kernel(depth, suffix, *refs):
    sources, (k_ref, v_ref), (o_ref, sc_ref, uc_ref), rest = refs[:7], refs[7:9], refs[9:12], refs[12:]
    q_ref, user_loaded, small_loaded, sems = rest[0], rest[1:4], rest[4:7], rest[7]
    copies = [
        pltpu.make_async_copy(source, target, sems.at[i])
        for i, (source, target) in enumerate(zip(sources, (*small_loaded, q_ref, *user_loaded)))
    ]
    for copy in copies:
        copy.start()
    for copy in copies[:3]:
        copy.wait()
    length_ref, slab_table, user_table = small_loaded
    head_count = q_ref.shape[1] // HD
    pick = functools.partial(
        choose_levels,
        position=lax.axis_index("seq").astype(jnp.int32),
        depth=depth,
        level_count=slab_table.shape[0] // head_count,
        head_count=head_count,
    )
    sc_ref[...] = matmul(slab_table[...], pick(lax.axis_index("seq").astype(jnp.int32)), ((0,), (0,)))
    for user in range(user_table.shape[0]):
        weights = matmul(user_table[user], pick(length_ref[user]), ((0,), (0,)))
        uc_ref[user * suffix : (user + 1) * suffix] = weights
    copies[3].wait()
    attend(causal_mask(), q_ref, k_ref, v_ref, sc_ref, o_ref, (1 << depth) * head_count)
    for copy in copies[4:]:
        copy.wait()


def user_kernel(depth, suffix, c_ref, q_ref, k_ref, v_ref, o_ref):
    own = (1 << depth) * (q_ref.shape[1] // HD)
    attend(causal_mask(suffix), q_ref, k_ref, v_ref, c_ref, o_ref, own)


def add_blocks(groups, state_refs, head_count, head, q_ref, c_ref, base):
    cols = slice(head * HD, (head + 1) * HD)
    query = q_ref[:, cols]
    total = base
    for group in groups:
        scaled = []
        for offset in group:
            column = offset * head_count + head
            weight = jnp.broadcast_to(c_ref[:, column : column + 1], query.shape).astype(jnp.bfloat16)
            scaled.append(query * weight)
        states = [state_refs[offset][0][state_refs[offset][1], head] for offset in group]
        total = total + matmul(jnp.concatenate(scaled, axis=1), jnp.concatenate(states, axis=0), ((1,), (0,)))
    return total


def read_kernel(groups, places, last, sq_ref, uq_ref, sc_ref, uc_ref, sa_ref, ua_ref, *rest):
    head_count = sq_ref.shape[1] // HD
    used = 1 + max(which for which, _ in places.values())
    state_refs = {offset: (rest[which], index) for offset, (which, index) in places.items()}
    st_ref, ut_ref = rest[used : used + 2]
    for head in range(head_count):
        cols = slice(head * HD, (head + 1) * HD)
        for side, (q_ref, c_ref, a_ref, t_ref) in enumerate(
            ((sq_ref, sc_ref, sa_ref, st_ref), (uq_ref, uc_ref, ua_ref, ut_ref))
        ):
            total = add_blocks(groups, state_refs, head_count, head, q_ref, c_ref, a_ref[:, cols])
            t_ref[:, cols] = total
            if last:
                acc_ref = rest[used + 3 + side]
                if head == 0:
                    acc_ref[...] = total * total
                else:
                    acc_ref[...] += total * total
    if last:
        square_ref = rest[used + 2]
        line = 0
        for acc_ref in rest[used + 3 : used + 5]:
            for start in range(0, acc_ref.shape[0], ROWS):
                turned = jnp.transpose(acc_ref[start : start + ROWS])
                square_ref[line : line + 1] = jnp.sum(turned, axis=0, keepdims=True)
                line += 1


def norm_kernel(features, chunks, st_ref, ut_ref, gain_ref, one_ref, two_ref, so_hbm, uo_hbm, so_ref, uo_ref, sems):
    square = one_ref[...] + two_ref[...]
    scale = lax.rsqrt(square / features + 1e-06)
    scales = [jnp.transpose(jnp.broadcast_to(scale[line : line + 1], (ROWS, ROWS))) for line in range(scale.shape[0])]
    size = st_ref.shape[1] // chunks
    copies = []
    for chunk in range(chunks):
        line = 0
        wide = pl.ds(chunk * size, size)
        for side, (t_ref, o_ref, o_hbm) in enumerate(((st_ref, so_ref, so_hbm), (ut_ref, uo_ref, uo_hbm))):
            for start in range(0, t_ref.shape[0], ROWS):
                rows = slice(start, start + ROWS)
                for low in range(chunk * size, (chunk + 1) * size, HD):
                    cols = slice(low, low + HD)
                    gain = gain_ref[:, cols].astype(jnp.float32)
                    o_ref[rows, cols] = (t_ref[rows, cols] * scales[line] * gain).astype(jnp.bfloat16)
                line += 1
            copies.append(pltpu.make_async_copy(o_ref.at[:, wide], o_hbm.at[:, wide], sems.at[side, chunk]))
            copies[-1].start()
    for copy in copies:
        copy.wait()


def local(
    slab_query,
    slab_key,
    slab_value,
    slab_levels,
    norm_gain,
    user_query,
    user_key,
    user_value,
    user_levels,
    prefix_lengths,
):
    seq_count = lax.axis_size("seq")
    head_axis = lax.axis_size("head")
    depth = seq_count.bit_length() - 1
    token_count, width = slab_query.shape
    head_count = width // HD
    half = head_count // 2
    user_count, suffix = user_query.shape[:2]
    user_rows = user_count * suffix
    lines = (token_count + user_rows) // ROWS
    params = pltpu.CompilerParams(vmem_limit_bytes=VMEM_BYTES)
    bf16 = functools.partial(jax.ShapeDtypeStruct, dtype=jnp.bfloat16)
    vmem = pl.BlockSpec(memory_space=pltpu.VMEM)
    anywhere = pl.BlockSpec(memory_space=pl.ANY)
    hbm = pl.BlockSpec(memory_space=pltpu.HBM)
    chunks = min(4, half)
    rows_cost = 2 * width * (token_count + user_rows)

    def pinned(*arrays):
        return [pltpu.with_memory_space_constraint(array, pltpu.HBM) for array in arrays]

    def cost(flops, moved):
        return pl.CostEstimate(flops=flops, bytes_accessed=moved, transcendentals=0)

    def swap(value, bit):
        return lax.ppermute(value, "seq", [(i, i ^ (1 << bit)) for i in range(seq_count)])

    def after(results, values):
        return list(lax.optimization_barrier((results, values))[1])

    def join(order, halves):
        return pl.pallas_call(
            join_kernel,
            out_shape=pltpu.VMEM((len(halves) // 2, head_count, HD, HD), jnp.bfloat16),
            in_specs=[anywhere] + [vmem] * len(halves),
            out_specs=vmem,
            compiler_params=params,
        )(order, *halves)

    half_state = pltpu.VMEM((half, HD, HD), jnp.bfloat16)
    slab_rows = pltpu.VMEM((token_count, width), jnp.bfloat16)
    first, second, state, slab_keys, slab_values = pl.pallas_call(
        functools.partial(state_kernel, chunks),
        out_shape=[half_state, half_state, pltpu.VMEM((1, head_count, HD, HD), jnp.bfloat16), slab_rows, slab_rows],
        in_specs=[hbm] * 2,
        out_specs=[vmem] * 5,
        scratch_shapes=[pltpu.SemaphoreType.DMA((2, chunks))],
        compiler_params=params,
    )(*pinned(slab_key, slab_value))
    halves = [first, second]

    outer = list(range(1, depth))
    places = [(bit, side) for bit in outer for side in range(2)]
    ahead = [(bit, 0) for bit in outer[:-1]] + [(bit, 1) for bit in outer[1:]] or places
    sides = {1 << bit: [None, None] for bit in outer}
    for bit, side in ahead:
        sides[1 << bit][side] = swap(halves[side], bit)
    slab_table = slab_levels.reshape(-1, token_count)
    user_table = user_levels.reshape(user_count, -1, suffix)
    columns = (seq_count + 1) * head_count
    slab_acc, slab_coef, user_coef, slab_queries, user_queries, user_keys, user_values = pl.pallas_call(
        functools.partial(slab_kernel, depth, suffix),
        out_shape=[
            pltpu.VMEM((token_count, width), jnp.float32),
            pltpu.VMEM((token_count, columns), jnp.float32),
            pltpu.VMEM((user_rows, columns), jnp.float32),
            slab_rows,
        ]
        + [pltpu.VMEM((user_rows, width), jnp.bfloat16)] * 3,
        in_specs=[hbm] * 7 + [vmem] * 2,
        out_specs=[vmem] * 7,
        scratch_shapes=[
            pltpu.SMEM((user_count,), jnp.int32),
            pltpu.VMEM(slab_table.shape, jnp.bfloat16),
            pltpu.VMEM(user_table.shape, jnp.bfloat16),
            pltpu.SemaphoreType.DMA((7,)),
        ],
        compiler_params=params,
        cost_estimate=cost(0, 0),
    )(
        *pinned(prefix_lengths, slab_table, user_table, slab_query),
        *pinned(*[array.reshape(user_rows, width) for array in (user_query, user_key, user_value)]),
        slab_keys,
        slab_values,
    )
    halves = after(slab_coef, halves)
    whole = {0: state, 1: swap(state, 0)}
    for bit, side in places:
        if (bit, side) not in ahead:
            sides[1 << bit][side] = swap(halves[side], bit)

    later = sorted((m for m in range(0, seq_count, 2) if m.bit_count() > 1), key=lambda m: m.bit_count())
    for m in later:
        high, low = m.bit_length() - 1, (m & -m).bit_length() - 1
        sides[m] = [swap(sides[m ^ (1 << high)][0], high), swap(sides[m ^ (1 << low)][1], low)]
    user_coef = after([sides[1 << bit][side] for bit, side in ahead], [user_coef])[0]
    user_acc = pl.pallas_call(
        functools.partial(user_kernel, depth, suffix),
        out_shape=pltpu.VMEM((user_rows, width), jnp.float32),
        in_specs=[vmem] * 4,
        out_specs=vmem,
        compiler_params=params,
        cost_estimate=cost(0, 0),
    )(user_coef, user_queries, user_keys, user_values)

    def read(groups, states, accs, last):
        found = {}
        for which, (offsets, _) in enumerate(states):
            found.update({offset: (which, index) for index, offset in enumerate(offsets)})
        outs = [pltpu.VMEM((token_count, width), jnp.float32), pltpu.VMEM((user_rows, width), jnp.float32)]
        scratch = []
        if last:
            outs.append(pltpu.VMEM((lines, ROWS), jnp.float32))
            scratch = [pltpu.VMEM((token_count, HD), jnp.float32), pltpu.VMEM((user_rows, HD), jnp.float32)]
        return pl.pallas_call(
            functools.partial(read_kernel, groups, found, last),
            out_shape=outs,
            in_specs=[vmem] * (6 + len(states)),
            out_specs=[vmem] * len(outs),
            scratch_shapes=scratch,
            compiler_params=params,
            cost_estimate=cost(0, 0),
        )(slab_queries, user_queries, slab_coef, user_coef, *accs, *[array for _, array in states])

    def pairs(offsets):
        return [tuple(offsets[i : i + 2]) for i in range(0, len(offsets), 2)]

    direct = [1 << bit for bit in outer]
    mates = [m | 1 for m in direct]
    for m in direct:
        whole[m] = join(user_acc, sides[m])
    for m in direct:
        whole[m | 1] = swap(whole[m], 0)
    accs = read(pairs([0, 1] + direct), [([m], whole[m]) for m in [0, 1] + direct], (slab_acc, user_acc), False)
    late = join(accs[0], [piece for m in later for piece in sides[m]])
    accs = read(pairs(mates), [([m], whole[m]) for m in mates], accs, False)
    late_mates = swap(late, 0)
    slab_total, user_total, square = read(
        [(m, m | 1) for m in later], [(later, late), ([m | 1 for m in later], late_mates)], accs, True
    )

    mate = jnp.zeros_like(square)
    for bit in range(head_axis.bit_length() - 1):
        square = square + mate
        mate = lax.ppermute(square, "head", [(i, i ^ (1 << bit)) for i in range(head_axis)])

    slab_out, user_out = pl.pallas_call(
        functools.partial(norm_kernel, float(width * head_axis), chunks),
        out_shape=[bf16((token_count, width)), bf16((user_rows, width))],
        in_specs=[vmem] * 5,
        out_specs=[hbm] * 2,
        scratch_shapes=[
            pltpu.VMEM((token_count, width), jnp.bfloat16),
            pltpu.VMEM((user_rows, width), jnp.bfloat16),
            pltpu.SemaphoreType.DMA((2, chunks)),
        ],
        compiler_params=params,
    )(slab_total, user_total, norm_gain.reshape(1, width), square, mate)
    return slab_out, user_out.reshape(user_count, suffix, width)


def solution(mesh):
    return jax.shard_map(
        local,
        mesh=mesh,
        in_specs=(
            P("seq", "head"),
            P("seq", "head"),
            P("seq", "head"),
            P(None, "head", "seq"),
            P("head"),
            P("seq", None, "head"),
            P("seq", None, "head"),
            P("seq", None, "head"),
            P("seq", None, "head", None),
            P("seq"),
        ),
        out_specs=(P("seq", "head"), P("seq", None, "head")),
        check_vma=False,
    )
```

```python
import functools

import jax
import jax.numpy as jnp
from jax import lax
from jax.experimental import pallas as pl
from jax.experimental.pallas import tpu as pltpu
from jax.sharding import PartitionSpec as P

HEADS = 64
HD = 128
ROWS = 128
VMEM_BYTES = 20 * 1024 * 1024


def matmul(a, b, contract):
    return lax.dot_general(a, b, (contract, ((), ())), preferred_element_type=jnp.float32)


def load_columns(sources, targets, sems, chunks):
    copies = []
    for chunk in range(chunks):
        group = []
        for i, (source, target) in enumerate(zip(sources, targets)):
            size = source.shape[1] // chunks
            cols = pl.ds(chunk * size, size)
            group.append(pltpu.make_async_copy(source.at[:, cols], target.at[:, cols], sems.at[i, chunk]))
            group[-1].start()
        copies.append(group)

    def wait(chunk):
        for copy in copies[chunk]:
            copy.wait()

    return wait


def state_kernel(chunks, key_hbm, value_hbm, first_ref, second_ref, whole_ref, key_ref, value_ref, sems):
    half = first_ref.shape[0]
    head_count = 2 * half
    wait = load_columns((key_hbm, value_hbm), (key_ref, value_ref), sems, chunks)
    for head in range(head_count):
        if head % (head_count // chunks) == 0:
            wait(head // (head_count // chunks))
        cols = slice(head * HD, (head + 1) * HD)
        state = matmul(key_ref[:, cols], value_ref[:, cols], ((0,), (0,)))
        whole_ref[0, head] = state.astype(jnp.bfloat16)
    parity = lax.axis_index("seq") & 1
    for head in range(half):
        first_ref[head] = whole_ref[0, parity * half + head]
        second_ref[head] = whole_ref[0, (1 - parity) * half + head]


def join_kernel(order_ref, *refs):
    out_ref = refs[-1]
    parity = lax.axis_index("seq") & 1
    half = out_ref.shape[1] // 2
    for i in range(out_ref.shape[0]):
        for side in range(2):
            for head in range(half):
                out_ref[i, (side ^ parity) * half + head] = refs[2 * i + side][head]


def turned(offset, depth):
    result = jnp.zeros_like(offset)
    for bit in range(1, depth):
        result = result | (((offset >> bit) & 1) << (depth - bit))
    return result


def choose_levels(target, position, depth, level_count, head_count):
    block_count = 1 << depth
    shift = head_count.bit_length() - 1
    shape = (level_count * head_count, (block_count + 1) * head_count)
    row = lax.broadcasted_iota(jnp.int32, shape, 0)
    col = lax.broadcasted_iota(jnp.int32, shape, 1)
    level = row >> shift
    offset = col >> shift
    low = offset & 1
    block = position ^ low ^ jnp.where((low ^ position) & 1 == 1, turned(offset, depth), offset - low)
    diff = block ^ target
    chosen = jnp.logical_and(level == 0, offset == block_count)
    below = jnp.logical_and(offset < block_count, block < target)
    for step in range(1, depth + 1):
        span = jnp.logical_and(diff >= (1 << (step - 1)), diff < (1 << step))
        chosen = jnp.logical_or(chosen, jnp.logical_and(below, jnp.logical_and(span, level == step)))
    same = (row & (head_count - 1)) == (col & (head_count - 1))
    return jnp.where(jnp.logical_and(chosen, same), 1.0, 0.0).astype(jnp.bfloat16)


def attend(mask, q_ref, k_ref, v_ref, c_ref, o_ref, own):
    head_count = q_ref.shape[1] // HD
    step = 2
    for first in range(0, head_count, step):
        units = [
            (head, slice(head * HD, (head + 1) * HD), slice(start, start + ROWS))
            for head in range(first, first + step)
            for start in range(0, q_ref.shape[0], ROWS)
        ]
        scores = [matmul(q_ref[rows, cols], k_ref[rows, cols], ((1,), (1,))) for _, cols, rows in units]
        scores = [jnp.where(mask, score, 0.0).astype(jnp.bfloat16) for score in scores]
        results = [matmul(score, v_ref[rows, cols], ((1,), (0,))) for score, (_, cols, rows) in zip(scores, units)]
        for result, (head, cols, rows) in zip(results, units):
            weight = jnp.broadcast_to(c_ref[rows, own + head : own + head + 1], (ROWS, HD))
            o_ref[rows, cols] = result * weight.astype(jnp.float32)


def causal_mask(suffix=ROWS):
    row = lax.broadcasted_iota(jnp.int32, (ROWS, ROWS), 0)
    col = lax.broadcasted_iota(jnp.int32, (ROWS, ROWS), 1)
    return jnp.logical_and(row >= col, row // suffix == col // suffix)


def load_kernel(depth, suffix, *refs):
    sources, (sc_ref, uc_ref), loaded, small_loaded, sems = refs[:7], refs[7:9], refs[9:13], refs[13:16], refs[16]
    copies = [
        pltpu.make_async_copy(source, target, sems.at[i])
        for i, (source, target) in enumerate(zip(sources, (*small_loaded, *loaded)))
    ]
    for copy in copies:
        copy.start()
    for copy in copies[:3]:
        copy.wait()
    length_ref, slab_table, user_table = small_loaded
    head_count = loaded[0].shape[1] // HD
    position = lax.axis_index("seq").astype(jnp.int32)
    pick = functools.partial(
        choose_levels,
        position=position,
        depth=depth,
        level_count=slab_table.shape[0] // head_count,
        head_count=head_count,
    )
    sc_ref[...] = matmul(slab_table[...], pick(position), ((0,), (0,))).astype(jnp.bfloat16)
    for user in range(user_table.shape[0]):
        weights = matmul(user_table[user], pick(length_ref[user]), ((0,), (0,)))
        uc_ref[user * suffix : (user + 1) * suffix] = weights.astype(jnp.bfloat16)
    for copy in copies[3:]:
        copy.wait()


def slab_kernel(depth, c_ref, q_ref, k_ref, v_ref, o_ref):
    attend(causal_mask(), q_ref, k_ref, v_ref, c_ref, o_ref, (1 << depth) * (q_ref.shape[1] // HD))


def spread(c_ref, column, width):
    return jnp.broadcast_to(c_ref[:, column : column + 1], (c_ref.shape[0], width))


def user_kernel(depth, suffix, group, c_ref, q_ref, k_ref, v_ref, sc_ref, sq_ref, o_ref, *scaled_refs):
    head_count = q_ref.shape[1] // HD
    attend(causal_mask(suffix), q_ref, k_ref, v_ref, c_ref, o_ref, (1 << depth) * head_count)
    for scaled_ref, query_ref, weight_ref in zip(scaled_refs, (sq_ref, q_ref), (sc_ref, c_ref)):
        for head in range(head_count):
            query = query_ref[:, head * HD : (head + 1) * HD]
            for i, offset in enumerate(group):
                start = (head * len(group) + i) * HD
                weight = spread(weight_ref, offset * head_count + head, HD)
                scaled_ref[:, start : start + HD] = query * weight


def read_kernel(groups, places, sq_ref, uq_ref, sc_ref, uc_ref, sa_ref, ua_ref, *rest):
    head_count = sq_ref.shape[1] // HD
    st_ref, ut_ref = rest[-2:]
    for head in range(head_count):
        cols = slice(head * HD, (head + 1) * HD)
        for q_ref, c_ref, a_ref, t_ref in ((sq_ref, sc_ref, sa_ref, st_ref), (uq_ref, uc_ref, ua_ref, ut_ref)):
            query = q_ref[:, cols]
            total = a_ref[:, cols]
            for group in groups:
                scaled = [query * spread(c_ref, offset * head_count + head, HD) for offset in group]
                states = [rest[places[offset][0]][places[offset][1], head] for offset in group]
                total = total + matmul(
                    jnp.concatenate(scaled, axis=1), jnp.concatenate(states, axis=0), ((1,), (0,))
                )
            t_ref[:, cols] = total


def last_kernel(ss_ref, us_ref, sa_ref, ua_ref, state_ref, mate_ref, st_ref, ut_ref, square_ref, s_square, u_square):
    head_count = sa_ref.shape[1] // HD
    for head in range(head_count):
        cols = slice(head * HD, (head + 1) * HD)
        wide = slice(2 * head * HD, 2 * (head + 1) * HD)
        states = jnp.concatenate([state_ref[0, head], mate_ref[0, head]], axis=0)
        for q_ref, a_ref, t_ref, acc_ref in ((ss_ref, sa_ref, st_ref, s_square), (us_ref, ua_ref, ut_ref, u_square)):
            total = a_ref[:, cols] + matmul(q_ref[:, wide], states, ((1,), (0,)))
            t_ref[:, cols] = total
            if head == 0:
                acc_ref[...] = total * total
            else:
                acc_ref[...] += total * total
    line = 0
    for acc_ref in (s_square, u_square):
        for start in range(0, acc_ref.shape[0], ROWS):
            turned_part = jnp.transpose(acc_ref[start : start + ROWS])
            square_ref[line : line + 1] = jnp.sum(turned_part, axis=0, keepdims=True)
            line += 1


def norm_kernel(features, chunks, st_ref, ut_ref, gain_ref, one_ref, two_ref, so_hbm, uo_hbm, so_ref, uo_ref, sems):
    square = one_ref[...] + two_ref[...]
    scale = lax.rsqrt(square / features + 1e-06)
    scales = [jnp.transpose(jnp.broadcast_to(scale[line : line + 1], (ROWS, ROWS))) for line in range(scale.shape[0])]
    size = st_ref.shape[1] // chunks
    copies = []
    for chunk in range(chunks):
        line = 0
        wide = pl.ds(chunk * size, size)
        for side, (t_ref, o_ref, o_hbm) in enumerate(((st_ref, so_ref, so_hbm), (ut_ref, uo_ref, uo_hbm))):
            for start in range(0, t_ref.shape[0], ROWS):
                rows = slice(start, start + ROWS)
                for low in range(chunk * size, (chunk + 1) * size, HD):
                    cols = slice(low, low + HD)
                    gain = gain_ref[:, cols].astype(jnp.float32)
                    o_ref[rows, cols] = (t_ref[rows, cols] * scales[line] * gain).astype(jnp.bfloat16)
                line += 1
            copies.append(pltpu.make_async_copy(o_ref.at[:, wide], o_hbm.at[:, wide], sems.at[side, chunk]))
            copies[-1].start()
    for copy in copies:
        copy.wait()


def local(
    slab_query,
    slab_key,
    slab_value,
    slab_levels,
    norm_gain,
    user_query,
    user_key,
    user_value,
    user_levels,
    prefix_lengths,
):
    seq_count = lax.axis_size("seq")
    head_axis = lax.axis_size("head")
    depth = seq_count.bit_length() - 1
    token_count, width = slab_query.shape
    head_count = width // HD
    half = head_count // 2
    user_count, suffix = user_query.shape[:2]
    user_rows = user_count * suffix
    lines = (token_count + user_rows) // ROWS
    params = pltpu.CompilerParams(vmem_limit_bytes=VMEM_BYTES)
    bf16 = functools.partial(jax.ShapeDtypeStruct, dtype=jnp.bfloat16)
    vmem = pl.BlockSpec(memory_space=pltpu.VMEM)
    anywhere = pl.BlockSpec(memory_space=pl.ANY)
    hbm = pl.BlockSpec(memory_space=pltpu.HBM)
    chunks = min(4, half)
    rows_cost = 2 * width * (token_count + user_rows)

    def pinned(*arrays):
        return [pltpu.with_memory_space_constraint(array, pltpu.HBM) for array in arrays]

    def cost(flops, moved):
        return pl.CostEstimate(flops=flops, bytes_accessed=moved, transcendentals=0)

    def swap(value, bit):
        other = depth - bit if bit else 0
        return lax.ppermute(value, "seq", [(i, i ^ (1 << (other if i & 1 else bit))) for i in range(seq_count)])

    def after(results, values):
        return list(lax.optimization_barrier((results, values))[1])

    def join(order, halves):
        return pl.pallas_call(
            join_kernel,
            out_shape=pltpu.VMEM((len(halves) // 2, head_count, HD, HD), jnp.bfloat16),
            in_specs=[anywhere] + [vmem] * len(halves),
            out_specs=vmem,
            compiler_params=params,
        )(order, *halves)

    half_state = pltpu.VMEM((half, HD, HD), jnp.bfloat16)
    slab_rows = pltpu.VMEM((token_count, width), jnp.bfloat16)
    first, second, state, slab_keys, slab_values = pl.pallas_call(
        functools.partial(state_kernel, chunks),
        out_shape=[half_state, half_state, pltpu.VMEM((1, head_count, HD, HD), jnp.bfloat16), slab_rows, slab_rows],
        in_specs=[hbm] * 2,
        out_specs=[vmem] * 5,
        scratch_shapes=[pltpu.SemaphoreType.DMA((2, chunks))],
        compiler_params=params,
    )(*pinned(slab_key, slab_value))
    halves = [first, second]

    outer = list(range(1, depth))
    places = [(bit, side) for bit in outer for side in range(2)]
    ahead = [(bit, 0) for bit in outer[:-1]] + [(bit, 1) for bit in outer[1:]] or places
    sides = {1 << bit: [None, None] for bit in outer}
    for bit, side in ahead:
        sides[1 << bit][side] = swap(halves[side], bit)
    slab_table = slab_levels.reshape(-1, token_count)
    user_table = user_levels.reshape(user_count, -1, suffix)
    columns = (seq_count + 1) * head_count
    slab_coef, user_coef, slab_queries, user_queries, user_keys, user_values = pl.pallas_call(
        functools.partial(load_kernel, depth, suffix),
        out_shape=[
            pltpu.VMEM((token_count, columns), jnp.bfloat16),
            pltpu.VMEM((user_rows, columns), jnp.bfloat16),
            slab_rows,
        ]
        + [pltpu.VMEM((user_rows, width), jnp.bfloat16)] * 3,
        in_specs=[hbm] * 7,
        out_specs=[vmem] * 6,
        scratch_shapes=[
            pltpu.SMEM((user_count,), jnp.int32),
            pltpu.VMEM(slab_table.shape, jnp.bfloat16),
            pltpu.VMEM(user_table.shape, jnp.bfloat16),
            pltpu.SemaphoreType.DMA((7,)),
        ],
        compiler_params=params,
        cost_estimate=cost(0, 0),
    )(
        *pinned(prefix_lengths, slab_table, user_table, slab_query),
        *pinned(*[array.reshape(user_rows, width) for array in (user_query, user_key, user_value)]),
    )
    halves = after(slab_coef, halves)
    for bit, side in places:
        if (bit, side) not in ahead:
            sides[1 << bit][side] = swap(halves[side], bit)
    slab_acc = pl.pallas_call(
        functools.partial(slab_kernel, depth),
        out_shape=pltpu.VMEM((token_count, width), jnp.float32),
        in_specs=[vmem] * 4,
        out_specs=vmem,
        compiler_params=params,
        cost_estimate=cost(0, 0),
    )(slab_coef, slab_queries, slab_keys, slab_values)

    later = sorted((m for m in range(0, seq_count, 2) if m.bit_count() > 1), key=lambda m: m.bit_count())
    for (bit, side), value in zip(ahead, after(slab_acc, [sides[1 << bit][side] for bit, side in ahead])):
        sides[1 << bit][side] = value
    for m in later:
        high, low = m.bit_length() - 1, (m & -m).bit_length() - 1
        sides[m] = [swap(sides[m ^ (1 << high)][0], high), swap(sides[m ^ (1 << low)][1], low)]
    user_coef = after([sides[1 << bit][side] for bit, side in ahead], [user_coef])[0]
    last = later[-1]
    user_acc, slab_scaled, user_scaled = pl.pallas_call(
        functools.partial(user_kernel, depth, suffix, (last, last | 1)),
        out_shape=[
            pltpu.VMEM((user_rows, width), jnp.float32),
            pltpu.VMEM((token_count, 2 * width), jnp.bfloat16),
            pltpu.VMEM((user_rows, 2 * width), jnp.bfloat16),
        ],
        in_specs=[vmem] * 6,
        out_specs=[vmem] * 3,
        compiler_params=params,
        cost_estimate=cost(0, 0),
    )(user_coef, user_queries, user_keys, user_values, slab_coef, slab_queries)

    totals = [pltpu.VMEM((token_count, width), jnp.float32), pltpu.VMEM((user_rows, width), jnp.float32)]

    def read(offsets, accs):
        found = {offset: (which, 0) for which, offset in enumerate(offsets)}
        groups = [tuple(offsets[i : i + 2]) for i in range(0, len(offsets), 2)]
        return pl.pallas_call(
            functools.partial(read_kernel, groups, found),
            out_shape=totals,
            in_specs=[vmem] * (6 + len(offsets)),
            out_specs=[vmem] * 2,
            compiler_params=params,
            cost_estimate=cost(0, 0),
        )(slab_queries, user_queries, slab_coef, user_coef, *accs, *[whole[m] for m in offsets])

    whole = {0: after(user_acc, [state])[0]}
    direct = [1 << bit for bit in outer]
    for m in direct:
        whole[m] = join(user_acc, sides[m])
    for m in [0] + direct:
        whole[m | 1] = swap(whole[m], 0)
    accs = read([0] + direct, (slab_acc, user_acc))
    for m in later:
        whole[m] = join(accs[0], sides[m])
        whole[m | 1] = swap(whole[m], 0)
    accs = read([m | 1 for m in [0] + direct], accs)
    if later[:-1]:
        accs = read([n for m in later[:-1] for n in (m, m | 1)], accs)
    slab_total, user_total, square = pl.pallas_call(
        last_kernel,
        out_shape=totals + [pltpu.VMEM((lines, ROWS), jnp.float32)],
        in_specs=[vmem] * 6,
        out_specs=[vmem] * 3,
        scratch_shapes=[pltpu.VMEM((token_count, HD), jnp.float32), pltpu.VMEM((user_rows, HD), jnp.float32)],
        compiler_params=params,
        cost_estimate=cost(0, 0),
    )(slab_scaled, user_scaled, *accs, whole[last], whole[last | 1])

    mate = jnp.zeros_like(square)
    for bit in range(head_axis.bit_length() - 1):
        square = square + mate
        mate = lax.ppermute(square, "head", [(i, i ^ (1 << bit)) for i in range(head_axis)])

    slab_out, user_out = pl.pallas_call(
        functools.partial(norm_kernel, float(width * head_axis), chunks),
        out_shape=[bf16((token_count, width)), bf16((user_rows, width))],
        in_specs=[vmem] * 5,
        out_specs=[hbm] * 2,
        scratch_shapes=[
            pltpu.VMEM((token_count, width), jnp.bfloat16),
            pltpu.VMEM((user_rows, width), jnp.bfloat16),
            pltpu.SemaphoreType.DMA((2, chunks)),
        ],
        compiler_params=params,
    )(slab_total, user_total, norm_gain.reshape(1, width), square, mate)
    return slab_out, user_out.reshape(user_count, suffix, width)


def solution(mesh):
    return jax.shard_map(
        local,
        mesh=mesh,
        in_specs=(
            P("seq", "head"),
            P("seq", "head"),
            P("seq", "head"),
            P(None, "head", "seq"),
            P("head"),
            P("seq", None, "head"),
            P("seq", None, "head"),
            P("seq", None, "head"),
            P("seq", None, "head", None),
            P("seq"),
        ),
        out_specs=(P("seq", "head"), P("seq", None, "head")),
        check_vma=False,
    )
```

```python
import functools

import jax
import jax.numpy as jnp
from jax import lax
from jax.experimental import pallas as pl
from jax.experimental.pallas import tpu as pltpu
from jax.sharding import PartitionSpec as P

HEADS = 64
HD = 128
ROWS = 128
VMEM_BYTES = 20 * 1024 * 1024


def matmul(a, b, contract):
    return lax.dot_general(a, b, (contract, ((), ())), preferred_element_type=jnp.float32)


def load_columns(sources, targets, sems, chunks):
    copies = []
    for chunk in range(chunks):
        group = []
        for i, (source, target) in enumerate(zip(sources, targets)):
            size = source.shape[1] // chunks
            cols = pl.ds(chunk * size, size)
            group.append(pltpu.make_async_copy(source.at[:, cols], target.at[:, cols], sems.at[i, chunk]))
            group[-1].start()
        copies.append(group)

    def wait(chunk):
        for copy in copies[chunk]:
            copy.wait()

    return wait


def state_kernel(chunks, key_hbm, value_hbm, first_ref, second_ref, whole_ref, key_ref, value_ref, sems):
    half = first_ref.shape[0]
    head_count = 2 * half
    wait = load_columns((key_hbm, value_hbm), (key_ref, value_ref), sems, chunks)
    for head in range(head_count):
        if head % (head_count // chunks) == 0:
            wait(head // (head_count // chunks))
        cols = slice(head * HD, (head + 1) * HD)
        state = matmul(key_ref[:, cols], value_ref[:, cols], ((0,), (0,)))
        whole_ref[0, head] = state.astype(jnp.bfloat16)
    parity = lax.axis_index("seq") & 1
    for head in range(half):
        first_ref[head] = whole_ref[0, parity * half + head]
        second_ref[head] = whole_ref[0, (1 - parity) * half + head]


def join_kernel(order_ref, *refs):
    out_ref = refs[-1]
    parity = lax.axis_index("seq") & 1
    half = out_ref.shape[1] // 2
    for i in range(out_ref.shape[0]):
        for side in range(2):
            for head in range(half):
                out_ref[i, (side ^ parity) * half + head] = refs[2 * i + side][head]


def turned(offset, depth):
    return sum(((offset >> bit) & 1) << (depth - bit) for bit in range(1, depth))


def level_of(offset, target, position, depth):
    low = offset & 1
    block = position ^ low ^ jnp.where(((position ^ low) & 1) == 1, turned(offset, depth), offset - low)
    diff = block ^ target
    level = sum((diff >= (1 << step)).astype(jnp.int32) for step in range(depth))
    return jnp.where(block < target, level, 0)


def attend(mask, q_ref, k_ref, v_ref, w_ref, o_ref):
    head_count = q_ref.shape[1] // HD
    step = 2
    for first in range(0, head_count, step):
        units = [
            (head, slice(head * HD, (head + 1) * HD), slice(start, start + ROWS))
            for head in range(first, first + step)
            for start in range(0, q_ref.shape[0], ROWS)
        ]
        scores = [matmul(q_ref[rows, cols], k_ref[rows, cols], ((1,), (1,))) for _, cols, rows in units]
        scores = [jnp.where(mask, score, 0.0).astype(jnp.bfloat16) for score in scores]
        results = [matmul(score, v_ref[rows, cols], ((1,), (0,))) for score, (_, cols, rows) in zip(scores, units)]
        for result, (head, cols, rows) in zip(results, units):
            o_ref[rows, cols] = result * w_ref[rows, head : head + 1]


def causal_mask(suffix=ROWS):
    row = lax.broadcasted_iota(jnp.int32, (ROWS, ROWS), 0)
    col = lax.broadcasted_iota(jnp.int32, (ROWS, ROWS), 1)
    return jnp.logical_and(row >= col, row // suffix == col // suffix)


def start_copies(sources, targets, sems):
    copies = [
        pltpu.make_async_copy(source, target, sems.at[i]) for i, (source, target) in enumerate(zip(sources, targets))
    ]
    for copy in copies:
        copy.start()
    return copies


def load_kernel(suffix, *refs):
    sources, (sw_ref, uw_ref), loaded, tables, sems = refs[:4], refs[4:6], refs[6:8], refs[8:10], refs[10]
    copies = start_copies(sources, (*tables, *loaded), sems)
    slab_table, user_table = tables
    for copy in copies[:2]:
        copy.wait()
    columns = sw_ref.shape[1]
    row = lax.broadcasted_iota(jnp.int32, (slab_table.shape[0], columns), 0)
    col = lax.broadcasted_iota(jnp.int32, (slab_table.shape[0], columns), 1)
    same = jnp.where(row == col, 1.0, 0.0).astype(jnp.bfloat16)
    sw_ref[...] = matmul(slab_table[...], same, ((0,), (0,)))
    for user in range(user_table.shape[0]):
        uw_ref[user * suffix : (user + 1) * suffix] = matmul(user_table[user], same, ((0,), (0,)))
    for copy in copies[2:]:
        copy.wait()


def scale_queries(q_ref, w_ref, scaled_ref):
    head_count = q_ref.shape[1] // HD
    scaled_ref[0] = jnp.zeros_like(scaled_ref[0])
    for head in range(head_count):
        cols = slice(head * HD, (head + 1) * HD)
        query = q_ref[:, cols]
        for level in range(1, scaled_ref.shape[0]):
            column = level * head_count + head
            weight = jnp.broadcast_to(w_ref[:, column : column + 1], query.shape).astype(jnp.bfloat16)
            scaled_ref[level, :, cols] = query * weight


def slab_kernel(*refs):
    sources, (w_ref, q_ref, k_ref, v_ref), (o_ref, scaled_ref), loaded, sems = (
        refs[:3],
        refs[3:7],
        refs[7:9],
        refs[9:12],
        refs[12],
    )
    copies = start_copies(sources, loaded, sems)
    attend(causal_mask(), q_ref, k_ref, v_ref, w_ref, o_ref)
    scale_queries(q_ref, w_ref, scaled_ref)
    for copy in copies:
        copy.wait()


def user_kernel(suffix, w_ref, q_ref, k_ref, v_ref, o_ref, scaled_ref):
    attend(causal_mask(suffix), q_ref, k_ref, v_ref, w_ref, o_ref)
    scale_queries(q_ref, w_ref, scaled_ref)


def read_kernel(depth, suffix, groups, ahead, length_ref, ss_ref, us_ref, sa_ref, ua_ref, *rest):
    offsets = [offset for group in groups for offset in group]
    states, outs, (lengths, sem) = rest[: len(offsets)], rest[len(offsets) : -2], rest[-2:]
    copy = pltpu.make_async_copy(length_ref, lengths, sem)
    copy.start()
    copy.wait()
    position = lax.axis_index("seq").astype(jnp.int32)
    head_count = sa_ref.shape[1] // HD
    users = range(ua_ref.shape[0] // suffix)
    targets = [lengths[user] for user in users]
    slab_level = {o: level_of(o, position, position, depth) for o in (*offsets, *ahead)}
    user_level = {o: [level_of(o, target, position, depth) for target in targets] for o in (*offsets, *ahead)}

    def slab_rows(offset, cols):
        return ss_ref[slab_level[offset], :, cols]

    def user_rows(offset, cols):
        parts = [us_ref[user_level[offset][user], user * suffix : (user + 1) * suffix, cols] for user in users]
        return jnp.concatenate(parts, axis=0)

    for head in range(head_count):
        cols = slice(head * HD, (head + 1) * HD)
        for pick, a_ref, t_ref in ((slab_rows, sa_ref, outs[0]), (user_rows, ua_ref, outs[1])):
            total = a_ref[:, cols]
            for group in groups:
                queries = jnp.concatenate([pick(offset, cols) for offset in group], axis=1)
                blocks = jnp.concatenate([states[offsets.index(offset)][0, head] for offset in group], axis=0)
                total = total + matmul(queries, blocks, ((1,), (0,)))
            t_ref[:, cols] = total
        for pick, out_ref in zip((slab_rows, user_rows), outs[2:]):
            for i, offset in enumerate(ahead):
                start = (head * len(ahead) + i) * HD
                out_ref[:, start : start + HD] = pick(offset, cols)


def last_kernel(ss_ref, us_ref, sa_ref, ua_ref, state_ref, mate_ref, st_ref, ut_ref, square_ref):
    head_count = sa_ref.shape[1] // HD
    line = 0
    for q_ref, a_ref, t_ref in ((ss_ref, sa_ref, st_ref), (us_ref, ua_ref, ut_ref)):
        for start in range(0, a_ref.shape[0], ROWS):
            rows = slice(start, start + ROWS)
            squares = None
            for head in range(head_count):
                cols = slice(head * HD, (head + 1) * HD)
                wide = slice(2 * head * HD, 2 * (head + 1) * HD)
                states = jnp.concatenate([state_ref[0, head], mate_ref[0, head]], axis=0)
                total = a_ref[rows, cols] + matmul(q_ref[rows, wide], states, ((1,), (0,)))
                t_ref[rows, cols] = total
                squares = total * total if squares is None else squares + total * total
            square_ref[line : line + 1] = jnp.sum(jnp.transpose(squares), axis=0, keepdims=True)
            line += 1


def norm_kernel(features, chunks, st_ref, ut_ref, gain_ref, one_ref, two_ref, so_hbm, uo_hbm, so_ref, uo_ref, sems):
    square = one_ref[...] + two_ref[...]
    scale = lax.rsqrt(square / features + 1e-06)
    scales = [jnp.transpose(jnp.broadcast_to(scale[line : line + 1], (ROWS, ROWS))) for line in range(scale.shape[0])]
    size = st_ref.shape[1] // chunks
    copies = []
    for chunk in range(chunks):
        line = 0
        wide = pl.ds(chunk * size, size)
        for side, (t_ref, o_ref, o_hbm) in enumerate(((st_ref, so_ref, so_hbm), (ut_ref, uo_ref, uo_hbm))):
            for start in range(0, t_ref.shape[0], ROWS):
                rows = slice(start, start + ROWS)
                for low in range(chunk * size, (chunk + 1) * size, HD):
                    cols = slice(low, low + HD)
                    gain = gain_ref[:, cols].astype(jnp.float32)
                    o_ref[rows, cols] = (t_ref[rows, cols] * scales[line] * gain).astype(jnp.bfloat16)
                line += 1
            copies.append(pltpu.make_async_copy(o_ref.at[:, wide], o_hbm.at[:, wide], sems.at[side, chunk]))
            copies[-1].start()
    for copy in copies:
        copy.wait()


def local(
    slab_query,
    slab_key,
    slab_value,
    slab_levels,
    norm_gain,
    user_query,
    user_key,
    user_value,
    user_levels,
    prefix_lengths,
):
    seq_count = lax.axis_size("seq")
    head_axis = lax.axis_size("head")
    depth = seq_count.bit_length() - 1
    token_count, width = slab_query.shape
    head_count = width // HD
    half = head_count // 2
    user_count, suffix = user_query.shape[:2]
    user_rows = user_count * suffix
    lines = (token_count + user_rows) // ROWS
    params = pltpu.CompilerParams(vmem_limit_bytes=VMEM_BYTES)
    bf16 = functools.partial(jax.ShapeDtypeStruct, dtype=jnp.bfloat16)
    vmem = pl.BlockSpec(memory_space=pltpu.VMEM)
    anywhere = pl.BlockSpec(memory_space=pl.ANY)
    hbm = pl.BlockSpec(memory_space=pltpu.HBM)
    chunks = min(4, half)
    rows_cost = 2 * width * (token_count + user_rows)

    def pinned(*arrays):
        return [pltpu.with_memory_space_constraint(array, pltpu.HBM) for array in arrays]

    def cost(flops, moved):
        return pl.CostEstimate(flops=flops, bytes_accessed=moved, transcendentals=0)

    def swap(value, bit):
        other = depth - bit if bit else 0
        return lax.ppermute(value, "seq", [(i, i ^ (1 << (other if i & 1 else bit))) for i in range(seq_count)])

    def after(results, values):
        return list(lax.optimization_barrier((results, values))[1])

    def join(order, halves):
        return pl.pallas_call(
            join_kernel,
            out_shape=pltpu.VMEM((len(halves) // 2, head_count, HD, HD), jnp.bfloat16),
            in_specs=[anywhere] + [vmem] * len(halves),
            out_specs=vmem,
            compiler_params=params,
        )(order, *halves)

    half_state = pltpu.VMEM((half, HD, HD), jnp.bfloat16)
    slab_rows = pltpu.VMEM((token_count, width), jnp.bfloat16)
    first, second, state, slab_keys, slab_values = pl.pallas_call(
        functools.partial(state_kernel, chunks),
        out_shape=[half_state, half_state, pltpu.VMEM((1, head_count, HD, HD), jnp.bfloat16), slab_rows, slab_rows],
        in_specs=[hbm] * 2,
        out_specs=[vmem] * 5,
        scratch_shapes=[pltpu.SemaphoreType.DMA((2, chunks))],
        compiler_params=params,
    )(*pinned(slab_key, slab_value))
    halves = [first, second]

    outer = list(range(1, depth))
    places = [(bit, side) for bit in outer for side in range(2)]
    ahead = [(bit, 0) for bit in outer[:-1]] + [(bit, 1) for bit in outer[1:]] or places
    sides = {1 << bit: [None, None] for bit in outer}
    for bit, side in ahead:
        sides[1 << bit][side] = swap(halves[side], bit)
    levels = depth + 1
    slab_table = slab_levels.reshape(-1, token_count)
    user_table = user_levels.reshape(user_count, -1, suffix)
    user_array = pltpu.VMEM((user_rows, width), jnp.bfloat16)
    slab_weights, user_weights, slab_queries, lengths = pl.pallas_call(
        functools.partial(load_kernel, suffix),
        out_shape=[
            pltpu.VMEM((token_count, levels * head_count), jnp.float32),
            pltpu.VMEM((user_rows, levels * head_count), jnp.float32),
            slab_rows,
            pltpu.VMEM((user_count,), jnp.int32),
        ],
        in_specs=[hbm] * 4,
        out_specs=[vmem] * 4,
        scratch_shapes=[
            pltpu.VMEM(slab_table.shape, jnp.bfloat16),
            pltpu.VMEM(user_table.shape, jnp.bfloat16),
            pltpu.SemaphoreType.DMA((4,)),
        ],
        compiler_params=params,
        cost_estimate=cost(0, 0),
    )(*pinned(slab_table, user_table, slab_query, prefix_lengths))
    halves = after(slab_weights, halves)
    for bit, side in places:
        if (bit, side) not in ahead:
            sides[1 << bit][side] = swap(halves[side], bit)
    slab_acc, slab_scaled, user_queries, user_keys, user_values = pl.pallas_call(
        slab_kernel,
        out_shape=[
            pltpu.VMEM((token_count, width), jnp.float32),
            pltpu.VMEM((levels, token_count, width), jnp.bfloat16),
        ]
        + [user_array] * 3,
        in_specs=[hbm] * 3 + [vmem] * 4,
        out_specs=[vmem] * 5,
        scratch_shapes=[pltpu.SemaphoreType.DMA((3,))],
        compiler_params=params,
        cost_estimate=cost(0, 0),
    )(
        *pinned(*[array.reshape(user_rows, width) for array in (user_query, user_key, user_value)]),
        slab_weights,
        slab_queries,
        slab_keys,
        slab_values,
    )

    later = sorted((m for m in range(0, seq_count, 2) if m.bit_count() > 1), key=lambda m: m.bit_count())
    for (bit, side), value in zip(ahead, after(slab_acc, [sides[1 << bit][side] for bit, side in ahead])):
        sides[1 << bit][side] = value
    for m in later:
        high, low = m.bit_length() - 1, (m & -m).bit_length() - 1
        sides[m] = [swap(sides[m ^ (1 << high)][0], high), swap(sides[m ^ (1 << low)][1], low)]
    user_weights = after([sides[1 << bit][side] for bit, side in ahead], [user_weights])[0]
    user_acc, user_scaled = pl.pallas_call(
        functools.partial(user_kernel, suffix),
        out_shape=[
            pltpu.VMEM((user_rows, width), jnp.float32),
            pltpu.VMEM((levels, user_rows, width), jnp.bfloat16),
        ],
        in_specs=[vmem] * 4,
        out_specs=[vmem] * 2,
        compiler_params=params,
        cost_estimate=cost(0, 0),
    )(user_weights, user_queries, user_keys, user_values)

    totals = [pltpu.VMEM((token_count, width), jnp.float32), pltpu.VMEM((user_rows, width), jnp.float32)]

    def read(offsets, accs, ahead=()):
        groups = [tuple(offsets[i : i + 2]) for i in range(0, len(offsets), 2)]
        wide = len(ahead) * width
        extra = [pltpu.VMEM((rows, wide), jnp.bfloat16) for rows in (token_count, user_rows) if ahead]
        return pl.pallas_call(
            functools.partial(read_kernel, depth, suffix, groups, ahead),
            out_shape=totals + extra,
            in_specs=[vmem] * (5 + len(offsets)),
            out_specs=[vmem] * (2 + len(extra)),
            scratch_shapes=[pltpu.SMEM((user_count,), jnp.int32), pltpu.SemaphoreType.DMA(())],
            compiler_params=params,
            cost_estimate=cost(0, 0),
        )(lengths, slab_scaled, user_scaled, *accs, *[whole[m] for m in offsets])

    state = after(slab_weights, [state])[0]
    whole = {0: state, 1: swap(state, 0)}
    direct = [1 << bit for bit in outer]
    for m in direct:
        whole[m] = join(user_acc, sides[m])
        whole[m | 1] = swap(whole[m], 0)
    accs = read([0, 1] + direct, (slab_acc, user_acc))
    for m in later:
        whole[m] = join(accs[0], sides[m])
        whole[m | 1] = swap(whole[m], 0)
    last = later[-1]
    if later[:-1]:
        accs = read([n for m in later[:-1] for n in (m, m | 1)], accs)
    *accs, slab_ahead, user_ahead = read([m | 1 for m in direct], accs, (last, last | 1))
    slab_total, user_total, square = pl.pallas_call(
        last_kernel,
        out_shape=totals + [pltpu.VMEM((lines, ROWS), jnp.float32)],
        in_specs=[vmem] * 6,
        out_specs=[vmem] * 3,
        compiler_params=params,
        cost_estimate=cost(0, 0),
    )(slab_ahead, user_ahead, *accs, whole[last], whole[last | 1])

    mate = jnp.zeros_like(square)
    for bit in range(head_axis.bit_length() - 1):
        square = square + mate
        mate = lax.ppermute(square, "head", [(i, i ^ (1 << bit)) for i in range(head_axis)])

    slab_out, user_out = pl.pallas_call(
        functools.partial(norm_kernel, float(width * head_axis), chunks),
        out_shape=[bf16((token_count, width)), bf16((user_rows, width))],
        in_specs=[vmem] * 5,
        out_specs=[hbm] * 2,
        scratch_shapes=[
            pltpu.VMEM((token_count, width), jnp.bfloat16),
            pltpu.VMEM((user_rows, width), jnp.bfloat16),
            pltpu.SemaphoreType.DMA((2, chunks)),
        ],
        compiler_params=params,
    )(slab_total, user_total, norm_gain.reshape(1, width), square, mate)
    return slab_out, user_out.reshape(user_count, suffix, width)


def solution(mesh):
    return jax.shard_map(
        local,
        mesh=mesh,
        in_specs=(
            P("seq", "head"),
            P("seq", "head"),
            P("seq", "head"),
            P(None, "head", "seq"),
            P("head"),
            P("seq", None, "head"),
            P("seq", None, "head"),
            P("seq", None, "head"),
            P("seq", None, "head", None),
            P("seq"),
        ),
        out_specs=(P("seq", "head"), P("seq", None, "head")),
        check_vma=False,
    )
```

```python
import functools

import jax
import jax.numpy as jnp
from jax import lax
from jax.experimental import pallas as pl
from jax.experimental.pallas import tpu as pltpu
from jax.sharding import PartitionSpec as P

HEADS = 64
HD = 128
ROWS = 128
VMEM_BYTES = 20 * 1024 * 1024


def matmul(a, b, contract):
    return lax.dot_general(a, b, (contract, ((), ())), preferred_element_type=jnp.float32)


def load_columns(sources, targets, sems, chunks):
    copies = []
    for chunk in range(chunks):
        group = []
        for i, (source, target) in enumerate(zip(sources, targets)):
            size = source.shape[1] // chunks
            cols = pl.ds(chunk * size, size)
            group.append(pltpu.make_async_copy(source.at[:, cols], target.at[:, cols], sems.at[i, chunk]))
            group[-1].start()
        copies.append(group)

    def wait(chunk):
        for copy in copies[chunk]:
            copy.wait()

    return wait


def state_kernel(chunks, key_hbm, value_hbm, first_ref, second_ref, whole_ref, key_ref, value_ref, sems):
    half = first_ref.shape[0]
    head_count = 2 * half
    wait = load_columns((key_hbm, value_hbm), (key_ref, value_ref), sems, chunks)
    for head in range(head_count):
        if head % (head_count // chunks) == 0:
            wait(head // (head_count // chunks))
        cols = slice(head * HD, (head + 1) * HD)
        state = matmul(key_ref[:, cols], value_ref[:, cols], ((0,), (0,)))
        whole_ref[0, head] = state.astype(jnp.bfloat16)
    parity = lax.axis_index("seq") & 1
    for head in range(half):
        first_ref[head] = whole_ref[0, parity * half + head]
        second_ref[head] = whole_ref[0, (1 - parity) * half + head]


def join_kernel(order_ref, *refs):
    out_ref = refs[-1]
    parity = lax.axis_index("seq") & 1
    half = out_ref.shape[1] // 2
    for i in range(out_ref.shape[0]):
        for side in range(2):
            for head in range(half):
                out_ref[i, (side ^ parity) * half + head] = refs[2 * i + side][head]


def turned(offset, depth):
    return sum(((offset >> bit) & 1) << (depth - bit) for bit in range(1, depth))


def level_of(offset, target, position, depth):
    low = offset & 1
    block = position ^ low ^ jnp.where(((position ^ low) & 1) == 1, turned(offset, depth), offset - low)
    diff = block ^ target
    level = sum((diff >= (1 << step)).astype(jnp.int32) for step in range(depth))
    return jnp.where(block < target, level, 0)


def attend(mask, q_ref, k_ref, v_ref, w_ref, o_ref):
    head_count = q_ref.shape[1] // HD
    step = 2
    for first in range(0, head_count, step):
        units = [
            (head, slice(head * HD, (head + 1) * HD), slice(start, start + ROWS))
            for head in range(first, first + step)
            for start in range(0, q_ref.shape[0], ROWS)
        ]
        scores = [matmul(q_ref[rows, cols], k_ref[rows, cols], ((1,), (1,))) for _, cols, rows in units]
        scores = [jnp.where(mask, score, 0.0).astype(jnp.bfloat16) for score in scores]
        results = [matmul(score, v_ref[rows, cols], ((1,), (0,))) for score, (_, cols, rows) in zip(scores, units)]
        for result, (head, cols, rows) in zip(results, units):
            o_ref[rows, cols] = result * w_ref[rows, head : head + 1]


def causal_mask(suffix=ROWS):
    row = lax.broadcasted_iota(jnp.int32, (ROWS, ROWS), 0)
    col = lax.broadcasted_iota(jnp.int32, (ROWS, ROWS), 1)
    return jnp.logical_and(row >= col, row // suffix == col // suffix)


def start_copies(sources, targets, sems):
    copies = [
        pltpu.make_async_copy(source, target, sems.at[i]) for i, (source, target) in enumerate(zip(sources, targets))
    ]
    for copy in copies:
        copy.start()
    return copies


def load_kernel(suffix, *refs):
    sources, (sw_ref, uw_ref), loaded, tables, sems = refs[:4], refs[4:6], refs[6:8], refs[8:10], refs[10]
    copies = start_copies(sources, (*tables, *loaded), sems)
    slab_table, user_table = tables
    for copy in copies[:2]:
        copy.wait()
    columns = sw_ref.shape[1]
    row = lax.broadcasted_iota(jnp.int32, (slab_table.shape[0], columns), 0)
    col = lax.broadcasted_iota(jnp.int32, (slab_table.shape[0], columns), 1)
    same = jnp.where(row == col, 1.0, 0.0).astype(jnp.bfloat16)
    sw_ref[...] = matmul(slab_table[...], same, ((0,), (0,)))
    for user in range(user_table.shape[0]):
        uw_ref[user * suffix : (user + 1) * suffix] = matmul(user_table[user], same, ((0,), (0,)))
    for copy in copies[2:]:
        copy.wait()


def scale_queries(q_ref, w_ref, scaled_ref):
    head_count = q_ref.shape[1] // HD
    scaled_ref[0] = jnp.zeros_like(scaled_ref[0])
    for head in range(head_count):
        cols = slice(head * HD, (head + 1) * HD)
        query = q_ref[:, cols]
        for level in range(1, scaled_ref.shape[0]):
            column = level * head_count + head
            weight = jnp.broadcast_to(w_ref[:, column : column + 1], query.shape).astype(jnp.bfloat16)
            scaled_ref[level, :, cols] = query * weight


def slab_kernel(*refs):
    sources, (w_ref, q_ref, k_ref, v_ref), (o_ref, scaled_ref), loaded, sems = (
        refs[:3],
        refs[3:7],
        refs[7:9],
        refs[9:12],
        refs[12],
    )
    copies = start_copies(sources, loaded, sems)
    attend(causal_mask(), q_ref, k_ref, v_ref, w_ref, o_ref)
    scale_queries(q_ref, w_ref, scaled_ref)
    for copy in copies:
        copy.wait()


def user_kernel(suffix, w_ref, q_ref, k_ref, v_ref, o_ref, scaled_ref):
    attend(causal_mask(suffix), q_ref, k_ref, v_ref, w_ref, o_ref)
    scale_queries(q_ref, w_ref, scaled_ref)


def read_kernel(depth, suffix, groups, ahead, length_ref, ss_ref, us_ref, sa_ref, ua_ref, *rest):
    offsets = [offset for group in groups for offset in group]
    states, outs, (lengths, sem) = rest[: len(offsets)], rest[len(offsets) : -2], rest[-2:]
    copy = pltpu.make_async_copy(length_ref, lengths, sem)
    copy.start()
    copy.wait()
    position = lax.axis_index("seq").astype(jnp.int32)
    head_count = sa_ref.shape[1] // HD
    users = range(ua_ref.shape[0] // suffix)
    targets = [lengths[user] for user in users]
    slab_level = {o: level_of(o, position, position, depth) for o in (*offsets, *ahead)}
    user_level = {o: [level_of(o, target, position, depth) for target in targets] for o in (*offsets, *ahead)}

    def slab_rows(offset, cols):
        return ss_ref[slab_level[offset], :, cols]

    def user_rows(offset, cols):
        parts = [us_ref[user_level[offset][user], user * suffix : (user + 1) * suffix, cols] for user in users]
        return jnp.concatenate(parts, axis=0)

    for head in range(head_count):
        cols = slice(head * HD, (head + 1) * HD)
        for pick, a_ref, t_ref in ((slab_rows, sa_ref, outs[0]), (user_rows, ua_ref, outs[1])):
            total = a_ref[:, cols]
            for group in groups:
                queries = jnp.concatenate([pick(offset, cols) for offset in group], axis=1)
                blocks = jnp.concatenate([states[offsets.index(offset)][0, head] for offset in group], axis=0)
                total = total + matmul(queries, blocks, ((1,), (0,)))
            t_ref[:, cols] = total
        for pick, out_ref in zip((slab_rows, user_rows), outs[2:]):
            for i, offset in enumerate(ahead):
                start = (head * len(ahead) + i) * HD
                out_ref[:, start : start + HD] = pick(offset, cols)


def last_kernel(ss_ref, us_ref, sa_ref, ua_ref, state_ref, mate_ref, st_ref, ut_ref, square_ref):
    head_count = sa_ref.shape[1] // HD
    line = 0
    for q_ref, a_ref, t_ref in ((ss_ref, sa_ref, st_ref), (us_ref, ua_ref, ut_ref)):
        for start in range(0, a_ref.shape[0], ROWS):
            rows = slice(start, start + ROWS)
            squares = None
            for head in range(head_count):
                cols = slice(head * HD, (head + 1) * HD)
                wide = slice(2 * head * HD, 2 * (head + 1) * HD)
                states = jnp.concatenate([state_ref[0, head], mate_ref[0, head]], axis=0)
                total = a_ref[rows, cols] + matmul(q_ref[rows, wide], states, ((1,), (0,)))
                t_ref[rows, cols] = total
                squares = total * total if squares is None else squares + total * total
            square_ref[line : line + 1] = jnp.sum(jnp.transpose(squares), axis=0, keepdims=True)
            line += 1


def norm_kernel(features, chunks, st_ref, ut_ref, gain_ref, one_ref, two_ref, so_hbm, uo_hbm, so_ref, uo_ref, sems):
    square = one_ref[...] + two_ref[...]
    scale = lax.rsqrt(square / features + 1e-06)
    size = st_ref.shape[1] // chunks
    copies = []
    line = 0
    for t_ref, o_ref, o_hbm in ((st_ref, so_ref, so_hbm), (ut_ref, uo_ref, uo_hbm)):
        for start in range(0, t_ref.shape[0], ROWS):
            rows = slice(start, start + ROWS)
            factor = jnp.transpose(jnp.broadcast_to(scale[line : line + 1], (ROWS, ROWS)))
            for chunk in range(chunks):
                for low in range(chunk * size, (chunk + 1) * size, HD):
                    cols = slice(low, low + HD)
                    gain = gain_ref[:, cols].astype(jnp.float32)
                    o_ref[rows, cols] = (t_ref[rows, cols] * factor * gain).astype(jnp.bfloat16)
                part = (pl.ds(start, ROWS), pl.ds(chunk * size, size))
                copies.append(pltpu.make_async_copy(o_ref.at[part], o_hbm.at[part], sems.at[line, chunk]))
                copies[-1].start()
            line += 1
    for copy in copies:
        copy.wait()


def local(
    slab_query,
    slab_key,
    slab_value,
    slab_levels,
    norm_gain,
    user_query,
    user_key,
    user_value,
    user_levels,
    prefix_lengths,
):
    seq_count = lax.axis_size("seq")
    head_axis = lax.axis_size("head")
    depth = seq_count.bit_length() - 1
    token_count, width = slab_query.shape
    head_count = width // HD
    half = head_count // 2
    user_count, suffix = user_query.shape[:2]
    user_rows = user_count * suffix
    lines = (token_count + user_rows) // ROWS
    params = pltpu.CompilerParams(vmem_limit_bytes=VMEM_BYTES)
    bf16 = functools.partial(jax.ShapeDtypeStruct, dtype=jnp.bfloat16)
    vmem = pl.BlockSpec(memory_space=pltpu.VMEM)
    anywhere = pl.BlockSpec(memory_space=pl.ANY)
    hbm = pl.BlockSpec(memory_space=pltpu.HBM)
    chunks = min(4, half)
    rows_cost = 2 * width * (token_count + user_rows)

    def pinned(*arrays):
        return [pltpu.with_memory_space_constraint(array, pltpu.HBM) for array in arrays]

    def cost(flops, moved):
        return pl.CostEstimate(flops=flops, bytes_accessed=moved, transcendentals=0)

    held = {0: list(range(seq_count))}

    def swap(value, bit, offset):
        other = depth - bit if bit else 0
        pairs = [(i, i ^ (1 << (other if i & 1 else bit))) for i in range(seq_count)]
        pairs = [(i, j) for i, j in pairs if held[offset][i] not in (None, seq_count - 1)]
        came = {j: held[offset][i] for i, j in pairs}
        held[offset | (1 << bit)] = [came.get(i) for i in range(seq_count)]
        return lax.ppermute(value, "seq", pairs)

    def after(results, values):
        return list(lax.optimization_barrier((results, values))[1])

    def join(order, halves):
        return pl.pallas_call(
            join_kernel,
            out_shape=pltpu.VMEM((len(halves) // 2, head_count, HD, HD), jnp.bfloat16),
            in_specs=[anywhere] + [vmem] * len(halves),
            out_specs=vmem,
            compiler_params=params,
        )(order, *halves)

    half_state = pltpu.VMEM((half, HD, HD), jnp.bfloat16)
    slab_rows = pltpu.VMEM((token_count, width), jnp.bfloat16)
    first, second, state, slab_keys, slab_values = pl.pallas_call(
        functools.partial(state_kernel, chunks),
        out_shape=[half_state, half_state, pltpu.VMEM((1, head_count, HD, HD), jnp.bfloat16), slab_rows, slab_rows],
        in_specs=[hbm] * 2,
        out_specs=[vmem] * 5,
        scratch_shapes=[pltpu.SemaphoreType.DMA((2, chunks))],
        compiler_params=params,
    )(*pinned(slab_key, slab_value))
    halves = [first, second]

    outer = list(range(1, depth))
    places = [(bit, side) for bit in outer for side in range(2)]
    ahead = [(bit, 0) for bit in outer[:-1]] + [(bit, 1) for bit in outer[1:]] or places
    sides = {1 << bit: [None, None] for bit in outer}
    for bit, side in ahead:
        sides[1 << bit][side] = swap(halves[side], bit, 0)
    levels = depth + 1
    slab_table = slab_levels.reshape(-1, token_count)
    user_table = user_levels.reshape(user_count, -1, suffix)
    user_array = pltpu.VMEM((user_rows, width), jnp.bfloat16)
    slab_weights, user_weights, slab_queries, lengths = pl.pallas_call(
        functools.partial(load_kernel, suffix),
        out_shape=[
            pltpu.VMEM((token_count, levels * head_count), jnp.float32),
            pltpu.VMEM((user_rows, levels * head_count), jnp.float32),
            slab_rows,
            pltpu.VMEM((user_count,), jnp.int32),
        ],
        in_specs=[hbm] * 4,
        out_specs=[vmem] * 4,
        scratch_shapes=[
            pltpu.VMEM(slab_table.shape, jnp.bfloat16),
            pltpu.VMEM(user_table.shape, jnp.bfloat16),
            pltpu.SemaphoreType.DMA((4,)),
        ],
        compiler_params=params,
        cost_estimate=cost(0, 0),
    )(*pinned(slab_table, user_table, slab_query, prefix_lengths))
    halves = after(slab_weights, halves)
    for bit, side in places:
        if (bit, side) not in ahead:
            sides[1 << bit][side] = swap(halves[side], bit, 0)
    slab_acc, slab_scaled, user_queries, user_keys, user_values = pl.pallas_call(
        slab_kernel,
        out_shape=[
            pltpu.VMEM((token_count, width), jnp.float32),
            pltpu.VMEM((levels, token_count, width), jnp.bfloat16),
        ]
        + [user_array] * 3,
        in_specs=[hbm] * 3 + [vmem] * 4,
        out_specs=[vmem] * 5,
        scratch_shapes=[pltpu.SemaphoreType.DMA((3,))],
        compiler_params=params,
        cost_estimate=cost(0, 0),
    )(
        *pinned(*[array.reshape(user_rows, width) for array in (user_query, user_key, user_value)]),
        slab_weights,
        slab_queries,
        slab_keys,
        slab_values,
    )

    later = sorted((m for m in range(0, seq_count, 2) if m.bit_count() > 1), key=lambda m: m.bit_count())
    for (bit, side), value in zip(ahead, after(slab_acc, [sides[1 << bit][side] for bit, side in ahead])):
        sides[1 << bit][side] = value
    for m in later:
        high, low = m.bit_length() - 1, (m & -m).bit_length() - 1
        sides[m] = [
            swap(sides[m ^ (1 << high)][0], high, m ^ (1 << high)),
            swap(sides[m ^ (1 << low)][1], low, m ^ (1 << low)),
        ]
    user_weights = after([sides[1 << bit][side] for bit, side in ahead], [user_weights])[0]
    user_acc, user_scaled = pl.pallas_call(
        functools.partial(user_kernel, suffix),
        out_shape=[
            pltpu.VMEM((user_rows, width), jnp.float32),
            pltpu.VMEM((levels, user_rows, width), jnp.bfloat16),
        ],
        in_specs=[vmem] * 4,
        out_specs=[vmem] * 2,
        compiler_params=params,
        cost_estimate=cost(0, 0),
    )(user_weights, user_queries, user_keys, user_values)

    totals = [pltpu.VMEM((token_count, width), jnp.float32), pltpu.VMEM((user_rows, width), jnp.float32)]

    def read(offsets, accs, ahead=()):
        groups = [tuple(offsets[i : i + 2]) for i in range(0, len(offsets), 2)]
        wide = len(ahead) * width
        extra = [pltpu.VMEM((rows, wide), jnp.bfloat16) for rows in (token_count, user_rows) if ahead]
        return pl.pallas_call(
            functools.partial(read_kernel, depth, suffix, groups, ahead),
            out_shape=totals + extra,
            in_specs=[vmem] * (5 + len(offsets)),
            out_specs=[vmem] * (2 + len(extra)),
            scratch_shapes=[pltpu.SMEM((user_count,), jnp.int32), pltpu.SemaphoreType.DMA(())],
            compiler_params=params,
            cost_estimate=cost(0, 0),
        )(lengths, slab_scaled, user_scaled, *accs, *[whole[m] for m in offsets])

    state = after(slab_weights, [state])[0]
    whole = {0: state, 1: swap(state, 0, 0)}
    direct = [1 << bit for bit in outer]
    for m in direct:
        whole[m] = join(user_acc, sides[m])
        whole[m | 1] = swap(whole[m], 0, m)
    last = later[-1]
    *accs, slab_ahead, user_ahead = read([0, 1] + direct, (slab_acc, user_acc), (last, last | 1))
    for m in later:
        whole[m] = join(accs[0], sides[m])
        whole[m | 1] = swap(whole[m], 0, m)
    if later[:-1]:
        accs = read([n for m in later[:-1] for n in (m, m | 1)], accs)
    accs = read([m | 1 for m in direct], accs)
    slab_total, user_total, square = pl.pallas_call(
        last_kernel,
        out_shape=totals + [pltpu.VMEM((lines, ROWS), jnp.float32)],
        in_specs=[vmem] * 6,
        out_specs=[vmem] * 3,
        compiler_params=params,
        cost_estimate=cost(0, 0),
    )(slab_ahead, user_ahead, *accs, whole[last], whole[last | 1])

    mate = jnp.zeros_like(square)
    for bit in range(head_axis.bit_length() - 1):
        square = square + mate
        mate = lax.ppermute(square, "head", [(i, i ^ (1 << bit)) for i in range(head_axis)])

    slab_out, user_out = pl.pallas_call(
        functools.partial(norm_kernel, float(width * head_axis), chunks),
        out_shape=[bf16((token_count, width)), bf16((user_rows, width))],
        in_specs=[vmem] * 5,
        out_specs=[hbm] * 2,
        scratch_shapes=[
            pltpu.VMEM((token_count, width), jnp.bfloat16),
            pltpu.VMEM((user_rows, width), jnp.bfloat16),
            pltpu.SemaphoreType.DMA((lines, chunks)),
        ],
        compiler_params=params,
    )(slab_total, user_total, norm_gain.reshape(1, width), square, mate)
    return slab_out, user_out.reshape(user_count, suffix, width)


def solution(mesh):
    return jax.shard_map(
        local,
        mesh=mesh,
        in_specs=(
            P("seq", "head"),
            P("seq", "head"),
            P("seq", "head"),
            P(None, "head", "seq"),
            P("head"),
            P("seq", None, "head"),
            P("seq", None, "head"),
            P("seq", None, "head"),
            P("seq", None, "head", None),
            P("seq"),
        ),
        out_specs=(P("seq", "head"), P("seq", None, "head")),
        check_vma=False,
    )
```

```python
import functools

import jax
import jax.numpy as jnp
from jax import lax
from jax.experimental import pallas as pl
from jax.experimental.pallas import tpu as pltpu
from jax.sharding import PartitionSpec as P

HEADS = 64
HD = 128
ROWS = 128
VMEM_BYTES = 20 * 1024 * 1024


def matmul(a, b, contract):
    return lax.dot_general(a, b, (contract, ((), ())), preferred_element_type=jnp.float32)


def start_copies(sources, targets, sems):
    copies = [
        pltpu.make_async_copy(source, target, sems.at[i]) for i, (source, target) in enumerate(zip(sources, targets))
    ]
    for copy in copies:
        copy.start()
    return copies


def block_states(key_ref, value_ref, base, out_ref):
    for head in range(out_ref.shape[0]):
        start = head * HD if isinstance(base, int) else pl.multiple_of(base + head * HD, HD)
        cols = pl.ds(start, HD)
        out_ref[head] = matmul(key_ref[:, cols], value_ref[:, cols], ((0,), (0,))).astype(jnp.bfloat16)


def first_kernel(key_hbm, value_hbm, out_ref, key_ref, value_ref, sems):
    width = key_ref.shape[1]
    parity = lax.axis_index("seq") & 1
    cols = pl.ds(pl.multiple_of(parity * width, width), width)
    copies = start_copies((key_hbm.at[:, cols], value_hbm.at[:, cols]), (key_ref, value_ref), sems)
    for copy in copies:
        copy.wait()
    block_states(key_ref, value_ref, 0, out_ref)


def join_kernel(order_ref, *refs):
    out_ref = refs[-1]
    parity = lax.axis_index("seq") & 1
    half = out_ref.shape[1] // 2
    for i in range(out_ref.shape[0]):
        for side in range(2):
            for head in range(half):
                out_ref[i, (side ^ parity) * half + head] = refs[2 * i + side][head]


def turned(offset, depth):
    return sum(((offset >> bit) & 1) << (depth - bit) for bit in range(1, depth))


def level_of(offset, target, position, depth):
    low = offset & 1
    block = position ^ low ^ jnp.where(((position ^ low) & 1) == 1, turned(offset, depth), offset - low)
    diff = block ^ target
    level = sum((diff >= (1 << step)).astype(jnp.int32) for step in range(depth))
    return jnp.where(block < target, level, 0)


def attend(mask, q_ref, k_ref, v_ref, w_ref, o_ref):
    head_count = q_ref.shape[1] // HD
    step = 2
    for first in range(0, head_count, step):
        units = [
            (head, slice(head * HD, (head + 1) * HD), slice(start, start + ROWS))
            for head in range(first, first + step)
            for start in range(0, q_ref.shape[0], ROWS)
        ]
        scores = [matmul(q_ref[rows, cols], k_ref[rows, cols], ((1,), (1,))) for _, cols, rows in units]
        scores = [jnp.where(mask, score, 0.0).astype(jnp.bfloat16) for score in scores]
        results = [matmul(score, v_ref[rows, cols], ((1,), (0,))) for score, (_, cols, rows) in zip(scores, units)]
        for result, (head, cols, rows) in zip(results, units):
            o_ref[rows, cols] = result * w_ref[rows, head : head + 1]


def causal_mask(suffix=ROWS):
    row = lax.broadcasted_iota(jnp.int32, (ROWS, ROWS), 0)
    col = lax.broadcasted_iota(jnp.int32, (ROWS, ROWS), 1)
    return jnp.logical_and(row >= col, row // suffix == col // suffix)


def load_kernel(suffix, *refs):
    first_ref, sources, (second_ref, whole_ref, sw_ref, uw_ref), rest = refs[0], refs[1:7], refs[7:11], refs[11:]
    loaded, tables, sems = rest[:4], rest[4:6], rest[6]
    key_ref, value_ref = loaded[:2]
    copies = start_copies(sources, (*loaded[:2], *tables, *loaded[2:]), sems)
    slab_table, user_table = tables
    half = first_ref.shape[0]
    parity = lax.axis_index("seq") & 1
    for copy in copies[:2]:
        copy.wait()
    block_states(key_ref, value_ref, (1 - parity) * (half * HD), second_ref)
    for head in range(half):
        whole_ref[0, parity * half + head] = first_ref[head]
        whole_ref[0, (1 - parity) * half + head] = second_ref[head]
    for copy in copies[2:4]:
        copy.wait()
    columns = sw_ref.shape[1]
    row = lax.broadcasted_iota(jnp.int32, (slab_table.shape[0], columns), 0)
    col = lax.broadcasted_iota(jnp.int32, (slab_table.shape[0], columns), 1)
    same = jnp.where(row == col, 1.0, 0.0).astype(jnp.bfloat16)
    sw_ref[...] = matmul(slab_table[...], same, ((0,), (0,)))
    for user in range(user_table.shape[0]):
        uw_ref[user * suffix : (user + 1) * suffix] = matmul(user_table[user], same, ((0,), (0,)))
    for copy in copies[4:]:
        copy.wait()


def scale_queries(q_ref, w_ref, scaled_ref):
    head_count = q_ref.shape[1] // HD
    scaled_ref[0] = jnp.zeros_like(scaled_ref[0])
    for head in range(head_count):
        cols = slice(head * HD, (head + 1) * HD)
        query = q_ref[:, cols]
        for level in range(1, scaled_ref.shape[0]):
            column = level * head_count + head
            weight = jnp.broadcast_to(w_ref[:, column : column + 1], query.shape).astype(jnp.bfloat16)
            scaled_ref[level, :, cols] = query * weight


def slab_kernel(*refs):
    sources, (w_ref, q_ref, k_ref, v_ref), (o_ref, scaled_ref), loaded, sems = (
        refs[:3],
        refs[3:7],
        refs[7:9],
        refs[9:12],
        refs[12],
    )
    copies = start_copies(sources, loaded, sems)
    attend(causal_mask(), q_ref, k_ref, v_ref, w_ref, o_ref)
    scale_queries(q_ref, w_ref, scaled_ref)
    for copy in copies:
        copy.wait()


def user_kernel(suffix, w_ref, q_ref, k_ref, v_ref, o_ref, scaled_ref):
    attend(causal_mask(suffix), q_ref, k_ref, v_ref, w_ref, o_ref)
    scale_queries(q_ref, w_ref, scaled_ref)


def read_kernel(depth, suffix, groups, ahead, length_ref, ss_ref, us_ref, sa_ref, ua_ref, *rest):
    offsets = [offset for group in groups for offset in group]
    states, outs, (lengths, sem) = rest[: len(offsets)], rest[len(offsets) : -2], rest[-2:]
    copy = pltpu.make_async_copy(length_ref, lengths, sem)
    copy.start()
    copy.wait()
    position = lax.axis_index("seq").astype(jnp.int32)
    head_count = sa_ref.shape[1] // HD
    users = range(ua_ref.shape[0] // suffix)
    targets = [lengths[user] for user in users]
    slab_level = {o: level_of(o, position, position, depth) for o in (*offsets, *ahead)}
    user_level = {o: [level_of(o, target, position, depth) for target in targets] for o in (*offsets, *ahead)}

    def slab_rows(offset, cols):
        return ss_ref[slab_level[offset], :, cols]

    def user_rows(offset, cols):
        parts = [us_ref[user_level[offset][user], user * suffix : (user + 1) * suffix, cols] for user in users]
        return jnp.concatenate(parts, axis=0)

    for head in range(head_count):
        cols = slice(head * HD, (head + 1) * HD)
        for pick, a_ref, t_ref in ((slab_rows, sa_ref, outs[0]), (user_rows, ua_ref, outs[1])):
            total = a_ref[:, cols]
            for group in groups:
                queries = jnp.concatenate([pick(offset, cols) for offset in group], axis=1)
                blocks = jnp.concatenate([states[offsets.index(offset)][0, head] for offset in group], axis=0)
                total = total + matmul(queries, blocks, ((1,), (0,)))
            t_ref[:, cols] = total
        for pick, out_ref in zip((slab_rows, user_rows), outs[2:]):
            for i, offset in enumerate(ahead):
                start = (head * len(ahead) + i) * HD
                out_ref[:, start : start + HD] = pick(offset, cols)


def last_kernel(ss_ref, us_ref, sa_ref, ua_ref, state_ref, mate_ref, st_ref, ut_ref, square_ref):
    head_count = sa_ref.shape[1] // HD
    line = 0
    for q_ref, a_ref, t_ref in ((ss_ref, sa_ref, st_ref), (us_ref, ua_ref, ut_ref)):
        for start in range(0, a_ref.shape[0], ROWS):
            rows = slice(start, start + ROWS)
            squares = None
            for head in range(head_count):
                cols = slice(head * HD, (head + 1) * HD)
                wide = slice(2 * head * HD, 2 * (head + 1) * HD)
                states = jnp.concatenate([state_ref[0, head], mate_ref[0, head]], axis=0)
                total = a_ref[rows, cols] + matmul(q_ref[rows, wide], states, ((1,), (0,)))
                t_ref[rows, cols] = total
                squares = total * total if squares is None else squares + total * total
            square_ref[line : line + 1] = jnp.sum(jnp.transpose(squares), axis=0, keepdims=True)
            line += 1


def norm_kernel(features, chunks, st_ref, ut_ref, gain_ref, one_ref, two_ref, so_hbm, uo_hbm, so_ref, uo_ref, sems):
    square = one_ref[...] + two_ref[...]
    scale = lax.rsqrt(square / features + 1e-06)
    size = st_ref.shape[1] // chunks
    copies = []
    line = 0
    for t_ref, o_ref, o_hbm in ((st_ref, so_ref, so_hbm), (ut_ref, uo_ref, uo_hbm)):
        for start in range(0, t_ref.shape[0], ROWS):
            rows = slice(start, start + ROWS)
            factor = jnp.transpose(jnp.broadcast_to(scale[line : line + 1], (ROWS, ROWS)))
            for chunk in range(chunks):
                for low in range(chunk * size, (chunk + 1) * size, HD):
                    cols = slice(low, low + HD)
                    gain = gain_ref[:, cols].astype(jnp.float32)
                    o_ref[rows, cols] = (t_ref[rows, cols] * factor * gain).astype(jnp.bfloat16)
                part = (pl.ds(start, ROWS), pl.ds(chunk * size, size))
                copies.append(pltpu.make_async_copy(o_ref.at[part], o_hbm.at[part], sems.at[line, chunk]))
                copies[-1].start()
            line += 1
    for copy in copies:
        copy.wait()


def local(
    slab_query,
    slab_key,
    slab_value,
    slab_levels,
    norm_gain,
    user_query,
    user_key,
    user_value,
    user_levels,
    prefix_lengths,
):
    seq_count = lax.axis_size("seq")
    head_axis = lax.axis_size("head")
    depth = seq_count.bit_length() - 1
    token_count, width = slab_query.shape
    head_count = width // HD
    half = head_count // 2
    user_count, suffix = user_query.shape[:2]
    user_rows = user_count * suffix
    lines = (token_count + user_rows) // ROWS
    params = pltpu.CompilerParams(vmem_limit_bytes=VMEM_BYTES)
    bf16 = functools.partial(jax.ShapeDtypeStruct, dtype=jnp.bfloat16)
    vmem = pl.BlockSpec(memory_space=pltpu.VMEM)
    anywhere = pl.BlockSpec(memory_space=pl.ANY)
    hbm = pl.BlockSpec(memory_space=pltpu.HBM)
    chunks = min(4, half)
    rows_cost = 2 * width * (token_count + user_rows)

    def pinned(*arrays):
        return [pltpu.with_memory_space_constraint(array, pltpu.HBM) for array in arrays]

    def cost(flops, moved):
        return pl.CostEstimate(flops=flops, bytes_accessed=moved, transcendentals=0)

    def swap(value, bit):
        other = depth - bit if bit else 0
        return lax.ppermute(value, "seq", [(i, i ^ (1 << (other if i & 1 else bit))) for i in range(seq_count)])

    def after(results, values):
        return list(lax.optimization_barrier((results, values))[1])

    def join(order, halves):
        return pl.pallas_call(
            join_kernel,
            out_shape=pltpu.VMEM((len(halves) // 2, head_count, HD, HD), jnp.bfloat16),
            in_specs=[anywhere] + [vmem] * len(halves),
            out_specs=vmem,
            compiler_params=params,
        )(order, *halves)

    half_state = pltpu.VMEM((half, HD, HD), jnp.bfloat16)
    slab_rows = pltpu.VMEM((token_count, width), jnp.bfloat16)
    first = pl.pallas_call(
        first_kernel,
        out_shape=half_state,
        in_specs=[hbm] * 2,
        out_specs=vmem,
        scratch_shapes=[pltpu.VMEM((token_count, width // 2), jnp.bfloat16)] * 2 + [pltpu.SemaphoreType.DMA((2,))],
        compiler_params=params,
    )(*pinned(slab_key, slab_value))

    outer = list(range(1, depth))
    places = [(bit, side) for bit in outer for side in range(2)]
    ahead = [(bit, 0) for bit in outer[:-1]] + [(bit, 1) for bit in outer[1:]]
    sides = {1 << bit: [None, None] for bit in outer}
    levels = depth + 1
    slab_table = slab_levels.reshape(-1, token_count)
    user_table = user_levels.reshape(user_count, -1, suffix)
    user_array = pltpu.VMEM((user_rows, width), jnp.bfloat16)
    second, state, slab_weights, user_weights, slab_keys, slab_values, slab_queries, lengths = pl.pallas_call(
        functools.partial(load_kernel, suffix),
        out_shape=[
            half_state,
            pltpu.VMEM((1, head_count, HD, HD), jnp.bfloat16),
            pltpu.VMEM((token_count, levels * head_count), jnp.float32),
            pltpu.VMEM((user_rows, levels * head_count), jnp.float32),
            slab_rows,
            slab_rows,
            slab_rows,
            pltpu.VMEM((user_count,), jnp.int32),
        ],
        in_specs=[vmem] + [hbm] * 6,
        out_specs=[vmem] * 8,
        scratch_shapes=[
            pltpu.VMEM(slab_table.shape, jnp.bfloat16),
            pltpu.VMEM(user_table.shape, jnp.bfloat16),
            pltpu.SemaphoreType.DMA((6,)),
        ],
        compiler_params=params,
        cost_estimate=cost(0, 0),
    )(first, *pinned(slab_key, slab_value, slab_table, user_table, slab_query, prefix_lengths))
    halves = [first, second]
    for bit, side in ahead:
        sides[1 << bit][side] = swap(halves[side], bit)
    halves = after(slab_weights, halves)
    for bit, side in places:
        if (bit, side) not in ahead:
            sides[1 << bit][side] = swap(halves[side], bit)
    slab_acc, slab_scaled, user_queries, user_keys, user_values = pl.pallas_call(
        slab_kernel,
        out_shape=[
            pltpu.VMEM((token_count, width), jnp.float32),
            pltpu.VMEM((levels, token_count, width), jnp.bfloat16),
        ]
        + [user_array] * 3,
        in_specs=[hbm] * 3 + [vmem] * 4,
        out_specs=[vmem] * 5,
        scratch_shapes=[pltpu.SemaphoreType.DMA((3,))],
        compiler_params=params,
        cost_estimate=cost(0, 0),
    )(
        *pinned(*[array.reshape(user_rows, width) for array in (user_query, user_key, user_value)]),
        slab_weights,
        slab_queries,
        slab_keys,
        slab_values,
    )

    later = sorted((m for m in range(0, seq_count, 2) if m.bit_count() > 1), key=lambda m: m.bit_count())
    for (bit, side), value in zip(ahead, after(slab_acc, [sides[1 << bit][side] for bit, side in ahead])):
        sides[1 << bit][side] = value
    for m in later:
        high, low = m.bit_length() - 1, (m & -m).bit_length() - 1
        sides[m] = [swap(sides[m ^ (1 << high)][0], high), swap(sides[m ^ (1 << low)][1], low)]
    user_weights = after([sides[1 << bit][side] for bit, side in ahead], [user_weights])[0]
    user_acc, user_scaled = pl.pallas_call(
        functools.partial(user_kernel, suffix),
        out_shape=[
            pltpu.VMEM((user_rows, width), jnp.float32),
            pltpu.VMEM((levels, user_rows, width), jnp.bfloat16),
        ],
        in_specs=[vmem] * 4,
        out_specs=[vmem] * 2,
        compiler_params=params,
        cost_estimate=cost(0, 0),
    )(user_weights, user_queries, user_keys, user_values)

    totals = [pltpu.VMEM((token_count, width), jnp.float32), pltpu.VMEM((user_rows, width), jnp.float32)]

    def read(offsets, accs, ahead=()):
        groups = [tuple(offsets[i : i + 2]) for i in range(0, len(offsets), 2)]
        wide = len(ahead) * width
        extra = [pltpu.VMEM((rows, wide), jnp.bfloat16) for rows in (token_count, user_rows) if ahead]
        return pl.pallas_call(
            functools.partial(read_kernel, depth, suffix, groups, ahead),
            out_shape=totals + extra,
            in_specs=[vmem] * (5 + len(offsets)),
            out_specs=[vmem] * (2 + len(extra)),
            scratch_shapes=[pltpu.SMEM((user_count,), jnp.int32), pltpu.SemaphoreType.DMA(())],
            compiler_params=params,
            cost_estimate=cost(0, 0),
        )(lengths, slab_scaled, user_scaled, *accs, *[whole[m] for m in offsets])

    whole = {0: state, 1: swap(state, 0)}
    direct = [1 << bit for bit in outer]
    for m in direct:
        whole[m] = join(user_acc, sides[m])
        whole[m | 1] = swap(whole[m], 0)
    last = later[-1]
    *accs, slab_ahead, user_ahead = read([0, 1] + direct, (slab_acc, user_acc), (last, last | 1))
    for m in later:
        whole[m] = join(accs[0], sides[m])
        whole[m | 1] = swap(whole[m], 0)
    if later[:-1]:
        accs = read([n for m in later[:-1] for n in (m, m | 1)], accs)
    accs = read([m | 1 for m in direct], accs)
    slab_total, user_total, square = pl.pallas_call(
        last_kernel,
        out_shape=totals + [pltpu.VMEM((lines, ROWS), jnp.float32)],
        in_specs=[vmem] * 6,
        out_specs=[vmem] * 3,
        compiler_params=params,
        cost_estimate=cost(0, 0),
    )(slab_ahead, user_ahead, *accs, whole[last], whole[last | 1])

    mate = jnp.zeros_like(square)
    for bit in range(head_axis.bit_length() - 1):
        square = square + mate
        mate = lax.ppermute(square, "head", [(i, i ^ (1 << bit)) for i in range(head_axis)])

    slab_out, user_out = pl.pallas_call(
        functools.partial(norm_kernel, float(width * head_axis), chunks),
        out_shape=[bf16((token_count, width)), bf16((user_rows, width))],
        in_specs=[vmem] * 5,
        out_specs=[hbm] * 2,
        scratch_shapes=[
            pltpu.VMEM((token_count, width), jnp.bfloat16),
            pltpu.VMEM((user_rows, width), jnp.bfloat16),
            pltpu.SemaphoreType.DMA((lines, chunks)),
        ],
        compiler_params=params,
    )(slab_total, user_total, norm_gain.reshape(1, width), square, mate)
    return slab_out, user_out.reshape(user_count, suffix, width)


def solution(mesh):
    return jax.shard_map(
        local,
        mesh=mesh,
        in_specs=(
            P("seq", "head"),
            P("seq", "head"),
            P("seq", "head"),
            P(None, "head", "seq"),
            P("head"),
            P("seq", None, "head"),
            P("seq", None, "head"),
            P("seq", None, "head"),
            P("seq", None, "head", None),
            P("seq"),
        ),
        out_specs=(P("seq", "head"), P("seq", None, "head")),
        check_vma=False,
    )
```

```python
import functools

import jax
import jax.numpy as jnp
from jax import lax
from jax.experimental import pallas as pl
from jax.experimental.pallas import tpu as pltpu
from jax.sharding import PartitionSpec as P

HEADS = 64
HD = 128
ROWS = 128
VMEM_BYTES = 20 * 1024 * 1024


def matmul(a, b, contract):
    return lax.dot_general(a, b, (contract, ((), ())), preferred_element_type=jnp.float32)


def start_copies(sources, targets, sems):
    copies = [
        pltpu.make_async_copy(source, target, sems.at[i]) for i, (source, target) in enumerate(zip(sources, targets))
    ]
    for copy in copies:
        copy.start()
    return copies


def block_states(key_ref, value_ref, base, out_ref):
    for head in range(out_ref.shape[0]):
        start = head * HD if isinstance(base, int) else pl.multiple_of(base + head * HD, HD)
        cols = pl.ds(start, HD)
        out_ref[head] = matmul(key_ref[:, cols], value_ref[:, cols], ((0,), (0,))).astype(jnp.bfloat16)


def first_kernel(key_hbm, value_hbm, out_ref, key_ref, value_ref, sems):
    width = key_ref.shape[1]
    parity = lax.axis_index("seq") & 1
    cols = pl.ds(pl.multiple_of(parity * width, width), width)
    copies = start_copies((key_hbm.at[:, cols], value_hbm.at[:, cols]), (key_ref, value_ref), sems)
    for copy in copies:
        copy.wait()
    block_states(key_ref, value_ref, 0, out_ref)


def join_kernel(order_ref, *refs):
    out_ref = refs[-1]
    parity = lax.axis_index("seq") & 1
    half = out_ref.shape[1] // 2
    for i in range(out_ref.shape[0]):
        for side in range(2):
            for head in range(half):
                out_ref[i, (side ^ parity) * half + head] = refs[2 * i + side][head]


def turned(offset, depth):
    return sum(((offset >> bit) & 1) << (depth - bit) for bit in range(1, depth))


def level_of(offset, target, position, depth):
    low = offset & 1
    block = position ^ low ^ jnp.where(((position ^ low) & 1) == 1, turned(offset, depth), offset - low)
    diff = block ^ target
    level = sum((diff >= (1 << step)).astype(jnp.int32) for step in range(depth))
    return jnp.where(block < target, level, 0)


def attend(mask, q_ref, k_ref, v_ref, w_ref, o_ref, wait=lambda head: None):
    head_count = q_ref.shape[1] // HD
    step = 2
    for first in range(0, head_count, step):
        wait(first)
        units = [
            (head, slice(head * HD, (head + 1) * HD), slice(start, start + ROWS))
            for head in range(first, first + step)
            for start in range(0, q_ref.shape[0], ROWS)
        ]
        scores = [matmul(q_ref[rows, cols], k_ref[rows, cols], ((1,), (1,))) for _, cols, rows in units]
        scores = [jnp.where(mask, score, 0.0).astype(jnp.bfloat16) for score in scores]
        results = [matmul(score, v_ref[rows, cols], ((1,), (0,))) for score, (_, cols, rows) in zip(scores, units)]
        for result, (head, cols, rows) in zip(results, units):
            o_ref[rows, cols] = result * w_ref[rows, head : head + 1]


def causal_mask(suffix=ROWS):
    row = lax.broadcasted_iota(jnp.int32, (ROWS, ROWS), 0)
    col = lax.broadcasted_iota(jnp.int32, (ROWS, ROWS), 1)
    return jnp.logical_and(row >= col, row // suffix == col // suffix)


def load_kernel(suffix, *refs):
    first_ref, sources, (second_ref, whole_ref, sw_ref, uw_ref), rest = refs[0], refs[1:7], refs[7:11], refs[11:]
    loaded, tables, sems = rest[:4], rest[4:6], rest[6]
    key_ref, value_ref = loaded[:2]
    copies = start_copies(sources, (*loaded[:2], *tables, *loaded[2:]), sems)
    slab_table, user_table = tables
    half = first_ref.shape[0]
    parity = lax.axis_index("seq") & 1
    for copy in copies[:2]:
        copy.wait()
    block_states(key_ref, value_ref, (1 - parity) * (half * HD), second_ref)
    for head in range(half):
        whole_ref[0, parity * half + head] = first_ref[head]
        whole_ref[0, (1 - parity) * half + head] = second_ref[head]
    for copy in copies[2:4]:
        copy.wait()
    columns = sw_ref.shape[1]
    row = lax.broadcasted_iota(jnp.int32, (slab_table.shape[0], columns), 0)
    col = lax.broadcasted_iota(jnp.int32, (slab_table.shape[0], columns), 1)
    same = jnp.where(row == col, 1.0, 0.0).astype(jnp.bfloat16)
    sw_ref[...] = matmul(slab_table[...], same, ((0,), (0,)))
    for user in range(user_table.shape[0]):
        uw_ref[user * suffix : (user + 1) * suffix] = matmul(user_table[user], same, ((0,), (0,)))
    for copy in copies[4:]:
        copy.wait()


def scale_queries(q_ref, w_ref, scaled_ref):
    head_count = q_ref.shape[1] // HD
    scaled_ref[0] = jnp.zeros_like(scaled_ref[0])
    for head in range(head_count):
        cols = slice(head * HD, (head + 1) * HD)
        query = q_ref[:, cols]
        for level in range(1, scaled_ref.shape[0]):
            column = level * head_count + head
            weight = jnp.broadcast_to(w_ref[:, column : column + 1], query.shape).astype(jnp.bfloat16)
            scaled_ref[level, :, cols] = query * weight


def slab_kernel(w_ref, q_ref, k_ref, v_ref, o_ref):
    attend(causal_mask(), q_ref, k_ref, v_ref, w_ref, o_ref)


def user_kernel(suffix, *refs):
    sources, (sw_ref, sq_ref, uw_ref), (ss_ref, o_ref, us_ref), loaded, sems = (
        refs[:3],
        refs[3:6],
        refs[6:9],
        refs[9:12],
        refs[12],
    )
    chunks = sems.shape[1]
    size = loaded[0].shape[1] // chunks
    copies = []
    for chunk in range(chunks):
        cols = pl.ds(chunk * size, size)
        group = [
            pltpu.make_async_copy(source.at[:, cols], target.at[:, cols], sems.at[i, chunk])
            for i, (source, target) in enumerate(zip(sources, loaded))
        ]
        for copy in group:
            copy.start()
        copies.append(group)
    scale_queries(sq_ref, sw_ref, ss_ref)

    def wait(head):
        if head * HD % size == 0:
            for copy in copies[head * HD // size]:
                copy.wait()

    attend(causal_mask(suffix), *loaded, uw_ref, o_ref, wait)
    scale_queries(loaded[0], uw_ref, us_ref)


def read_kernel(depth, suffix, groups, ahead, length_ref, ss_ref, us_ref, sa_ref, ua_ref, *rest):
    offsets = [offset for group in groups for offset in group]
    states, outs, (lengths, sem) = rest[: len(offsets)], rest[len(offsets) : -2], rest[-2:]
    copy = pltpu.make_async_copy(length_ref, lengths, sem)
    copy.start()
    copy.wait()
    position = lax.axis_index("seq").astype(jnp.int32)
    head_count = sa_ref.shape[1] // HD
    users = range(ua_ref.shape[0] // suffix)
    targets = [lengths[user] for user in users]
    slab_level = {o: level_of(o, position, position, depth) for o in (*offsets, *ahead)}
    user_level = {o: [level_of(o, target, position, depth) for target in targets] for o in (*offsets, *ahead)}

    def slab_rows(offset, cols):
        return ss_ref[slab_level[offset], :, cols]

    def user_rows(offset, cols):
        parts = [us_ref[user_level[offset][user], user * suffix : (user + 1) * suffix, cols] for user in users]
        return jnp.concatenate(parts, axis=0)

    for head in range(head_count):
        cols = slice(head * HD, (head + 1) * HD)
        for pick, a_ref, t_ref in ((slab_rows, sa_ref, outs[0]), (user_rows, ua_ref, outs[1])):
            total = a_ref[:, cols]
            for group in groups:
                queries = jnp.concatenate([pick(offset, cols) for offset in group], axis=1)
                blocks = jnp.concatenate([states[offsets.index(offset)][0, head] for offset in group], axis=0)
                total = total + matmul(queries, blocks, ((1,), (0,)))
            t_ref[:, cols] = total
        for pick, out_ref in zip((slab_rows, user_rows), outs[2:]):
            for i, offset in enumerate(ahead):
                start = (head * len(ahead) + i) * HD
                out_ref[:, start : start + HD] = pick(offset, cols)


def last_kernel(ss_ref, us_ref, sa_ref, ua_ref, state_ref, mate_ref, st_ref, ut_ref, square_ref):
    head_count = sa_ref.shape[1] // HD
    line = 0
    for q_ref, a_ref, t_ref in ((ss_ref, sa_ref, st_ref), (us_ref, ua_ref, ut_ref)):
        for start in range(0, a_ref.shape[0], ROWS):
            rows = slice(start, start + ROWS)
            squares = None
            for head in range(head_count):
                cols = slice(head * HD, (head + 1) * HD)
                wide = slice(2 * head * HD, 2 * (head + 1) * HD)
                states = jnp.concatenate([state_ref[0, head], mate_ref[0, head]], axis=0)
                total = a_ref[rows, cols] + matmul(q_ref[rows, wide], states, ((1,), (0,)))
                t_ref[rows, cols] = total
                squares = total * total if squares is None else squares + total * total
            square_ref[line : line + 1] = jnp.sum(jnp.transpose(squares), axis=0, keepdims=True)
            line += 1


def norm_kernel(features, chunks, st_ref, ut_ref, gain_ref, one_ref, two_ref, so_hbm, uo_hbm, so_ref, uo_ref, sems):
    square = one_ref[...] + two_ref[...]
    scale = lax.rsqrt(square / features + 1e-06)
    size = st_ref.shape[1] // chunks
    copies = []
    line = 0
    for t_ref, o_ref, o_hbm in ((st_ref, so_ref, so_hbm), (ut_ref, uo_ref, uo_hbm)):
        for start in range(0, t_ref.shape[0], ROWS):
            rows = slice(start, start + ROWS)
            factor = jnp.transpose(jnp.broadcast_to(scale[line : line + 1], (ROWS, ROWS)))
            for chunk in range(chunks):
                for low in range(chunk * size, (chunk + 1) * size, HD):
                    cols = slice(low, low + HD)
                    gain = gain_ref[:, cols].astype(jnp.float32)
                    o_ref[rows, cols] = (t_ref[rows, cols] * factor * gain).astype(jnp.bfloat16)
                part = (pl.ds(start, ROWS), pl.ds(chunk * size, size))
                copies.append(pltpu.make_async_copy(o_ref.at[part], o_hbm.at[part], sems.at[line, chunk]))
                copies[-1].start()
            line += 1
    for copy in copies:
        copy.wait()


def local(
    slab_query,
    slab_key,
    slab_value,
    slab_levels,
    norm_gain,
    user_query,
    user_key,
    user_value,
    user_levels,
    prefix_lengths,
):
    seq_count = lax.axis_size("seq")
    head_axis = lax.axis_size("head")
    depth = seq_count.bit_length() - 1
    token_count, width = slab_query.shape
    head_count = width // HD
    half = head_count // 2
    user_count, suffix = user_query.shape[:2]
    user_rows = user_count * suffix
    lines = (token_count + user_rows) // ROWS
    params = pltpu.CompilerParams(vmem_limit_bytes=VMEM_BYTES)
    bf16 = functools.partial(jax.ShapeDtypeStruct, dtype=jnp.bfloat16)
    vmem = pl.BlockSpec(memory_space=pltpu.VMEM)
    anywhere = pl.BlockSpec(memory_space=pl.ANY)
    hbm = pl.BlockSpec(memory_space=pltpu.HBM)
    chunks = min(4, half)
    rows_cost = 2 * width * (token_count + user_rows)

    def pinned(*arrays):
        return [pltpu.with_memory_space_constraint(array, pltpu.HBM) for array in arrays]

    def cost(flops, moved):
        return pl.CostEstimate(flops=flops, bytes_accessed=moved, transcendentals=0)

    def swap(value, bit):
        other = depth - bit if bit else 0
        return lax.ppermute(value, "seq", [(i, i ^ (1 << (other if i & 1 else bit))) for i in range(seq_count)])

    def after(results, values):
        return list(lax.optimization_barrier((results, values))[1])

    def join(order, halves):
        return pl.pallas_call(
            join_kernel,
            out_shape=pltpu.VMEM((len(halves) // 2, head_count, HD, HD), jnp.bfloat16),
            in_specs=[anywhere] + [vmem] * len(halves),
            out_specs=vmem,
            compiler_params=params,
        )(order, *halves)

    half_state = pltpu.VMEM((half, HD, HD), jnp.bfloat16)
    slab_rows = pltpu.VMEM((token_count, width), jnp.bfloat16)
    first = pl.pallas_call(
        first_kernel,
        out_shape=half_state,
        in_specs=[hbm] * 2,
        out_specs=vmem,
        scratch_shapes=[pltpu.VMEM((token_count, width // 2), jnp.bfloat16)] * 2 + [pltpu.SemaphoreType.DMA((2,))],
        compiler_params=params,
    )(*pinned(slab_key, slab_value))

    outer = list(range(1, depth))
    places = [(bit, side) for bit in outer for side in range(2)]
    ahead = [(bit, 0) for bit in outer[:-1]] + [(bit, 1) for bit in outer[1:]]
    sides = {1 << bit: [None, None] for bit in outer}
    levels = depth + 1
    slab_table = slab_levels.reshape(-1, token_count)
    user_table = user_levels.reshape(user_count, -1, suffix)
    second, state, slab_weights, user_weights, slab_keys, slab_values, slab_queries, lengths = pl.pallas_call(
        functools.partial(load_kernel, suffix),
        out_shape=[
            half_state,
            pltpu.VMEM((1, head_count, HD, HD), jnp.bfloat16),
            pltpu.VMEM((token_count, levels * head_count), jnp.float32),
            pltpu.VMEM((user_rows, levels * head_count), jnp.float32),
            slab_rows,
            slab_rows,
            slab_rows,
            pltpu.VMEM((user_count,), jnp.int32),
        ],
        in_specs=[vmem] + [hbm] * 6,
        out_specs=[vmem] * 8,
        scratch_shapes=[
            pltpu.VMEM(slab_table.shape, jnp.bfloat16),
            pltpu.VMEM(user_table.shape, jnp.bfloat16),
            pltpu.SemaphoreType.DMA((6,)),
        ],
        compiler_params=params,
        cost_estimate=cost(0, 0),
    )(first, *pinned(slab_key, slab_value, slab_table, user_table, slab_query, prefix_lengths))
    halves = [first, second]
    for bit, side in ahead:
        sides[1 << bit][side] = swap(halves[side], bit)
    slab_acc = pl.pallas_call(
        slab_kernel,
        out_shape=pltpu.VMEM((token_count, width), jnp.float32),
        in_specs=[vmem] * 4,
        out_specs=vmem,
        compiler_params=params,
        cost_estimate=cost(0, 0),
    )(slab_weights, slab_queries, slab_keys, slab_values)
    halves = after(slab_acc, halves)
    for bit, side in places:
        if (bit, side) not in ahead:
            sides[1 << bit][side] = swap(halves[side], bit)
    later = sorted((m for m in range(0, seq_count, 2) if m.bit_count() > 1), key=lambda m: m.bit_count())
    for (bit, side), value in zip(ahead, after(slab_acc, [sides[1 << bit][side] for bit, side in ahead])):
        sides[1 << bit][side] = value
    for m in later:
        high, low = m.bit_length() - 1, (m & -m).bit_length() - 1
        sides[m] = [swap(sides[m ^ (1 << high)][0], high), swap(sides[m ^ (1 << low)][1], low)]
    user_weights = after([sides[1 << bit][side] for bit, side in ahead], [user_weights])[0]
    slab_scaled, user_acc, user_scaled = pl.pallas_call(
        functools.partial(user_kernel, suffix),
        out_shape=[
            pltpu.VMEM((levels, token_count, width), jnp.bfloat16),
            pltpu.VMEM((user_rows, width), jnp.float32),
            pltpu.VMEM((levels, user_rows, width), jnp.bfloat16),
        ],
        in_specs=[hbm] * 3 + [vmem] * 3,
        out_specs=[vmem] * 3,
        scratch_shapes=[pltpu.VMEM((user_rows, width), jnp.bfloat16)] * 3 + [pltpu.SemaphoreType.DMA((3, chunks))],
        compiler_params=params,
        cost_estimate=cost(0, 0),
    )(
        *pinned(*[array.reshape(user_rows, width) for array in (user_query, user_key, user_value)]),
        slab_weights,
        slab_queries,
        user_weights,
    )

    totals = [pltpu.VMEM((token_count, width), jnp.float32), pltpu.VMEM((user_rows, width), jnp.float32)]

    def read(offsets, accs, ahead=()):
        groups = [tuple(offsets[i : i + 2]) for i in range(0, len(offsets), 2)]
        wide = len(ahead) * width
        extra = [pltpu.VMEM((rows, wide), jnp.bfloat16) for rows in (token_count, user_rows) if ahead]
        return pl.pallas_call(
            functools.partial(read_kernel, depth, suffix, groups, ahead),
            out_shape=totals + extra,
            in_specs=[vmem] * (5 + len(offsets)),
            out_specs=[vmem] * (2 + len(extra)),
            scratch_shapes=[pltpu.SMEM((user_count,), jnp.int32), pltpu.SemaphoreType.DMA(())],
            compiler_params=params,
            cost_estimate=cost(0, 0),
        )(lengths, slab_scaled, user_scaled, *accs, *[whole[m] for m in offsets])

    whole = {0: state, 1: swap(state, 0)}
    direct = [1 << bit for bit in outer]
    for m in direct:
        whole[m] = join(user_acc, sides[m])
        whole[m | 1] = swap(whole[m], 0)
    last = later[-1]
    *accs, slab_ahead, user_ahead = read([0, 1] + direct, (slab_acc, user_acc), (last, last | 1))
    for m in later:
        whole[m] = join(accs[0], sides[m])
        whole[m | 1] = swap(whole[m], 0)
    if later[:-1]:
        accs = read([n for m in later[:-1] for n in (m, m | 1)], accs)
    accs = read([m | 1 for m in direct], accs)
    slab_total, user_total, square = pl.pallas_call(
        last_kernel,
        out_shape=totals + [pltpu.VMEM((lines, ROWS), jnp.float32)],
        in_specs=[vmem] * 6,
        out_specs=[vmem] * 3,
        compiler_params=params,
        cost_estimate=cost(0, 0),
    )(slab_ahead, user_ahead, *accs, whole[last], whole[last | 1])

    mate = jnp.zeros_like(square)
    for bit in range(head_axis.bit_length() - 1):
        square = square + mate
        mate = lax.ppermute(square, "head", [(i, i ^ (1 << bit)) for i in range(head_axis)])

    slab_out, user_out = pl.pallas_call(
        functools.partial(norm_kernel, float(width * head_axis), chunks),
        out_shape=[bf16((token_count, width)), bf16((user_rows, width))],
        in_specs=[vmem] * 5,
        out_specs=[hbm] * 2,
        scratch_shapes=[
            pltpu.VMEM((token_count, width), jnp.bfloat16),
            pltpu.VMEM((user_rows, width), jnp.bfloat16),
            pltpu.SemaphoreType.DMA((lines, chunks)),
        ],
        compiler_params=params,
    )(slab_total, user_total, norm_gain.reshape(1, width), square, mate)
    return slab_out, user_out.reshape(user_count, suffix, width)


def solution(mesh):
    return jax.shard_map(
        local,
        mesh=mesh,
        in_specs=(
            P("seq", "head"),
            P("seq", "head"),
            P("seq", "head"),
            P(None, "head", "seq"),
            P("head"),
            P("seq", None, "head"),
            P("seq", None, "head"),
            P("seq", None, "head"),
            P("seq", None, "head", None),
            P("seq"),
        ),
        out_specs=(P("seq", "head"), P("seq", None, "head")),
        check_vma=False,
    )
```

```python
import functools

import jax
import jax.numpy as jnp
from jax import lax
from jax.experimental import pallas as pl
from jax.experimental.pallas import tpu as pltpu
from jax.sharding import PartitionSpec as P

HEADS = 64
HD = 128
ROWS = 128
VMEM_BYTES = 20 * 1024 * 1024


def matmul(a, b, contract):
    return lax.dot_general(a, b, (contract, ((), ())), preferred_element_type=jnp.float32)


def load_columns(sources, targets, sems, chunks):
    copies = []
    for chunk in range(chunks):
        group = []
        for i, (source, target) in enumerate(zip(sources, targets)):
            size = source.shape[1] // chunks
            cols = pl.ds(chunk * size, size)
            group.append(pltpu.make_async_copy(source.at[:, cols], target.at[:, cols], sems.at[i, chunk]))
            group[-1].start()
        copies.append(group)

    def wait(chunk):
        for copy in copies[chunk]:
            copy.wait()

    return wait


def state_kernel(chunks, key_hbm, value_hbm, first_ref, second_ref, whole_ref, key_ref, value_ref, sems):
    half = first_ref.shape[0]
    head_count = 2 * half
    wait = load_columns((key_hbm, value_hbm), (key_ref, value_ref), sems, chunks)
    for head in range(head_count):
        if head % (head_count // chunks) == 0:
            wait(head // (head_count // chunks))
        cols = slice(head * HD, (head + 1) * HD)
        state = matmul(key_ref[:, cols], value_ref[:, cols], ((0,), (0,)))
        whole_ref[0, head] = state.astype(jnp.bfloat16)
    parity = lax.axis_index("seq") & 1
    for head in range(half):
        first_ref[head] = whole_ref[0, parity * half + head]
        second_ref[head] = whole_ref[0, (1 - parity) * half + head]


def join_kernel(order_ref, *refs):
    out_ref = refs[-1]
    parity = lax.axis_index("seq") & 1
    half = out_ref.shape[1] // 2
    for i in range(out_ref.shape[0]):
        for side in range(2):
            for head in range(half):
                out_ref[i, (side ^ parity) * half + head] = refs[2 * i + side][head]


def turned(offset, depth):
    return sum(((offset >> bit) & 1) << (depth - bit) for bit in range(1, depth))


def level_of(offset, target, position, depth):
    low = offset & 1
    block = position ^ low ^ jnp.where(((position ^ low) & 1) == 1, turned(offset, depth), offset - low)
    diff = block ^ target
    level = sum((diff >= (1 << step)).astype(jnp.int32) for step in range(depth))
    return jnp.where(block < target, level, 0)


def attend(mask, q_ref, k_ref, v_ref, w_ref, o_ref):
    head_count = q_ref.shape[1] // HD
    step = 2
    for first in range(0, head_count, step):
        units = [
            (head, slice(head * HD, (head + 1) * HD), slice(start, start + ROWS))
            for head in range(first, first + step)
            for start in range(0, q_ref.shape[0], ROWS)
        ]
        scores = [matmul(q_ref[rows, cols], k_ref[rows, cols], ((1,), (1,))) for _, cols, rows in units]
        scores = [jnp.where(mask, score, 0.0).astype(jnp.bfloat16) for score in scores]
        results = [matmul(score, v_ref[rows, cols], ((1,), (0,))) for score, (_, cols, rows) in zip(scores, units)]
        for result, (head, cols, rows) in zip(results, units):
            o_ref[rows, cols] = result * w_ref[rows, head : head + 1]


def causal_mask(suffix=ROWS):
    row = lax.broadcasted_iota(jnp.int32, (ROWS, ROWS), 0)
    col = lax.broadcasted_iota(jnp.int32, (ROWS, ROWS), 1)
    return jnp.logical_and(row >= col, row // suffix == col // suffix)


def start_copies(sources, targets, sems):
    copies = [
        pltpu.make_async_copy(source, target, sems.at[i]) for i, (source, target) in enumerate(zip(sources, targets))
    ]
    for copy in copies:
        copy.start()
    return copies


def load_kernel(suffix, *refs):
    sources, (k_ref, v_ref), (sw_ref, uw_ref), rest = refs[:4], refs[4:6], refs[6:8], refs[8:]
    loaded, o_ref, tables, sems = rest[:2], rest[2], rest[3:5], rest[5]
    copies = start_copies(sources, (*tables, *loaded), sems)
    slab_table, user_table = tables
    for copy in copies[:2]:
        copy.wait()
    columns = sw_ref.shape[1]
    row = lax.broadcasted_iota(jnp.int32, (slab_table.shape[0], columns), 0)
    col = lax.broadcasted_iota(jnp.int32, (slab_table.shape[0], columns), 1)
    same = jnp.where(row == col, 1.0, 0.0).astype(jnp.bfloat16)
    sw_ref[...] = matmul(slab_table[...], same, ((0,), (0,)))
    for user in range(user_table.shape[0]):
        uw_ref[user * suffix : (user + 1) * suffix] = matmul(user_table[user], same, ((0,), (0,)))
    for copy in copies[2:]:
        copy.wait()
    attend(causal_mask(), loaded[0], k_ref, v_ref, sw_ref, o_ref)


def scale_queries(q_ref, w_ref, scaled_ref):
    head_count = q_ref.shape[1] // HD
    scaled_ref[0] = jnp.zeros_like(scaled_ref[0])
    for head in range(head_count):
        cols = slice(head * HD, (head + 1) * HD)
        query = q_ref[:, cols]
        for level in range(1, scaled_ref.shape[0]):
            column = level * head_count + head
            weight = jnp.broadcast_to(w_ref[:, column : column + 1], query.shape).astype(jnp.bfloat16)
            scaled_ref[level, :, cols] = query * weight


def scale_kernel(*refs):
    sources, (w_ref, q_ref), scaled_ref, loaded, sems = refs[:3], refs[3:5], refs[5], refs[6:9], refs[9]
    copies = start_copies(sources, loaded, sems)
    scale_queries(q_ref, w_ref, scaled_ref)
    for copy in copies:
        copy.wait()


def user_kernel(suffix, w_ref, q_ref, k_ref, v_ref, o_ref, scaled_ref):
    attend(causal_mask(suffix), q_ref, k_ref, v_ref, w_ref, o_ref)
    scale_queries(q_ref, w_ref, scaled_ref)


def read_kernel(depth, suffix, groups, ahead, length_ref, ss_ref, us_ref, sa_ref, ua_ref, *rest):
    offsets = [offset for group in groups for offset in group]
    states, outs, (lengths, sem) = rest[: len(offsets)], rest[len(offsets) : -2], rest[-2:]
    copy = pltpu.make_async_copy(length_ref, lengths, sem)
    copy.start()
    copy.wait()
    position = lax.axis_index("seq").astype(jnp.int32)
    head_count = sa_ref.shape[1] // HD
    users = range(ua_ref.shape[0] // suffix)
    targets = [lengths[user] for user in users]
    slab_level = {o: level_of(o, position, position, depth) for o in (*offsets, *ahead)}
    user_level = {o: [level_of(o, target, position, depth) for target in targets] for o in (*offsets, *ahead)}

    def slab_rows(offset, cols):
        return ss_ref[slab_level[offset], :, cols]

    def user_rows(offset, cols):
        parts = [us_ref[user_level[offset][user], user * suffix : (user + 1) * suffix, cols] for user in users]
        return jnp.concatenate(parts, axis=0)

    for head in range(head_count):
        cols = slice(head * HD, (head + 1) * HD)
        for pick, a_ref, t_ref in ((slab_rows, sa_ref, outs[0]), (user_rows, ua_ref, outs[1])):
            total = a_ref[:, cols]
            for group in groups:
                queries = jnp.concatenate([pick(offset, cols) for offset in group], axis=1)
                blocks = jnp.concatenate([states[offsets.index(offset)][0, head] for offset in group], axis=0)
                total = total + matmul(queries, blocks, ((1,), (0,)))
            t_ref[:, cols] = total
        for pick, out_ref in zip((slab_rows, user_rows), outs[2:]):
            for i, offset in enumerate(ahead):
                start = (head * len(ahead) + i) * HD
                out_ref[:, start : start + HD] = pick(offset, cols)


def last_kernel(ss_ref, us_ref, sa_ref, ua_ref, state_ref, mate_ref, st_ref, ut_ref, square_ref):
    head_count = sa_ref.shape[1] // HD
    square_ref[...] = jnp.zeros_like(square_ref)
    line = 0
    for q_ref, a_ref, t_ref in ((ss_ref, sa_ref, st_ref), (us_ref, ua_ref, ut_ref)):
        for start in range(0, a_ref.shape[0], ROWS):
            rows = slice(start, start + ROWS)
            squares = None
            for head in range(head_count):
                cols = slice(head * HD, (head + 1) * HD)
                wide = slice(2 * head * HD, 2 * (head + 1) * HD)
                states = jnp.concatenate([state_ref[0, head], mate_ref[0, head]], axis=0)
                total = a_ref[rows, cols] + matmul(q_ref[rows, wide], states, ((1,), (0,)))
                t_ref[rows, cols] = total
                squares = total * total if squares is None else squares + total * total
            square_ref[line : line + 1] = jnp.sum(jnp.transpose(squares), axis=0, keepdims=True)
            line += 1


def norm_kernel(features, chunks, st_ref, ut_ref, gain_ref, one_ref, two_ref, so_hbm, uo_hbm, so_ref, uo_ref, sems):
    square = one_ref[...] + two_ref[...]
    scale = lax.rsqrt(square / features + 1e-06)
    size = st_ref.shape[1] // chunks
    copies = []
    line = 0
    for t_ref, o_ref, o_hbm in ((st_ref, so_ref, so_hbm), (ut_ref, uo_ref, uo_hbm)):
        for start in range(0, t_ref.shape[0], ROWS):
            rows = slice(start, start + ROWS)
            factor = jnp.transpose(jnp.broadcast_to(scale[line : line + 1], (ROWS, ROWS)))
            for chunk in range(chunks):
                for low in range(chunk * size, (chunk + 1) * size, HD):
                    cols = slice(low, low + HD)
                    gain = gain_ref[:, cols].astype(jnp.float32)
                    o_ref[rows, cols] = (t_ref[rows, cols] * factor * gain).astype(jnp.bfloat16)
                part = (pl.ds(start, ROWS), pl.ds(chunk * size, size))
                copies.append(pltpu.make_async_copy(o_ref.at[part], o_hbm.at[part], sems.at[line, chunk]))
                copies[-1].start()
            line += 1
    for copy in copies:
        copy.wait()


def local(
    slab_query,
    slab_key,
    slab_value,
    slab_levels,
    norm_gain,
    user_query,
    user_key,
    user_value,
    user_levels,
    prefix_lengths,
):
    seq_count = lax.axis_size("seq")
    head_axis = lax.axis_size("head")
    depth = seq_count.bit_length() - 1
    token_count, width = slab_query.shape
    head_count = width // HD
    half = head_count // 2
    user_count, suffix = user_query.shape[:2]
    user_rows = user_count * suffix
    lines = (token_count + user_rows) // ROWS
    params = pltpu.CompilerParams(vmem_limit_bytes=VMEM_BYTES)
    bf16 = functools.partial(jax.ShapeDtypeStruct, dtype=jnp.bfloat16)
    vmem = pl.BlockSpec(memory_space=pltpu.VMEM)
    anywhere = pl.BlockSpec(memory_space=pl.ANY)
    hbm = pl.BlockSpec(memory_space=pltpu.HBM)
    chunks = min(4, half)
    rows_cost = 2 * width * (token_count + user_rows)

    def pinned(*arrays):
        return [pltpu.with_memory_space_constraint(array, pltpu.HBM) for array in arrays]

    def cost(flops, moved):
        return pl.CostEstimate(flops=flops, bytes_accessed=moved, transcendentals=0)

    def swap(value, bit):
        other = depth - bit if bit else 0
        return lax.ppermute(value, "seq", [(i, i ^ (1 << (other if i & 1 else bit))) for i in range(seq_count)])

    def after(results, values):
        return list(lax.optimization_barrier((results, values))[1])

    def join(order, halves):
        return pl.pallas_call(
            join_kernel,
            out_shape=pltpu.VMEM((len(halves) // 2, head_count, HD, HD), jnp.bfloat16),
            in_specs=[anywhere] + [vmem] * len(halves),
            out_specs=vmem,
            compiler_params=params,
        )(order, *halves)

    half_state = pltpu.VMEM((half, HD, HD), jnp.bfloat16)
    slab_rows = pltpu.VMEM((token_count, width), jnp.bfloat16)
    first, second, state, slab_keys, slab_values = pl.pallas_call(
        functools.partial(state_kernel, chunks),
        out_shape=[half_state, half_state, pltpu.VMEM((1, head_count, HD, HD), jnp.bfloat16), slab_rows, slab_rows],
        in_specs=[hbm] * 2,
        out_specs=[vmem] * 5,
        scratch_shapes=[pltpu.SemaphoreType.DMA((2, chunks))],
        compiler_params=params,
    )(*pinned(slab_key, slab_value))
    halves = [first, second]

    outer = list(range(1, depth))
    places = [(bit, side) for bit in outer for side in range(2)]
    ahead = [(bit, 0) for bit in outer[:-1]] + [(bit, 1) for bit in outer[1:]] or places
    sides = {1 << bit: [None, None] for bit in outer}
    for bit, side in ahead:
        sides[1 << bit][side] = swap(halves[side], bit)
    levels = depth + 1
    slab_table = slab_levels.reshape(-1, token_count)
    user_table = user_levels.reshape(user_count, -1, suffix)
    user_array = pltpu.VMEM((user_rows, width), jnp.bfloat16)
    slab_weights, user_weights, slab_queries, lengths, slab_acc = pl.pallas_call(
        functools.partial(load_kernel, suffix),
        out_shape=[
            pltpu.VMEM((token_count, levels * head_count), jnp.float32),
            pltpu.VMEM((user_rows, levels * head_count), jnp.float32),
            slab_rows,
            pltpu.VMEM((user_count,), jnp.int32),
            pltpu.VMEM((token_count, width), jnp.float32),
        ],
        in_specs=[hbm] * 4 + [vmem] * 2,
        out_specs=[vmem] * 5,
        scratch_shapes=[
            pltpu.VMEM(slab_table.shape, jnp.bfloat16),
            pltpu.VMEM(user_table.shape, jnp.bfloat16),
            pltpu.SemaphoreType.DMA((4,)),
        ],
        compiler_params=params,
        cost_estimate=cost(0, 0),
    )(*pinned(slab_table, user_table, slab_query, prefix_lengths), slab_keys, slab_values)
    halves = after(slab_weights, halves)
    for bit, side in places:
        if (bit, side) not in ahead:
            sides[1 << bit][side] = swap(halves[side], bit)
    slab_scaled, user_queries, user_keys, user_values = pl.pallas_call(
        scale_kernel,
        out_shape=[pltpu.VMEM((levels, token_count, width), jnp.bfloat16)] + [user_array] * 3,
        in_specs=[hbm] * 3 + [vmem] * 2,
        out_specs=[vmem] * 4,
        scratch_shapes=[pltpu.SemaphoreType.DMA((3,))],
        compiler_params=params,
        cost_estimate=cost(0, 0),
    )(
        *pinned(*[array.reshape(user_rows, width) for array in (user_query, user_key, user_value)]),
        slab_weights,
        slab_queries,
    )

    later = sorted((m for m in range(0, seq_count, 2) if m.bit_count() > 1), key=lambda m: m.bit_count())
    for (bit, side), value in zip(ahead, after(slab_scaled, [sides[1 << bit][side] for bit, side in ahead])):
        sides[1 << bit][side] = value
    for m in later:
        high, low = m.bit_length() - 1, (m & -m).bit_length() - 1
        sides[m] = [swap(sides[m ^ (1 << high)][0], high), swap(sides[m ^ (1 << low)][1], low)]
    user_weights = after([sides[1 << bit][side] for bit, side in ahead], [user_weights])[0]
    user_acc, user_scaled = pl.pallas_call(
        functools.partial(user_kernel, suffix),
        out_shape=[
            pltpu.VMEM((user_rows, width), jnp.float32),
            pltpu.VMEM((levels, user_rows, width), jnp.bfloat16),
        ],
        in_specs=[vmem] * 4,
        out_specs=[vmem] * 2,
        compiler_params=params,
        cost_estimate=cost(0, 0),
    )(user_weights, user_queries, user_keys, user_values)

    totals = [pltpu.VMEM((token_count, width), jnp.float32), pltpu.VMEM((user_rows, width), jnp.float32)]

    def read(offsets, accs, ahead=()):
        groups = [tuple(offsets[i : i + 2]) for i in range(0, len(offsets), 2)]
        wide = len(ahead) * width
        extra = [pltpu.VMEM((rows, wide), jnp.bfloat16) for rows in (token_count, user_rows) if ahead]
        return pl.pallas_call(
            functools.partial(read_kernel, depth, suffix, groups, ahead),
            out_shape=totals + extra,
            in_specs=[vmem] * (5 + len(offsets)),
            out_specs=[vmem] * (2 + len(extra)),
            scratch_shapes=[pltpu.SMEM((user_count,), jnp.int32), pltpu.SemaphoreType.DMA(())],
            compiler_params=params,
            cost_estimate=cost(0, 0),
        )(lengths, slab_scaled, user_scaled, *accs, *[whole[m] for m in offsets])

    state = after(slab_weights, [state])[0]
    whole = {0: state, 1: swap(state, 0)}
    direct = [1 << bit for bit in outer]
    for m in direct:
        whole[m] = join(user_acc, sides[m])
        whole[m | 1] = swap(whole[m], 0)
    last = later[-1]
    *accs, slab_ahead, user_ahead = read([0, 1] + direct, (slab_acc, user_acc), (last, last | 1))
    for m in later:
        whole[m] = join(accs[0], sides[m])
        whole[m | 1] = swap(whole[m], 0)
    if later[:-1]:
        accs = read([n for m in later[:-1] for n in (m, m | 1)], accs)
    accs = read([m | 1 for m in direct], accs)
    slab_total, user_total, square = pl.pallas_call(
        last_kernel,
        out_shape=totals + [pltpu.VMEM((-(-lines // 8) * 8, ROWS), jnp.float32)],
        in_specs=[vmem] * 6,
        out_specs=[vmem] * 3,
        compiler_params=params,
        cost_estimate=cost(0, 0),
    )(slab_ahead, user_ahead, *accs, whole[last], whole[last | 1])

    mate = jnp.zeros_like(square)
    for bit in range(head_axis.bit_length() - 1):
        square = square + mate
        mate = lax.ppermute(square, "head", [(i, i ^ (1 << bit)) for i in range(head_axis)])

    slab_out, user_out = pl.pallas_call(
        functools.partial(norm_kernel, float(width * head_axis), chunks),
        out_shape=[bf16((token_count, width)), bf16((user_rows, width))],
        in_specs=[vmem] * 5,
        out_specs=[hbm] * 2,
        scratch_shapes=[
            pltpu.VMEM((token_count, width), jnp.bfloat16),
            pltpu.VMEM((user_rows, width), jnp.bfloat16),
            pltpu.SemaphoreType.DMA((lines, chunks)),
        ],
        compiler_params=params,
    )(slab_total, user_total, norm_gain.reshape(1, width), square, mate)
    return slab_out, user_out.reshape(user_count, suffix, width)


def solution(mesh):
    return jax.shard_map(
        local,
        mesh=mesh,
        in_specs=(
            P("seq", "head"),
            P("seq", "head"),
            P("seq", "head"),
            P(None, "head", "seq"),
            P("head"),
            P("seq", None, "head"),
            P("seq", None, "head"),
            P("seq", None, "head"),
            P("seq", None, "head", None),
            P("seq"),
        ),
        out_specs=(P("seq", "head"), P("seq", None, "head")),
        check_vma=False,
    )
```

```python
import functools

import jax
import jax.numpy as jnp
from jax import lax
from jax.experimental import pallas as pl
from jax.experimental.pallas import tpu as pltpu
from jax.sharding import PartitionSpec as P

HEADS = 64
HD = 128
ROWS = 128
VMEM_BYTES = 20 * 1024 * 1024


def matmul(a, b, contract):
    return lax.dot_general(a, b, (contract, ((), ())), preferred_element_type=jnp.float32)


def state_kernel(key_hbm, value_hbm, first_ref, second_ref, key_ref, value_ref, sems):
    half, width = first_ref.shape[0], key_ref.shape[2]
    parity = lax.axis_index("seq") & 1
    copies = []
    for part in range(2):
        cols = pl.ds(pl.multiple_of((parity ^ part) * width, width), width)
        for i, (source, target) in enumerate(((key_hbm, key_ref), (value_hbm, value_ref))):
            copies.append(pltpu.make_async_copy(source.at[:, cols], target.at[part], sems.at[i, part]))
            copies[-1].start()
    for part, out_ref in enumerate((first_ref, second_ref)):
        for copy in copies[2 * part : 2 * part + 2]:
            copy.wait()
        for head in range(half):
            cols = slice(head * HD, (head + 1) * HD)
            state = matmul(key_ref[part, :, cols], value_ref[part, :, cols], ((0,), (0,)))
            out_ref[head] = state.astype(jnp.bfloat16)


def join_kernel(order_ref, *refs):
    out_ref = refs[-1]
    parity = lax.axis_index("seq") & 1
    half = out_ref.shape[1] // 2
    for i in range(out_ref.shape[0]):
        for side in range(2):
            for head in range(half):
                out_ref[i, (side ^ parity) * half + head] = refs[2 * i + side][head]


def turned(offset, depth):
    return sum(((offset >> bit) & 1) << (depth - bit) for bit in range(1, depth))


def level_of(offset, target, position, depth):
    low = offset & 1
    block = position ^ low ^ jnp.where(((position ^ low) & 1) == 1, turned(offset, depth), offset - low)
    diff = block ^ target
    level = sum((diff >= (1 << step)).astype(jnp.int32) for step in range(depth))
    return jnp.where(block < target, level, 0)


def attend(mask, q_ref, k_ref, v_ref, w_ref, o_ref, parity=None):
    head_count = q_ref.shape[1] // HD
    half = head_count // 2

    def pick(ref, head, rows, cols):
        if parity is None:
            return ref[rows, cols]
        start = head % half * HD
        return ref[(head // half) ^ parity, rows, start : start + HD]

    step = 2
    for first in range(0, head_count, step):
        units = [
            (head, slice(head * HD, (head + 1) * HD), slice(start, start + ROWS))
            for head in range(first, first + step)
            for start in range(0, q_ref.shape[0], ROWS)
        ]
        scores = [matmul(q_ref[rows, cols], pick(k_ref, head, rows, cols), ((1,), (1,))) for head, cols, rows in units]
        scores = [jnp.where(mask, score, 0.0).astype(jnp.bfloat16) for score in scores]
        results = [
            matmul(score, pick(v_ref, head, rows, cols), ((1,), (0,))) for score, (head, cols, rows) in zip(scores, units)
        ]
        for result, (head, cols, rows) in zip(results, units):
            o_ref[rows, cols] = result * w_ref[rows, head : head + 1]


def causal_mask(suffix=ROWS):
    row = lax.broadcasted_iota(jnp.int32, (ROWS, ROWS), 0)
    col = lax.broadcasted_iota(jnp.int32, (ROWS, ROWS), 1)
    return jnp.logical_and(row >= col, row // suffix == col // suffix)


def start_copies(sources, targets, sems):
    copies = [
        pltpu.make_async_copy(source, target, sems.at[i]) for i, (source, target) in enumerate(zip(sources, targets))
    ]
    for copy in copies:
        copy.start()
    return copies


def load_kernel(suffix, *refs):
    sources, (k_ref, v_ref), halves, (sw_ref, uw_ref), rest = refs[:4], refs[4:6], refs[6:8], refs[8:10], refs[10:]
    loaded, o_ref, whole_ref, tables, sems = rest[:2], rest[2], rest[3], rest[4:6], rest[6]
    copies = start_copies(sources, (*tables, *loaded), sems)
    parity = lax.axis_index("seq") & 1
    half = halves[0].shape[0]
    for part, half_ref in enumerate(halves):
        for head in range(half):
            whole_ref[0, (part ^ parity) * half + head] = half_ref[head]
    slab_table, user_table = tables
    for copy in copies[:2]:
        copy.wait()
    columns = sw_ref.shape[1]
    row = lax.broadcasted_iota(jnp.int32, (slab_table.shape[0], columns), 0)
    col = lax.broadcasted_iota(jnp.int32, (slab_table.shape[0], columns), 1)
    same = jnp.where(row == col, 1.0, 0.0).astype(jnp.bfloat16)
    sw_ref[...] = matmul(slab_table[...], same, ((0,), (0,)))
    for user in range(user_table.shape[0]):
        uw_ref[user * suffix : (user + 1) * suffix] = matmul(user_table[user], same, ((0,), (0,)))
    for copy in copies[2:]:
        copy.wait()
    attend(causal_mask(), loaded[0], k_ref, v_ref, sw_ref, o_ref, parity)


def scale_queries(q_ref, w_ref, scaled_ref):
    head_count = q_ref.shape[1] // HD
    scaled_ref[0] = jnp.zeros_like(scaled_ref[0])
    for head in range(head_count):
        cols = slice(head * HD, (head + 1) * HD)
        query = q_ref[:, cols]
        for level in range(1, scaled_ref.shape[0]):
            column = level * head_count + head
            weight = jnp.broadcast_to(w_ref[:, column : column + 1], query.shape).astype(jnp.bfloat16)
            scaled_ref[level, :, cols] = query * weight


def scale_kernel(*refs):
    sources, (w_ref, q_ref), scaled_ref, loaded, sems = refs[:3], refs[3:5], refs[5], refs[6:9], refs[9]
    copies = start_copies(sources, loaded, sems)
    scale_queries(q_ref, w_ref, scaled_ref)
    for copy in copies:
        copy.wait()


def user_kernel(suffix, w_ref, q_ref, k_ref, v_ref, o_ref, scaled_ref):
    attend(causal_mask(suffix), q_ref, k_ref, v_ref, w_ref, o_ref)
    scale_queries(q_ref, w_ref, scaled_ref)


def read_kernel(depth, suffix, groups, ahead, length_ref, ss_ref, us_ref, sa_ref, ua_ref, *rest):
    offsets = [offset for group in groups for offset in group]
    states, outs, (lengths, sem) = rest[: len(offsets)], rest[len(offsets) : -2], rest[-2:]
    copy = pltpu.make_async_copy(length_ref, lengths, sem)
    copy.start()
    copy.wait()
    position = lax.axis_index("seq").astype(jnp.int32)
    head_count = sa_ref.shape[1] // HD
    users = range(ua_ref.shape[0] // suffix)
    targets = [lengths[user] for user in users]
    slab_level = {o: level_of(o, position, position, depth) for o in (*offsets, *ahead)}
    user_level = {o: [level_of(o, target, position, depth) for target in targets] for o in (*offsets, *ahead)}

    def slab_rows(offset, cols):
        return ss_ref[slab_level[offset], :, cols]

    def user_rows(offset, cols):
        parts = [us_ref[user_level[offset][user], user * suffix : (user + 1) * suffix, cols] for user in users]
        return jnp.concatenate(parts, axis=0)

    for head in range(head_count):
        cols = slice(head * HD, (head + 1) * HD)
        for pick, a_ref, t_ref in ((slab_rows, sa_ref, outs[0]), (user_rows, ua_ref, outs[1])):
            total = a_ref[:, cols]
            for group in groups:
                queries = jnp.concatenate([pick(offset, cols) for offset in group], axis=1)
                blocks = jnp.concatenate([states[offsets.index(offset)][0, head] for offset in group], axis=0)
                total = total + matmul(queries, blocks, ((1,), (0,)))
            t_ref[:, cols] = total
        for pick, out_ref in zip((slab_rows, user_rows), outs[2:]):
            for i, offset in enumerate(ahead):
                start = (head * len(ahead) + i) * HD
                out_ref[:, start : start + HD] = pick(offset, cols)


def last_kernel(ss_ref, us_ref, sa_ref, ua_ref, state_ref, mate_ref, st_ref, ut_ref, square_ref):
    head_count = sa_ref.shape[1] // HD
    square_ref[...] = jnp.zeros_like(square_ref)
    line = 0
    for q_ref, a_ref, t_ref in ((ss_ref, sa_ref, st_ref), (us_ref, ua_ref, ut_ref)):
        for start in range(0, a_ref.shape[0], ROWS):
            rows = slice(start, start + ROWS)
            squares = None
            for head in range(head_count):
                cols = slice(head * HD, (head + 1) * HD)
                wide = slice(2 * head * HD, 2 * (head + 1) * HD)
                states = jnp.concatenate([state_ref[0, head], mate_ref[0, head]], axis=0)
                total = a_ref[rows, cols] + matmul(q_ref[rows, wide], states, ((1,), (0,)))
                t_ref[rows, cols] = total
                squares = total * total if squares is None else squares + total * total
            square_ref[line : line + 1] = jnp.sum(jnp.transpose(squares), axis=0, keepdims=True)
            line += 1


def norm_kernel(features, chunks, st_ref, ut_ref, gain_ref, one_ref, two_ref, so_hbm, uo_hbm, so_ref, uo_ref, sems):
    square = one_ref[...] + two_ref[...]
    scale = lax.rsqrt(square / features + 1e-06)
    size = st_ref.shape[1] // chunks
    copies = []
    line = 0
    for t_ref, o_ref, o_hbm in ((st_ref, so_ref, so_hbm), (ut_ref, uo_ref, uo_hbm)):
        for start in range(0, t_ref.shape[0], ROWS):
            rows = slice(start, start + ROWS)
            factor = jnp.transpose(jnp.broadcast_to(scale[line : line + 1], (ROWS, ROWS)))
            for chunk in range(chunks):
                for low in range(chunk * size, (chunk + 1) * size, HD):
                    cols = slice(low, low + HD)
                    gain = gain_ref[:, cols].astype(jnp.float32)
                    o_ref[rows, cols] = (t_ref[rows, cols] * factor * gain).astype(jnp.bfloat16)
                part = (pl.ds(start, ROWS), pl.ds(chunk * size, size))
                copies.append(pltpu.make_async_copy(o_ref.at[part], o_hbm.at[part], sems.at[line, chunk]))
                copies[-1].start()
            line += 1
    for copy in copies:
        copy.wait()


def local(
    slab_query,
    slab_key,
    slab_value,
    slab_levels,
    norm_gain,
    user_query,
    user_key,
    user_value,
    user_levels,
    prefix_lengths,
):
    seq_count = lax.axis_size("seq")
    head_axis = lax.axis_size("head")
    depth = seq_count.bit_length() - 1
    token_count, width = slab_query.shape
    head_count = width // HD
    half = head_count // 2
    user_count, suffix = user_query.shape[:2]
    user_rows = user_count * suffix
    lines = (token_count + user_rows) // ROWS
    params = pltpu.CompilerParams(vmem_limit_bytes=VMEM_BYTES)
    bf16 = functools.partial(jax.ShapeDtypeStruct, dtype=jnp.bfloat16)
    vmem = pl.BlockSpec(memory_space=pltpu.VMEM)
    anywhere = pl.BlockSpec(memory_space=pl.ANY)
    hbm = pl.BlockSpec(memory_space=pltpu.HBM)
    chunks = min(4, half)
    rows_cost = 2 * width * (token_count + user_rows)

    def pinned(*arrays):
        return [pltpu.with_memory_space_constraint(array, pltpu.HBM) for array in arrays]

    def cost(flops, moved):
        return pl.CostEstimate(flops=flops, bytes_accessed=moved, transcendentals=0)

    def swap(value, bit):
        other = depth - bit if bit else 0
        return lax.ppermute(value, "seq", [(i, i ^ (1 << (other if i & 1 else bit))) for i in range(seq_count)])

    def after(results, values):
        return list(lax.optimization_barrier((results, values))[1])

    def join(order, halves):
        return pl.pallas_call(
            join_kernel,
            out_shape=pltpu.VMEM((len(halves) // 2, head_count, HD, HD), jnp.bfloat16),
            in_specs=[anywhere] + [vmem] * len(halves),
            out_specs=vmem,
            compiler_params=params,
        )(order, *halves)

    half_state = pltpu.VMEM((half, HD, HD), jnp.bfloat16)
    slab_rows = pltpu.VMEM((token_count, width), jnp.bfloat16)
    half_rows = pltpu.VMEM((2, token_count, width // 2), jnp.bfloat16)
    first, second, slab_keys, slab_values = pl.pallas_call(
        state_kernel,
        out_shape=[half_state, half_state, half_rows, half_rows],
        in_specs=[hbm] * 2,
        out_specs=[vmem] * 4,
        scratch_shapes=[pltpu.SemaphoreType.DMA((2, 2))],
        compiler_params=params,
    )(*pinned(slab_key, slab_value))
    halves = [first, second]

    outer = list(range(1, depth))
    places = [(bit, side) for bit in outer for side in range(2)]
    ahead = [(bit, 0) for bit in outer[:-1]] + [(bit, 1) for bit in outer[1:]] or places
    sides = {1 << bit: [None, None] for bit in outer}
    for bit, side in ahead:
        sides[1 << bit][side] = swap(halves[side], bit)
    levels = depth + 1
    slab_table = slab_levels.reshape(-1, token_count)
    user_table = user_levels.reshape(user_count, -1, suffix)
    user_array = pltpu.VMEM((user_rows, width), jnp.bfloat16)
    slab_weights, user_weights, slab_queries, lengths, slab_acc, state = pl.pallas_call(
        functools.partial(load_kernel, suffix),
        out_shape=[
            pltpu.VMEM((token_count, levels * head_count), jnp.float32),
            pltpu.VMEM((user_rows, levels * head_count), jnp.float32),
            slab_rows,
            pltpu.VMEM((user_count,), jnp.int32),
            pltpu.VMEM((token_count, width), jnp.float32),
            pltpu.VMEM((1, head_count, HD, HD), jnp.bfloat16),
        ],
        in_specs=[hbm] * 4 + [vmem] * 4,
        out_specs=[vmem] * 6,
        scratch_shapes=[
            pltpu.VMEM(slab_table.shape, jnp.bfloat16),
            pltpu.VMEM(user_table.shape, jnp.bfloat16),
            pltpu.SemaphoreType.DMA((4,)),
        ],
        compiler_params=params,
        cost_estimate=cost(0, 0),
    )(*pinned(slab_table, user_table, slab_query, prefix_lengths), slab_keys, slab_values, first, second)
    halves = after(slab_weights, halves)
    for bit, side in places:
        if (bit, side) not in ahead:
            sides[1 << bit][side] = swap(halves[side], bit)
    slab_scaled, user_queries, user_keys, user_values = pl.pallas_call(
        scale_kernel,
        out_shape=[pltpu.VMEM((levels, token_count, width), jnp.bfloat16)] + [user_array] * 3,
        in_specs=[hbm] * 3 + [vmem] * 2,
        out_specs=[vmem] * 4,
        scratch_shapes=[pltpu.SemaphoreType.DMA((3,))],
        compiler_params=params,
        cost_estimate=cost(0, 0),
    )(
        *pinned(*[array.reshape(user_rows, width) for array in (user_query, user_key, user_value)]),
        slab_weights,
        slab_queries,
    )

    later = sorted((m for m in range(0, seq_count, 2) if m.bit_count() > 1), key=lambda m: m.bit_count())
    for (bit, side), value in zip(ahead, after(slab_scaled, [sides[1 << bit][side] for bit, side in ahead])):
        sides[1 << bit][side] = value
    for m in later:
        high, low = m.bit_length() - 1, (m & -m).bit_length() - 1
        sides[m] = [swap(sides[m ^ (1 << high)][0], high), swap(sides[m ^ (1 << low)][1], low)]
    user_weights = after([sides[1 << bit][side] for bit, side in ahead], [user_weights])[0]
    user_acc, user_scaled = pl.pallas_call(
        functools.partial(user_kernel, suffix),
        out_shape=[
            pltpu.VMEM((user_rows, width), jnp.float32),
            pltpu.VMEM((levels, user_rows, width), jnp.bfloat16),
        ],
        in_specs=[vmem] * 4,
        out_specs=[vmem] * 2,
        compiler_params=params,
        cost_estimate=cost(0, 0),
    )(user_weights, user_queries, user_keys, user_values)

    totals = [pltpu.VMEM((token_count, width), jnp.float32), pltpu.VMEM((user_rows, width), jnp.float32)]

    def read(offsets, accs, ahead=()):
        groups = [tuple(offsets[i : i + 2]) for i in range(0, len(offsets), 2)]
        wide = len(ahead) * width
        extra = [pltpu.VMEM((rows, wide), jnp.bfloat16) for rows in (token_count, user_rows) if ahead]
        return pl.pallas_call(
            functools.partial(read_kernel, depth, suffix, groups, ahead),
            out_shape=totals + extra,
            in_specs=[vmem] * (5 + len(offsets)),
            out_specs=[vmem] * (2 + len(extra)),
            scratch_shapes=[pltpu.SMEM((user_count,), jnp.int32), pltpu.SemaphoreType.DMA(())],
            compiler_params=params,
            cost_estimate=cost(0, 0),
        )(lengths, slab_scaled, user_scaled, *accs, *[whole[m] for m in offsets])

    whole = {0: state, 1: swap(state, 0)}
    direct = [1 << bit for bit in outer]
    for m in direct:
        whole[m] = join(user_acc, sides[m])
        whole[m | 1] = swap(whole[m], 0)
    last = later[-1]
    *accs, slab_ahead, user_ahead = read([0, 1] + direct, (slab_acc, user_acc), (last, last | 1))
    for m in later:
        whole[m] = join(accs[0], sides[m])
        whole[m | 1] = swap(whole[m], 0)
    if later[:-1]:
        accs = read([n for m in later[:-1] for n in (m, m | 1)], accs)
    accs = read([m | 1 for m in direct], accs)
    slab_total, user_total, square = pl.pallas_call(
        last_kernel,
        out_shape=totals + [pltpu.VMEM((-(-lines // 8) * 8, ROWS), jnp.float32)],
        in_specs=[vmem] * 6,
        out_specs=[vmem] * 3,
        compiler_params=params,
        cost_estimate=cost(0, 0),
    )(slab_ahead, user_ahead, *accs, whole[last], whole[last | 1])

    mate = jnp.zeros_like(square)
    for bit in range(head_axis.bit_length() - 1):
        square = square + mate
        mate = lax.ppermute(square, "head", [(i, i ^ (1 << bit)) for i in range(head_axis)])

    slab_out, user_out = pl.pallas_call(
        functools.partial(norm_kernel, float(width * head_axis), chunks),
        out_shape=[bf16((token_count, width)), bf16((user_rows, width))],
        in_specs=[vmem] * 5,
        out_specs=[hbm] * 2,
        scratch_shapes=[
            pltpu.VMEM((token_count, width), jnp.bfloat16),
            pltpu.VMEM((user_rows, width), jnp.bfloat16),
            pltpu.SemaphoreType.DMA((lines, chunks)),
        ],
        compiler_params=params,
    )(slab_total, user_total, norm_gain.reshape(1, width), square, mate)
    return slab_out, user_out.reshape(user_count, suffix, width)


def solution(mesh):
    return jax.shard_map(
        local,
        mesh=mesh,
        in_specs=(
            P("seq", "head"),
            P("seq", "head"),
            P("seq", "head"),
            P(None, "head", "seq"),
            P("head"),
            P("seq", None, "head"),
            P("seq", None, "head"),
            P("seq", None, "head"),
            P("seq", None, "head", None),
            P("seq"),
        ),
        out_specs=(P("seq", "head"), P("seq", None, "head")),
        check_vma=False,
    )
```

```python
import functools

import jax
import jax.numpy as jnp
from jax import lax
from jax.experimental import pallas as pl
from jax.experimental.pallas import tpu as pltpu
from jax.sharding import PartitionSpec as P

HEADS = 64
HD = 128
ROWS = 128
VMEM_BYTES = 20 * 1024 * 1024


def matmul(a, b, contract):
    return lax.dot_general(a, b, (contract, ((), ())), preferred_element_type=jnp.float32)


def state_kernel(key_hbm, value_hbm, first_ref, second_ref, key_ref, value_ref, sems):
    half, width = first_ref.shape[0], key_ref.shape[2]
    parity = lax.axis_index("seq") & 1
    copies = []
    for part in range(2):
        cols = pl.ds(pl.multiple_of((parity ^ part) * width, width), width)
        for i, (source, target) in enumerate(((key_hbm, key_ref), (value_hbm, value_ref))):
            copies.append(pltpu.make_async_copy(source.at[:, cols], target.at[part], sems.at[i, part]))
            copies[-1].start()
    for part, out_ref in enumerate((first_ref, second_ref)):
        for copy in copies[2 * part : 2 * part + 2]:
            copy.wait()
        for head in range(half):
            cols = slice(head * HD, (head + 1) * HD)
            state = matmul(key_ref[part, :, cols], value_ref[part, :, cols], ((0,), (0,)))
            out_ref[head] = state.astype(jnp.bfloat16)


def join_kernel(order_ref, *refs):
    out_ref = refs[-1]
    parity = lax.axis_index("seq") & 1
    half = out_ref.shape[1] // 2
    for i in range(out_ref.shape[0]):
        for side in range(2):
            for head in range(half):
                out_ref[i, (side ^ parity) * half + head] = refs[2 * i + side][head]


def turned(offset, depth):
    return sum(((offset >> bit) & 1) << (depth - bit) for bit in range(1, depth))


def level_of(offset, target, position, depth):
    low = offset & 1
    block = position ^ low ^ jnp.where(((position ^ low) & 1) == 1, turned(offset, depth), offset - low)
    diff = block ^ target
    level = sum((diff >= (1 << step)).astype(jnp.int32) for step in range(depth))
    return jnp.where(block < target, level, 0)


def attend(mask, q_ref, k_ref, v_ref, w_ref, o_ref, parity=None):
    head_count = q_ref.shape[1] // HD
    half = head_count // 2

    def pick(ref, head, rows, cols):
        if parity is None:
            return ref[rows, cols]
        start = head % half * HD
        return ref[(head // half) ^ parity, rows, start : start + HD]

    step = 2
    for first in range(0, head_count, step):
        units = [
            (head, slice(head * HD, (head + 1) * HD), slice(start, start + ROWS))
            for head in range(first, first + step)
            for start in range(0, q_ref.shape[0], ROWS)
        ]
        scores = [matmul(q_ref[rows, cols], pick(k_ref, head, rows, cols), ((1,), (1,))) for head, cols, rows in units]
        scores = [jnp.where(mask, score, 0.0).astype(jnp.bfloat16) for score in scores]
        results = [
            matmul(score, pick(v_ref, head, rows, cols), ((1,), (0,))) for score, (head, cols, rows) in zip(scores, units)
        ]
        for result, (head, cols, rows) in zip(results, units):
            o_ref[rows, cols] = result * w_ref[rows, head : head + 1]


def causal_mask(suffix=ROWS):
    row = lax.broadcasted_iota(jnp.int32, (ROWS, ROWS), 0)
    col = lax.broadcasted_iota(jnp.int32, (ROWS, ROWS), 1)
    return jnp.logical_and(row >= col, row // suffix == col // suffix)


def start_copies(sources, targets, sems):
    copies = [
        pltpu.make_async_copy(source, target, sems.at[i]) for i, (source, target) in enumerate(zip(sources, targets))
    ]
    for copy in copies:
        copy.start()
    return copies


def load_kernel(suffix, *refs):
    sources, (k_ref, v_ref), halves, (sw_ref, uw_ref), rest = refs[:4], refs[4:6], refs[6:8], refs[8:10], refs[10:]
    loaded, o_ref, whole_ref, tables, sems = rest[:2], rest[2], rest[3], rest[4:6], rest[6]
    copies = start_copies(sources, (*tables, *loaded), sems)
    parity = lax.axis_index("seq") & 1
    half = halves[0].shape[0]
    for part, half_ref in enumerate(halves):
        for head in range(half):
            whole_ref[0, (part ^ parity) * half + head] = half_ref[head]
    slab_table, user_table = tables
    for copy in copies[:2]:
        copy.wait()
    columns = sw_ref.shape[1]
    row = lax.broadcasted_iota(jnp.int32, (slab_table.shape[0], columns), 0)
    col = lax.broadcasted_iota(jnp.int32, (slab_table.shape[0], columns), 1)
    same = jnp.where(row == col, 1.0, 0.0).astype(jnp.bfloat16)
    sw_ref[...] = matmul(slab_table[...], same, ((0,), (0,)))
    for user in range(user_table.shape[0]):
        uw_ref[user * suffix : (user + 1) * suffix] = matmul(user_table[user], same, ((0,), (0,)))
    for copy in copies[2:]:
        copy.wait()
    attend(causal_mask(), loaded[0], k_ref, v_ref, sw_ref, o_ref, parity)


def scale_queries(q_ref, w_ref, scaled_ref):
    head_count = q_ref.shape[1] // HD
    scaled_ref[0] = jnp.zeros_like(scaled_ref[0])
    for head in range(head_count):
        cols = slice(head * HD, (head + 1) * HD)
        query = q_ref[:, cols]
        for level in range(1, scaled_ref.shape[0]):
            column = level * head_count + head
            weight = jnp.broadcast_to(w_ref[:, column : column + 1], query.shape).astype(jnp.bfloat16)
            scaled_ref[level, :, cols] = query * weight


def scale_kernel(*refs):
    sources, (w_ref, q_ref), scaled_ref, loaded, sems = refs[:3], refs[3:5], refs[5], refs[6:9], refs[9]
    copies = start_copies(sources, loaded, sems)
    scale_queries(q_ref, w_ref, scaled_ref)
    for copy in copies:
        copy.wait()


def user_kernel(suffix, w_ref, q_ref, k_ref, v_ref, o_ref, scaled_ref):
    attend(causal_mask(suffix), q_ref, k_ref, v_ref, w_ref, o_ref)
    scale_queries(q_ref, w_ref, scaled_ref)


def read_kernel(depth, suffix, groups, ahead, length_ref, ss_ref, us_ref, sa_ref, ua_ref, *rest):
    offsets = [offset for group in groups for offset in group]
    states, outs, (lengths, sem) = rest[: len(offsets)], rest[len(offsets) : -2], rest[-2:]
    copy = pltpu.make_async_copy(length_ref, lengths, sem)
    copy.start()
    copy.wait()
    position = lax.axis_index("seq").astype(jnp.int32)
    head_count = sa_ref.shape[1] // HD
    users = range(ua_ref.shape[0] // suffix)
    targets = [lengths[user] for user in users]
    slab_level = {o: level_of(o, position, position, depth) for o in (*offsets, *ahead)}
    user_level = {o: [level_of(o, target, position, depth) for target in targets] for o in (*offsets, *ahead)}

    def slab_rows(offset, cols):
        return ss_ref[slab_level[offset], :, cols]

    def user_rows(offset, cols):
        parts = [us_ref[user_level[offset][user], user * suffix : (user + 1) * suffix, cols] for user in users]
        return jnp.concatenate(parts, axis=0)

    for head in range(head_count):
        cols = slice(head * HD, (head + 1) * HD)
        for pick, a_ref, t_ref in ((slab_rows, sa_ref, outs[0]), (user_rows, ua_ref, outs[1])):
            total = a_ref[:, cols]
            for group in groups:
                queries = jnp.concatenate([pick(offset, cols) for offset in group], axis=1)
                blocks = jnp.concatenate([states[offsets.index(offset)][0, head] for offset in group], axis=0)
                total = total + matmul(queries, blocks, ((1,), (0,)))
            t_ref[:, cols] = total
        for pick, out_ref in zip((slab_rows, user_rows), outs[2:]):
            for i, offset in enumerate(ahead):
                start = (head * len(ahead) + i) * HD
                out_ref[:, start : start + HD] = pick(offset, cols)


def last_kernel(ss_ref, us_ref, sa_ref, ua_ref, state_ref, mate_ref, st_ref, ut_ref, square_ref):
    head_count = sa_ref.shape[1] // HD
    square_ref[...] = jnp.zeros_like(square_ref)
    line = 0
    for q_ref, a_ref, t_ref in ((ss_ref, sa_ref, st_ref), (us_ref, ua_ref, ut_ref)):
        for start in range(0, a_ref.shape[0], ROWS):
            rows = slice(start, start + ROWS)
            squares = None
            for head in range(head_count):
                cols = slice(head * HD, (head + 1) * HD)
                wide = slice(2 * head * HD, 2 * (head + 1) * HD)
                states = jnp.concatenate([state_ref[0, head], mate_ref[0, head]], axis=0)
                total = a_ref[rows, cols] + matmul(q_ref[rows, wide], states, ((1,), (0,)))
                t_ref[rows, cols] = total
                squares = total * total if squares is None else squares + total * total
            square_ref[line : line + 1] = jnp.sum(jnp.transpose(squares), axis=0, keepdims=True)
            line += 1


def norm_kernel(features, chunks, st_ref, ut_ref, gain_ref, *rest):
    squares, (so_hbm, uo_hbm, so_ref, uo_ref, sems) = rest[:-5], rest[-5:]
    square = squares[0][...]
    for part_ref in squares[1:]:
        square = square + part_ref[...]
    scale = lax.rsqrt(square / features + 1e-06)
    size = st_ref.shape[1] // chunks
    copies = []
    line = 0
    for t_ref, o_ref, o_hbm in ((st_ref, so_ref, so_hbm), (ut_ref, uo_ref, uo_hbm)):
        for start in range(0, t_ref.shape[0], ROWS):
            rows = slice(start, start + ROWS)
            factor = jnp.transpose(jnp.broadcast_to(scale[line : line + 1], (ROWS, ROWS)))
            for chunk in range(chunks):
                for low in range(chunk * size, (chunk + 1) * size, HD):
                    cols = slice(low, low + HD)
                    gain = gain_ref[:, cols].astype(jnp.float32)
                    o_ref[rows, cols] = (t_ref[rows, cols] * factor * gain).astype(jnp.bfloat16)
                part = (pl.ds(start, ROWS), pl.ds(chunk * size, size))
                copies.append(pltpu.make_async_copy(o_ref.at[part], o_hbm.at[part], sems.at[line, chunk]))
                copies[-1].start()
            line += 1
    for copy in copies:
        copy.wait()


def local(
    slab_query,
    slab_key,
    slab_value,
    slab_levels,
    norm_gain,
    user_query,
    user_key,
    user_value,
    user_levels,
    prefix_lengths,
):
    seq_count = lax.axis_size("seq")
    head_axis = lax.axis_size("head")
    depth = seq_count.bit_length() - 1
    token_count, width = slab_query.shape
    head_count = width // HD
    half = head_count // 2
    user_count, suffix = user_query.shape[:2]
    user_rows = user_count * suffix
    lines = (token_count + user_rows) // ROWS
    params = pltpu.CompilerParams(vmem_limit_bytes=VMEM_BYTES)
    bf16 = functools.partial(jax.ShapeDtypeStruct, dtype=jnp.bfloat16)
    vmem = pl.BlockSpec(memory_space=pltpu.VMEM)
    anywhere = pl.BlockSpec(memory_space=pl.ANY)
    hbm = pl.BlockSpec(memory_space=pltpu.HBM)
    chunks = min(4, half)
    rows_cost = 2 * width * (token_count + user_rows)

    def pinned(*arrays):
        return [pltpu.with_memory_space_constraint(array, pltpu.HBM) for array in arrays]

    def cost(flops, moved):
        return pl.CostEstimate(flops=flops, bytes_accessed=moved, transcendentals=0)

    def swap(value, bit):
        other = depth - bit if bit else 0
        return lax.ppermute(value, "seq", [(i, i ^ (1 << (other if i & 1 else bit))) for i in range(seq_count)])

    def after(results, values):
        return list(lax.optimization_barrier((results, values))[1])

    def join(order, halves):
        return pl.pallas_call(
            join_kernel,
            out_shape=pltpu.VMEM((len(halves) // 2, head_count, HD, HD), jnp.bfloat16),
            in_specs=[anywhere] + [vmem] * len(halves),
            out_specs=vmem,
            compiler_params=params,
        )(order, *halves)

    half_state = pltpu.VMEM((half, HD, HD), jnp.bfloat16)
    slab_rows = pltpu.VMEM((token_count, width), jnp.bfloat16)
    half_rows = pltpu.VMEM((2, token_count, width // 2), jnp.bfloat16)
    first, second, slab_keys, slab_values = pl.pallas_call(
        state_kernel,
        out_shape=[half_state, half_state, half_rows, half_rows],
        in_specs=[hbm] * 2,
        out_specs=[vmem] * 4,
        scratch_shapes=[pltpu.SemaphoreType.DMA((2, 2))],
        compiler_params=params,
    )(*pinned(slab_key, slab_value))
    halves = [first, second]

    outer = list(range(1, depth))
    places = [(bit, side) for bit in outer for side in range(2)]
    ahead = [(bit, 0) for bit in outer[:-1]] + [(bit, 1) for bit in outer[1:]] or places
    sides = {1 << bit: [None, None] for bit in outer}
    for bit, side in ahead:
        sides[1 << bit][side] = swap(halves[side], bit)
    levels = depth + 1
    slab_table = slab_levels.reshape(-1, token_count)
    user_table = user_levels.reshape(user_count, -1, suffix)
    user_array = pltpu.VMEM((user_rows, width), jnp.bfloat16)
    slab_weights, user_weights, slab_queries, lengths, slab_acc, state = pl.pallas_call(
        functools.partial(load_kernel, suffix),
        out_shape=[
            pltpu.VMEM((token_count, levels * head_count), jnp.float32),
            pltpu.VMEM((user_rows, levels * head_count), jnp.float32),
            slab_rows,
            pltpu.VMEM((user_count,), jnp.int32),
            pltpu.VMEM((token_count, width), jnp.float32),
            pltpu.VMEM((1, head_count, HD, HD), jnp.bfloat16),
        ],
        in_specs=[hbm] * 4 + [vmem] * 4,
        out_specs=[vmem] * 6,
        scratch_shapes=[
            pltpu.VMEM(slab_table.shape, jnp.bfloat16),
            pltpu.VMEM(user_table.shape, jnp.bfloat16),
            pltpu.SemaphoreType.DMA((4,)),
        ],
        compiler_params=params,
        cost_estimate=cost(0, 0),
    )(*pinned(slab_table, user_table, slab_query, prefix_lengths), slab_keys, slab_values, first, second)
    halves = after(slab_weights, halves)
    for bit, side in places:
        if (bit, side) not in ahead:
            sides[1 << bit][side] = swap(halves[side], bit)
    slab_scaled, user_queries, user_keys, user_values = pl.pallas_call(
        scale_kernel,
        out_shape=[pltpu.VMEM((levels, token_count, width), jnp.bfloat16)] + [user_array] * 3,
        in_specs=[hbm] * 3 + [vmem] * 2,
        out_specs=[vmem] * 4,
        scratch_shapes=[pltpu.SemaphoreType.DMA((3,))],
        compiler_params=params,
        cost_estimate=cost(0, 0),
    )(
        *pinned(*[array.reshape(user_rows, width) for array in (user_query, user_key, user_value)]),
        slab_weights,
        slab_queries,
    )

    later = sorted((m for m in range(0, seq_count, 2) if m.bit_count() > 1), key=lambda m: m.bit_count())
    for (bit, side), value in zip(ahead, after(slab_scaled, [sides[1 << bit][side] for bit, side in ahead])):
        sides[1 << bit][side] = value
    for m in later:
        high, low = m.bit_length() - 1, (m & -m).bit_length() - 1
        sides[m] = [swap(sides[m ^ (1 << high)][0], high), swap(sides[m ^ (1 << low)][1], low)]
    user_weights = after([sides[1 << bit][side] for bit, side in ahead], [user_weights])[0]
    user_acc, user_scaled = pl.pallas_call(
        functools.partial(user_kernel, suffix),
        out_shape=[
            pltpu.VMEM((user_rows, width), jnp.float32),
            pltpu.VMEM((levels, user_rows, width), jnp.bfloat16),
        ],
        in_specs=[vmem] * 4,
        out_specs=[vmem] * 2,
        compiler_params=params,
        cost_estimate=cost(0, 0),
    )(user_weights, user_queries, user_keys, user_values)

    totals = [pltpu.VMEM((token_count, width), jnp.float32), pltpu.VMEM((user_rows, width), jnp.float32)]

    def read(offsets, accs, ahead=()):
        groups = [tuple(offsets[i : i + 2]) for i in range(0, len(offsets), 2)]
        wide = len(ahead) * width
        extra = [pltpu.VMEM((rows, wide), jnp.bfloat16) for rows in (token_count, user_rows) if ahead]
        return pl.pallas_call(
            functools.partial(read_kernel, depth, suffix, groups, ahead),
            out_shape=totals + extra,
            in_specs=[vmem] * (5 + len(offsets)),
            out_specs=[vmem] * (2 + len(extra)),
            scratch_shapes=[pltpu.SMEM((user_count,), jnp.int32), pltpu.SemaphoreType.DMA(())],
            compiler_params=params,
            cost_estimate=cost(0, 0),
        )(lengths, slab_scaled, user_scaled, *accs, *[whole[m] for m in offsets])

    whole = {0: state, 1: swap(state, 0)}
    direct = [1 << bit for bit in outer]
    for m in direct:
        whole[m] = join(user_acc, sides[m])
        whole[m | 1] = swap(whole[m], 0)
    last = later[-1]
    *accs, slab_ahead, user_ahead = read([0, 1] + direct, (slab_acc, user_acc), (last, last | 1))
    for m in later:
        whole[m] = join(accs[0], sides[m])
        whole[m | 1] = swap(whole[m], 0)
    if later[:-1]:
        accs = read([n for m in later[:-1] for n in (m, m | 1)], accs)
    accs = read([m | 1 for m in direct], accs)
    slab_total, user_total, square = pl.pallas_call(
        last_kernel,
        out_shape=totals + [pltpu.VMEM((-(-lines // 8) * 8, ROWS), jnp.float32)],
        in_specs=[vmem] * 6,
        out_specs=[vmem] * 3,
        compiler_params=params,
        cost_estimate=cost(0, 0),
    )(slab_ahead, user_ahead, *accs, whole[last], whole[last | 1])

    squares = [square]
    for shift in range(1, head_axis):
        squares.append(lax.ppermute(square, "head", [(i, (i + shift) % head_axis) for i in range(head_axis)]))

    slab_out, user_out = pl.pallas_call(
        functools.partial(norm_kernel, float(width * head_axis), chunks),
        out_shape=[bf16((token_count, width)), bf16((user_rows, width))],
        in_specs=[vmem] * (3 + head_axis),
        out_specs=[hbm] * 2,
        scratch_shapes=[
            pltpu.VMEM((token_count, width), jnp.bfloat16),
            pltpu.VMEM((user_rows, width), jnp.bfloat16),
            pltpu.SemaphoreType.DMA((lines, chunks)),
        ],
        compiler_params=params,
    )(slab_total, user_total, norm_gain.reshape(1, width), *squares)
    return slab_out, user_out.reshape(user_count, suffix, width)


def solution(mesh):
    return jax.shard_map(
        local,
        mesh=mesh,
        in_specs=(
            P("seq", "head"),
            P("seq", "head"),
            P("seq", "head"),
            P(None, "head", "seq"),
            P("head"),
            P("seq", None, "head"),
            P("seq", None, "head"),
            P("seq", None, "head"),
            P("seq", None, "head", None),
            P("seq"),
        ),
        out_specs=(P("seq", "head"), P("seq", None, "head")),
        check_vma=False,
    )
```

```python
import functools

import jax
import jax.numpy as jnp
from jax import lax
from jax.experimental import pallas as pl
from jax.experimental.pallas import tpu as pltpu
from jax.sharding import PartitionSpec as P

HEADS = 64
HD = 128
ROWS = 128
VMEM_BYTES = 20 * 1024 * 1024


def matmul(a, b, contract):
    return lax.dot_general(a, b, (contract, ((), ())), preferred_element_type=jnp.float32)


def state_kernel(key_hbm, value_hbm, first_ref, second_ref, key_ref, value_ref, sems):
    half, width = first_ref.shape[0], key_ref.shape[2]
    parity = lax.axis_index("seq") & 1
    copies = []
    for part in range(2):
        cols = pl.ds(pl.multiple_of((parity ^ part) * width, width), width)
        for i, (source, target) in enumerate(((key_hbm, key_ref), (value_hbm, value_ref))):
            copies.append(pltpu.make_async_copy(source.at[:, cols], target.at[part], sems.at[i, part]))
            copies[-1].start()
    for part, out_ref in enumerate((first_ref, second_ref)):
        for copy in copies[2 * part : 2 * part + 2]:
            copy.wait()
        for head in range(half):
            cols = slice(head * HD, (head + 1) * HD)
            state = matmul(key_ref[part, :, cols], value_ref[part, :, cols], ((0,), (0,)))
            out_ref[head] = state.astype(jnp.bfloat16)


def join_kernel(order_ref, *refs):
    out_ref = refs[-1]
    parity = lax.axis_index("seq") & 1
    half = out_ref.shape[1] // 2
    for i in range(out_ref.shape[0]):
        for side in range(2):
            for head in range(half):
                out_ref[i, (side ^ parity) * half + head] = refs[2 * i + side][head]


def turned(offset, depth):
    return sum(((offset >> bit) & 1) << (depth - bit) for bit in range(1, depth))


def level_of(offset, target, position, depth):
    low = offset & 1
    block = position ^ low ^ jnp.where(((position ^ low) & 1) == 1, turned(offset, depth), offset - low)
    diff = block ^ target
    level = sum((diff >= (1 << step)).astype(jnp.int32) for step in range(depth))
    return jnp.where(block < target, level, 0)


def attend(mask, q_ref, k_ref, v_ref, w_ref, o_ref, parity=None):
    head_count = q_ref.shape[1] // HD
    half = head_count // 2

    def pick(ref, head, rows, cols):
        if parity is None:
            return ref[rows, cols]
        start = head % half * HD
        return ref[(head // half) ^ parity, rows, start : start + HD]

    step = 2
    for first in range(0, head_count, step):
        units = [
            (head, slice(head * HD, (head + 1) * HD), slice(start, start + ROWS))
            for head in range(first, first + step)
            for start in range(0, q_ref.shape[0], ROWS)
        ]
        scores = [matmul(q_ref[rows, cols], pick(k_ref, head, rows, cols), ((1,), (1,))) for head, cols, rows in units]
        scores = [jnp.where(mask, score, 0.0).astype(jnp.bfloat16) for score in scores]
        results = [
            matmul(score, pick(v_ref, head, rows, cols), ((1,), (0,))) for score, (head, cols, rows) in zip(scores, units)
        ]
        for result, (head, cols, rows) in zip(results, units):
            o_ref[rows, cols] = result * w_ref[rows, head : head + 1]


def causal_mask(suffix=ROWS):
    row = lax.broadcasted_iota(jnp.int32, (ROWS, ROWS), 0)
    col = lax.broadcasted_iota(jnp.int32, (ROWS, ROWS), 1)
    return jnp.logical_and(row >= col, row // suffix == col // suffix)


def start_copies(sources, targets, sems):
    copies = [
        pltpu.make_async_copy(source, target, sems.at[i]) for i, (source, target) in enumerate(zip(sources, targets))
    ]
    for copy in copies:
        copy.start()
    return copies


def load_kernel(suffix, *refs):
    sources, (k_ref, v_ref), halves, (sw_ref, uw_ref), rest = refs[:4], refs[4:6], refs[6:8], refs[8:10], refs[10:]
    loaded, o_ref, whole_ref, tables, sems = rest[:2], rest[2], rest[3], rest[4:6], rest[6]
    copies = start_copies(sources, (*tables, *loaded), sems)
    parity = lax.axis_index("seq") & 1
    half = halves[0].shape[0]
    for part, half_ref in enumerate(halves):
        for head in range(half):
            whole_ref[0, (part ^ parity) * half + head] = half_ref[head]
    slab_table, user_table = tables
    for copy in copies[:2]:
        copy.wait()
    columns = sw_ref.shape[1]
    row = lax.broadcasted_iota(jnp.int32, (slab_table.shape[0], columns), 0)
    col = lax.broadcasted_iota(jnp.int32, (slab_table.shape[0], columns), 1)
    same = jnp.where(row == col, 1.0, 0.0).astype(jnp.bfloat16)
    sw_ref[...] = matmul(slab_table[...], same, ((0,), (0,)))
    for user in range(user_table.shape[0]):
        uw_ref[user * suffix : (user + 1) * suffix] = matmul(user_table[user], same, ((0,), (0,)))
    for copy in copies[2:]:
        copy.wait()
    attend(causal_mask(), loaded[0], k_ref, v_ref, sw_ref, o_ref, parity)


def scale_queries(q_ref, w_ref, scaled_ref):
    head_count = q_ref.shape[1] // HD
    scaled_ref[0] = jnp.zeros_like(scaled_ref[0])
    for head in range(head_count):
        cols = slice(head * HD, (head + 1) * HD)
        query = q_ref[:, cols]
        for level in range(1, scaled_ref.shape[0]):
            column = level * head_count + head
            weight = jnp.broadcast_to(w_ref[:, column : column + 1], query.shape).astype(jnp.bfloat16)
            scaled_ref[level, :, cols] = query * weight


def scale_kernel(*refs):
    sources, (w_ref, q_ref), scaled_ref, loaded, sems = refs[:3], refs[3:5], refs[5], refs[6:9], refs[9]
    copies = start_copies(sources, loaded, sems)
    scale_queries(q_ref, w_ref, scaled_ref)
    for copy in copies:
        copy.wait()


def user_kernel(suffix, w_ref, q_ref, k_ref, v_ref, o_ref, scaled_ref):
    attend(causal_mask(suffix), q_ref, k_ref, v_ref, w_ref, o_ref)
    scale_queries(q_ref, w_ref, scaled_ref)


def read_kernel(depth, suffix, groups, ahead, length_ref, ss_ref, us_ref, sa_ref, ua_ref, *rest):
    offsets = [offset for group in groups for offset in group]
    states, outs, (lengths, sem) = rest[: len(offsets)], rest[len(offsets) : -2], rest[-2:]
    copy = pltpu.make_async_copy(length_ref, lengths, sem)
    copy.start()
    copy.wait()
    position = lax.axis_index("seq").astype(jnp.int32)
    head_count = sa_ref.shape[1] // HD
    users = range(ua_ref.shape[0] // suffix)
    targets = [lengths[user] for user in users]
    slab_level = {o: level_of(o, position, position, depth) for o in (*offsets, *ahead)}
    user_level = {o: [level_of(o, target, position, depth) for target in targets] for o in (*offsets, *ahead)}

    def slab_rows(offset, cols):
        return ss_ref[slab_level[offset], :, cols]

    def user_rows(offset, cols):
        parts = [us_ref[user_level[offset][user], user * suffix : (user + 1) * suffix, cols] for user in users]
        return jnp.concatenate(parts, axis=0)

    for head in range(head_count):
        cols = slice(head * HD, (head + 1) * HD)
        for pick, a_ref, t_ref in ((slab_rows, sa_ref, outs[0]), (user_rows, ua_ref, outs[1])):
            total = a_ref[:, cols]
            for group in groups:
                queries = jnp.concatenate([pick(offset, cols) for offset in group], axis=1)
                blocks = jnp.concatenate([states[offsets.index(offset)][0, head] for offset in group], axis=0)
                total = total + matmul(queries, blocks, ((1,), (0,)))
            t_ref[:, cols] = total
        for pick, out_ref in zip((slab_rows, user_rows), outs[2:]):
            for i, offset in enumerate(ahead):
                start = (head * len(ahead) + i) * HD
                out_ref[:, start : start + HD] = pick(offset, cols)


def last_kernel(ss_ref, us_ref, sa_ref, ua_ref, state_ref, mate_ref, st_ref, ut_ref, square_ref):
    head_count = sa_ref.shape[1] // HD
    square_ref[...] = jnp.zeros_like(square_ref)
    line = 0
    for q_ref, a_ref, t_ref in ((ss_ref, sa_ref, st_ref), (us_ref, ua_ref, ut_ref)):
        for start in range(0, a_ref.shape[0], ROWS):
            rows = slice(start, start + ROWS)
            squares = None
            for head in range(head_count):
                cols = slice(head * HD, (head + 1) * HD)
                wide = slice(2 * head * HD, 2 * (head + 1) * HD)
                states = jnp.concatenate([state_ref[0, head], mate_ref[0, head]], axis=0)
                total = a_ref[rows, cols] + matmul(q_ref[rows, wide], states, ((1,), (0,)))
                t_ref[rows, cols] = total
                squares = total * total if squares is None else squares + total * total
            square_ref[line : line + 1] = jnp.sum(jnp.transpose(squares), axis=0, keepdims=True)
            line += 1


def norm_kernel(features, chunks, st_ref, ut_ref, gain_ref, *rest):
    squares, (so_hbm, uo_hbm, so_ref, uo_ref, sems) = rest[:-5], rest[-5:]
    square = squares[0][...]
    for part_ref in squares[1:]:
        square = square + part_ref[...]
    scale = lax.rsqrt(square / features + 1e-06)
    size = st_ref.shape[1] // chunks
    copies = []
    line = 0
    for t_ref, o_ref, o_hbm in ((st_ref, so_ref, so_hbm), (ut_ref, uo_ref, uo_hbm)):
        for start in range(0, t_ref.shape[0], ROWS):
            rows = slice(start, start + ROWS)
            factor = jnp.transpose(jnp.broadcast_to(scale[line : line + 1], (ROWS, ROWS)))
            for chunk in range(chunks):
                for low in range(chunk * size, (chunk + 1) * size, HD):
                    cols = slice(low, low + HD)
                    gain = gain_ref[:, cols].astype(jnp.float32)
                    o_ref[rows, cols] = (t_ref[rows, cols] * factor * gain).astype(jnp.bfloat16)
                part = (pl.ds(start, ROWS), pl.ds(chunk * size, size))
                copies.append(pltpu.make_async_copy(o_ref.at[part], o_hbm.at[part], sems.at[line, chunk]))
                copies[-1].start()
            line += 1
    for copy in copies:
        copy.wait()


def local(
    slab_query,
    slab_key,
    slab_value,
    slab_levels,
    norm_gain,
    user_query,
    user_key,
    user_value,
    user_levels,
    prefix_lengths,
):
    seq_count = lax.axis_size("seq")
    head_axis = lax.axis_size("head")
    depth = seq_count.bit_length() - 1
    token_count, width = slab_query.shape
    head_count = width // HD
    half = head_count // 2
    user_count, suffix = user_query.shape[:2]
    user_rows = user_count * suffix
    lines = (token_count + user_rows) // ROWS
    params = pltpu.CompilerParams(vmem_limit_bytes=VMEM_BYTES)
    bf16 = functools.partial(jax.ShapeDtypeStruct, dtype=jnp.bfloat16)
    vmem = pl.BlockSpec(memory_space=pltpu.VMEM)
    anywhere = pl.BlockSpec(memory_space=pl.ANY)
    hbm = pl.BlockSpec(memory_space=pltpu.HBM)
    chunks = min(4, half)
    rows_cost = 2 * width * (token_count + user_rows)

    def pinned(*arrays):
        return [pltpu.with_memory_space_constraint(array, pltpu.HBM) for array in arrays]

    def cost(flops, moved):
        return pl.CostEstimate(flops=flops, bytes_accessed=moved, transcendentals=0)

    def swap(value, bit):
        other = depth - bit if bit else 0
        return lax.ppermute(value, "seq", [(i, i ^ (1 << (other if i & 1 else bit))) for i in range(seq_count)])

    def after(results, values):
        return list(lax.optimization_barrier((results, values))[1])

    def join(order, halves):
        return pl.pallas_call(
            join_kernel,
            out_shape=pltpu.VMEM((len(halves) // 2, head_count, HD, HD), jnp.bfloat16),
            in_specs=[anywhere] + [vmem] * len(halves),
            out_specs=vmem,
            compiler_params=params,
        )(order, *halves)

    half_state = pltpu.VMEM((half, HD, HD), jnp.bfloat16)
    slab_rows = pltpu.VMEM((token_count, width), jnp.bfloat16)
    half_rows = pltpu.VMEM((2, token_count, width // 2), jnp.bfloat16)
    first, second, slab_keys, slab_values = pl.pallas_call(
        state_kernel,
        out_shape=[half_state, half_state, half_rows, half_rows],
        in_specs=[hbm] * 2,
        out_specs=[vmem] * 4,
        scratch_shapes=[pltpu.SemaphoreType.DMA((2, 2))],
        compiler_params=params,
    )(*pinned(slab_key, slab_value))
    halves = [first, second]

    outer = list(range(1, depth))
    places = [(bit, side) for bit in outer for side in range(2)]
    ahead = [(bit, 0) for bit in outer[:-1]] + [(bit, 1) for bit in outer[1:]] or places
    sides = {1 << bit: [None, None] for bit in outer}
    for bit, side in ahead:
        sides[1 << bit][side] = swap(halves[side], bit)
    levels = depth + 1
    slab_table = slab_levels.reshape(-1, token_count)
    user_table = user_levels.reshape(user_count, -1, suffix)
    user_array = pltpu.VMEM((user_rows, width), jnp.bfloat16)
    slab_weights, user_weights, slab_queries, lengths, slab_acc, state = pl.pallas_call(
        functools.partial(load_kernel, suffix),
        out_shape=[
            pltpu.VMEM((token_count, levels * head_count), jnp.float32),
            pltpu.VMEM((user_rows, levels * head_count), jnp.float32),
            slab_rows,
            pltpu.VMEM((user_count,), jnp.int32),
            pltpu.VMEM((token_count, width), jnp.float32),
            pltpu.VMEM((1, head_count, HD, HD), jnp.bfloat16),
        ],
        in_specs=[hbm] * 4 + [vmem] * 4,
        out_specs=[vmem] * 6,
        scratch_shapes=[
            pltpu.VMEM(slab_table.shape, jnp.bfloat16),
            pltpu.VMEM(user_table.shape, jnp.bfloat16),
            pltpu.SemaphoreType.DMA((4,)),
        ],
        compiler_params=params,
        cost_estimate=cost(0, 0),
    )(*pinned(slab_table, user_table, slab_query, prefix_lengths), slab_keys, slab_values, first, second)
    halves = after(slab_weights, halves)
    for bit, side in places:
        if (bit, side) not in ahead:
            sides[1 << bit][side] = swap(halves[side], bit)
    slab_scaled, user_queries, user_keys, user_values = pl.pallas_call(
        scale_kernel,
        out_shape=[pltpu.VMEM((levels, token_count, width), jnp.bfloat16)] + [user_array] * 3,
        in_specs=[hbm] * 3 + [vmem] * 2,
        out_specs=[vmem] * 4,
        scratch_shapes=[pltpu.SemaphoreType.DMA((3,))],
        compiler_params=params,
        cost_estimate=cost(0, 0),
    )(
        *pinned(*[array.reshape(user_rows, width) for array in (user_query, user_key, user_value)]),
        slab_weights,
        slab_queries,
    )

    later = sorted((m for m in range(0, seq_count, 2) if m.bit_count() > 1), key=lambda m: m.bit_count())
    for (bit, side), value in zip(ahead, after(slab_scaled, [sides[1 << bit][side] for bit, side in ahead])):
        sides[1 << bit][side] = value
    for m in later:
        high, low = m.bit_length() - 1, (m & -m).bit_length() - 1
        sides[m] = [swap(sides[m ^ (1 << high)][0], high), swap(sides[m ^ (1 << low)][1], low)]
    user_weights = after([sides[1 << bit][side] for bit, side in ahead], [user_weights])[0]
    user_acc, user_scaled = pl.pallas_call(
        functools.partial(user_kernel, suffix),
        out_shape=[
            pltpu.VMEM((user_rows, width), jnp.float32),
            pltpu.VMEM((levels, user_rows, width), jnp.bfloat16),
        ],
        in_specs=[vmem] * 4,
        out_specs=[vmem] * 2,
        compiler_params=params,
        cost_estimate=cost(0, 0),
    )(user_weights, user_queries, user_keys, user_values)

    totals = [pltpu.VMEM((token_count, width), jnp.float32), pltpu.VMEM((user_rows, width), jnp.float32)]

    def read(offsets, accs, ahead=()):
        groups = [tuple(offsets[i : i + 2]) for i in range(0, len(offsets), 2)]
        wide = len(ahead) * width
        extra = [pltpu.VMEM((rows, wide), jnp.bfloat16) for rows in (token_count, user_rows) if ahead]
        return pl.pallas_call(
            functools.partial(read_kernel, depth, suffix, groups, ahead),
            out_shape=totals + extra,
            in_specs=[vmem] * (5 + len(offsets)),
            out_specs=[vmem] * (2 + len(extra)),
            scratch_shapes=[pltpu.SMEM((user_count,), jnp.int32), pltpu.SemaphoreType.DMA(())],
            compiler_params=params,
            cost_estimate=cost(0, 0),
        )(lengths, slab_scaled, user_scaled, *accs, *[whole[m] for m in offsets])

    other = [swap(halves[side], 0) for side in (1, 0)]
    whole = {0: state, 1: join(user_acc, other)}
    direct = [1 << bit for bit in outer]
    for m in direct:
        whole[m] = join(user_acc, sides[m])
        whole[m | 1] = swap(whole[m], 0)
    last = later[-1]
    *accs, slab_ahead, user_ahead = read([0, 1] + direct, (slab_acc, user_acc), (last, last | 1))
    for m in later:
        whole[m] = join(accs[0], sides[m])
        whole[m | 1] = swap(whole[m], 0)
    if later[:-1]:
        accs = read([n for m in later[:-1] for n in (m, m | 1)], accs)
    accs = read([m | 1 for m in direct], accs)
    slab_total, user_total, square = pl.pallas_call(
        last_kernel,
        out_shape=totals + [pltpu.VMEM((-(-lines // 8) * 8, ROWS), jnp.float32)],
        in_specs=[vmem] * 6,
        out_specs=[vmem] * 3,
        compiler_params=params,
        cost_estimate=cost(0, 0),
    )(slab_ahead, user_ahead, *accs, whole[last], whole[last | 1])

    squares = [square]
    for shift in range(1, head_axis):
        squares.append(lax.ppermute(square, "head", [(i, (i + shift) % head_axis) for i in range(head_axis)]))

    slab_out, user_out = pl.pallas_call(
        functools.partial(norm_kernel, float(width * head_axis), chunks),
        out_shape=[bf16((token_count, width)), bf16((user_rows, width))],
        in_specs=[vmem] * (3 + head_axis),
        out_specs=[hbm] * 2,
        scratch_shapes=[
            pltpu.VMEM((token_count, width), jnp.bfloat16),
            pltpu.VMEM((user_rows, width), jnp.bfloat16),
            pltpu.SemaphoreType.DMA((lines, chunks)),
        ],
        compiler_params=params,
    )(slab_total, user_total, norm_gain.reshape(1, width), *squares)
    return slab_out, user_out.reshape(user_count, suffix, width)


def solution(mesh):
    return jax.shard_map(
        local,
        mesh=mesh,
        in_specs=(
            P("seq", "head"),
            P("seq", "head"),
            P("seq", "head"),
            P(None, "head", "seq"),
            P("head"),
            P("seq", None, "head"),
            P("seq", None, "head"),
            P("seq", None, "head"),
            P("seq", None, "head", None),
            P("seq"),
        ),
        out_specs=(P("seq", "head"), P("seq", None, "head")),
        check_vma=False,
    )
```
